32 devices in a mesh: grp: 2 (over core), dev: 16 (over z, y, x).
Axes of the slice: x: 2, y: 2, z: 4, core: 2. Of those that a mesh axis runs over, the one named last changes fastest.
Arguments:
- images: bfloat16 [4096, 512], P(('grp', 'dev')), may hold values from -128 to 128
- texts: bfloat16 [4096, 512], P(('grp', 'dev')), may hold values from -128 to 128
- logit_scale: float32 [1], replicated, may hold values from 20 to 50
- logit_bias: float32 [1], replicated, may hold values from -12 to -6
Outputs:
- image_grad: float32 [4096, 512], P(('grp', 'dev'))
- text_grad: float32 [4096, 512], P(('grp', 'dev'))
The draws below stay inside these ranges and needn't reach their ends.
All inputs are finite; a program needn't handle non-finite values.
Results may differ from the reference program's by a relative error of at most 0.0047.
Values may be sent and summed in bfloat16 or wider, within the bound.
No kernel may reach another device: no remote copies, remote signals or barrier semaphores. Data moves between devices by JAX's collectives and lax.ppermute only.
A program may use at most 64 MiB of HBM per device.

```python
import math
import jax
import jax.numpy as jnp
from jax import lax

D = 512
ROWS = 128
BATCH = 4096


cluster_count = 64


def shared_rows(key):
    centers = jax.random.truncated_normal(jax.random.fold_in(key, 101), -5.0, 5.0, (cluster_count, D), jnp.float32)
    labels = jax.random.randint(jax.random.fold_in(key, 102), (BATCH,), 0, cluster_count)
    members = jnp.take(centers, labels, axis=0)
    share = jax.random.uniform(jax.random.fold_in(key, 103), (BATCH, 1), jnp.float32, 0.05, 0.6)
    noise = jax.random.truncated_normal(jax.random.fold_in(key, 104), -5.0, 5.0, (BATCH, D), jnp.float32)
    columns = jnp.exp(jax.random.uniform(jax.random.fold_in(key, 106), (1, D), jnp.float32, 0.0, math.log(10.0)))
    base = jnp.sqrt(share) * members + jnp.sqrt(1.0 - share) * noise
    return (base, columns)


def draw_images(key, part):
    own_key = jax.random.fold_in(key, 3)
    lowest = 0.1
    base, columns = shared_rows(key)
    row_scale = jnp.exp(jax.random.uniform(own_key, (BATCH, 1), jnp.float32, math.log(lowest), 0.0))
    return (base * columns * row_scale).astype(jnp.bfloat16)


def draw_texts(key, part):
    own_key = jax.random.fold_in(key, 4)
    lowest = 0.1
    fresh = jax.random.truncated_normal(jax.random.fold_in(own_key, 2), -5.0, 5.0, (BATCH, D), jnp.float32)
    base, columns = shared_rows(key)
    match = jax.random.uniform(jax.random.fold_in(own_key, 1), (BATCH, 1), jnp.float32, 0.2, 0.8)
    row_scale = jnp.exp(jax.random.uniform(jax.random.fold_in(own_key, 3), (BATCH, 1), jnp.float32, math.log(lowest), 0.0))
    mixed = jnp.sqrt(match) * base + jnp.sqrt(1.0 - match) * fresh
    return (mixed * columns * row_scale).astype(jnp.bfloat16)


def setup_inputs(seed: int = 0) -> dict:
    keys = jax.random.split(jax.random.key(seed), 5)
    return {
        "images": draw_images(jax.random.fold_in(keys[4], 71), 0),
        "texts": draw_texts(jax.random.fold_in(keys[4], 71), 0),
        "logit_scale": jnp.clip(jax.random.uniform(keys[2], (1,), jnp.float32, 20.0, 50.0), 20.0, 50.0),
        "logit_bias": jnp.clip(jax.random.uniform(keys[3], (1,), jnp.float32, -12.0, -6.0), -12.0, -6.0),
    }


def normalized(raw_rows):
    widened = raw_rows.astype(jnp.float32)
    factor = lax.rsqrt(lax.optimization_barrier(jnp.sum(widened * widened, axis=-1, keepdims=True)) + 1e-06)
    return (widened * factor, factor)

def unnormalize(grad_unit, unit_rows, factor):
    along = lax.optimization_barrier(jnp.sum(unit_rows * grad_unit, axis=-1, keepdims=True))
    return factor * (grad_unit - unit_rows * along)

def reference(images, texts, logit_scale, logit_bias):
    img_unit, img_factor = normalized(images)
    txt_unit, txt_factor = normalized(texts)
    img_wide = img_unit.astype(jnp.bfloat16).astype(jnp.float32)
    txt_wide = txt_unit.astype(jnp.bfloat16).astype(jnp.float32)
    temper = logit_scale[0]
    offset = logit_bias[0]
    text_ids = jnp.arange(BATCH, dtype=jnp.int32)
    block_count = BATCH // ROWS

    def block_step(carried, block_in):
        block_data, first_row = block_in
        logits = temper * jnp.dot(block_data, txt_wide.T, precision=lax.Precision.HIGHEST) + offset
        image_ids = first_row + jnp.arange(ROWS, dtype=jnp.int32)
        same_pair = (image_ids[:, None] == text_ids[None, :]).astype(jnp.float32)
        coefficient = (temper * (jax.nn.sigmoid(logits) - same_pair)).astype(jnp.bfloat16).astype(jnp.float32)
        image_part = jnp.dot(coefficient, txt_wide, precision=lax.Precision.HIGHEST)
        carried = carried + jnp.dot(coefficient.T, block_data, precision=lax.Precision.HIGHEST)
        return (carried, image_part)
    starts = jnp.arange(block_count, dtype=jnp.int32) * ROWS
    text_grad_unit, image_parts = lax.scan(block_step, jnp.zeros((BATCH, D), jnp.float32), (img_wide.reshape(block_count, ROWS, D), starts))
    image_grad_unit = image_parts.reshape(BATCH, D)
    return (unnormalize(image_grad_unit, img_unit, img_factor), unnormalize(text_grad_unit, txt_unit, txt_factor))
```

```python
import functools
import math

import jax
import jax.numpy as jnp
from jax import lax
from jax.experimental import pallas as pl
from jax.experimental.pallas import tpu as pltpu
from jax.sharding import PartitionSpec as P

AXES = ("grp", "dev")
VMEM_LIMIT = 50 * 1024 * 1024


def unit_rows(raw):
    wide = raw.astype(jnp.float32)
    factor = lax.rsqrt(jnp.sum(wide * wide, axis=-1, keepdims=True) + 1e-06)
    return wide * factor, factor


def pairs_kernel(image_count, text_count, rows, span, *refs):
    scale_ref, bias_ref = refs[:2]
    image_refs = refs[2:2 + image_count]
    text_refs = refs[2 + image_count:2 + image_count + text_count]
    outs = refs[2 + image_count + text_count:]
    image_out = outs[:image_count]
    text_out = outs[image_count:image_count + text_count]
    v_images, image_acc = outs[image_count + text_count:]
    temper = scale_ref[0]
    offset = bias_ref[0]
    for a, ref in enumerate(image_refs):
        unit, _ = unit_rows(ref[...])
        v_images[a * rows:(a + 1) * rows, :] = unit.astype(jnp.bfloat16)
    vi = v_images[...]
    for first in range(0, text_count, span):
        here = range(first, min(first + span, text_count))
        vt = jnp.concatenate(
            [unit_rows(text_refs[c][...])[0].astype(jnp.bfloat16) for c in here], axis=0
        )
        logits = temper * lax.dot_general(
            vi, vt, (((1,), (1,)), ((), ())), preferred_element_type=jnp.float32
        ) + offset
        chance = 1.0 / (1.0 + jnp.exp(-logits))
        if first == 0:
            row = lax.broadcasted_iota(jnp.int32, chance.shape, 0)
            column = lax.broadcasted_iota(jnp.int32, chance.shape, 1)
            same = (row == column) & (row < rows)
            chance = chance - same.astype(jnp.float32)
        coefficient = (temper * chance).astype(jnp.bfloat16)
        image_part = jnp.dot(coefficient, vt, preferred_element_type=jnp.float32)
        text_part = lax.dot_general(
            coefficient, vi, (((0,), (0,)), ((), ())), preferred_element_type=jnp.float32
        )
        for at, c in enumerate(here):
            text_out[c][...] = text_part[at * rows:(at + 1) * rows, :].astype(text_out[c].dtype)
        if first == 0:
            image_acc[...] = image_part
        else:
            image_acc[...] += image_part
    for a, ref in enumerate(image_out):
        ref[...] = image_acc[a * rows:(a + 1) * rows, :].astype(ref.dtype)


def pair_terms(images, texts, scale, bias):
    rows, width = images[0].shape
    image_count, text_count = len(images), len(texts)
    own = jax.ShapeDtypeStruct((rows, width), jnp.float32)
    sent = jax.ShapeDtypeStruct((rows, width), jnp.bfloat16)
    out_shape = [own] + [sent] * (image_count - 1) + [own] + [sent] * (text_count - 1)
    smem = pl.BlockSpec(memory_space=pltpu.SMEM)
    vmem = pl.BlockSpec(memory_space=pltpu.VMEM)
    pairs = image_count * text_count * rows * rows
    outs = pl.pallas_call(
        functools.partial(pairs_kernel, image_count, text_count, rows, 2),
        out_shape=out_shape,
        in_specs=[smem, smem] + [vmem] * (image_count + text_count),
        out_specs=[vmem] * len(out_shape),
        scratch_shapes=[
            pltpu.VMEM((image_count * rows, width), jnp.bfloat16),
            pltpu.VMEM((image_count * rows, width), jnp.float32),
        ],
        compiler_params=pltpu.CompilerParams(vmem_limit_bytes=VMEM_LIMIT),
        cost_estimate=pl.CostEstimate(
            flops=6 * pairs * width,
            bytes_accessed=4 * (image_count + text_count) * rows * width,
            transcendentals=2 * pairs,
        ),
        name="pair_terms",
    )(scale, bias, *images, *texts)
    return outs[:image_count], outs[image_count:]


def finish_kernel(image_count, text_count, image_ref, text_ref, *refs):
    image_parts = refs[:image_count]
    text_parts = refs[image_count:image_count + text_count]
    outs = refs[image_count + text_count:]
    for raw, parts, out in ((image_ref, image_parts, outs[0]), (text_ref, text_parts, outs[1])):
        unit, factor = unit_rows(raw[...])
        total = parts[0][...].astype(jnp.float32)
        for part in parts[1:]:
            total = total + part[...].astype(jnp.float32)
        along = jnp.sum(unit * total, axis=-1, keepdims=True)
        out[...] = factor * (total - unit * along)


def finish(images, texts, image_parts, text_parts):
    out = jax.ShapeDtypeStruct(images.shape, jnp.float32)
    vmem = pl.BlockSpec(memory_space=pltpu.VMEM)
    count = len(image_parts) + len(text_parts)
    return pl.pallas_call(
        functools.partial(finish_kernel, len(image_parts), len(text_parts)),
        out_shape=(out, out),
        in_specs=[vmem] * (2 + count),
        out_specs=(vmem, vmem),
        compiler_params=pltpu.CompilerParams(vmem_limit_bytes=VMEM_LIMIT),
        cost_estimate=pl.CostEstimate(
            flops=10 * count * images.size, bytes_accessed=3 * count * images.size,
            transcendentals=0,
        ),
        name="finish",
    )(images, texts, *image_parts, *text_parts)


def plan(grp_count, dev_count):
    options = [n for n in range(1, dev_count + 1) if dev_count % n == 0]
    near = min(options, key=lambda n: (dev_count // n + grp_count * n, -n))
    return dev_count // near, near


def shift(value, grp_count, far_count, near_count, by_grp, by_far, by_near):
    perm = []
    for g in range(grp_count):
        for f in range(far_count):
            for n in range(near_count):
                source = (g * far_count + f) * near_count + n
                g2 = (g + by_grp) % grp_count
                f2 = (f + by_far) % far_count
                n2 = (n + by_near) % near_count
                perm.append((source, (g2 * far_count + f2) * near_count + n2))
    return lax.ppermute(value, AXES, perm)


def solution(mesh):
    grp_count, dev_count = mesh.shape["grp"], mesh.shape["dev"]
    far_count, near_count = plan(grp_count, dev_count)
    move = functools.partial(
        shift, grp_count=grp_count, far_count=far_count, near_count=near_count
    )
    image_steps = [dict(by_grp=0, by_far=f, by_near=0) for f in range(far_count)]
    text_steps = [
        dict(by_grp=g, by_far=0, by_near=n) for n in range(near_count) for g in range(grp_count)
    ]

    def back(step):
        return {name: -by for name, by in step.items()}

    def on_device(images, texts, logit_scale, logit_bias):
        image_rows = [images] + [move(images, **step) for step in image_steps[1:]]
        text_rows = [texts] + [move(texts, **step) for step in text_steps[1:]]
        image_parts, text_parts = pair_terms(image_rows, text_rows, logit_scale, logit_bias)
        image_parts = [image_parts[0]] + [
            move(part, **back(step)) for part, step in zip(image_parts[1:], image_steps[1:])
        ]
        text_parts = [text_parts[0]] + [
            move(part, **back(step)) for part, step in zip(text_parts[1:], text_steps[1:])
        ]
        return finish(images, texts, image_parts, text_parts)

    in_specs = (P(AXES, None), P(AXES, None), P(), P())
    out_specs = (P(AXES, None), P(AXES, None))
    return jax.shard_map(
        on_device, mesh=mesh, in_specs=in_specs, out_specs=out_specs, check_vma=False
    )
```

```python
import functools
import math

import jax
import jax.numpy as jnp
from jax import lax
from jax.experimental import pallas as pl
from jax.experimental.pallas import tpu as pltpu
from jax.sharding import PartitionSpec as P

AXES = ("grp", "dev")
VMEM_LIMIT = 50 * 1024 * 1024


def unit_rows(raw):
    wide = raw.astype(jnp.float32)
    factor = lax.rsqrt(jnp.sum(wide * wide, axis=-1, keepdims=True) + 1e-06)
    return wide * factor, factor


def pairs_kernel(image_count, text_count, rows, span, *refs):
    scale_ref, bias_ref = refs[:2]
    image_refs = [refs[2].at[a] for a in range(image_count)]
    text_refs = [refs[3].at[c] for c in range(text_count)]
    at_ref = refs[4]
    image_out = [refs[5].at[a] for a in range(image_count)]
    text_out = [refs[6].at[c] for c in range(text_count)]
    v_images, image_acc = refs[7:]
    image_at, text_at = at_ref[0], at_ref[1]
    temper = scale_ref[0]
    offset = bias_ref[0]
    for a, ref in enumerate(image_refs):
        unit, _ = unit_rows(ref[...])
        v_images[a * rows:(a + 1) * rows, :] = unit.astype(jnp.bfloat16)
    vi = v_images[...]
    for first in range(0, text_count, span):
        here = range(first, min(first + span, text_count))
        vt = jnp.concatenate(
            [unit_rows(text_refs[c][...])[0].astype(jnp.bfloat16) for c in here], axis=0
        )
        logits = temper * lax.dot_general(
            vi, vt, (((1,), (1,)), ((), ())), preferred_element_type=jnp.float32
        ) + offset
        chance = 1.0 / (1.0 + jnp.exp(-logits))
        row = lax.broadcasted_iota(jnp.int32, chance.shape, 0) - image_at * rows
        column = lax.broadcasted_iota(jnp.int32, chance.shape, 1) - (text_at - first) * rows
        same = (row == column) & (row >= 0) & (row < rows)
        chance = chance - same.astype(jnp.float32)
        coefficient = (temper * chance).astype(jnp.bfloat16)
        image_part = jnp.dot(coefficient, vt, preferred_element_type=jnp.float32)
        text_part = lax.dot_general(
            coefficient, vi, (((0,), (0,)), ((), ())), preferred_element_type=jnp.float32
        )
        for at, c in enumerate(here):
            text_out[c][...] = text_part[at * rows:(at + 1) * rows, :].astype(text_out[c].dtype)
        if first == 0:
            image_acc[...] = image_part
        else:
            image_acc[...] += image_part
    for a, ref in enumerate(image_out):
        ref[...] = image_acc[a * rows:(a + 1) * rows, :].astype(ref.dtype)


def pair_terms(images, texts, scale, bias, image_at, text_at):
    image_count, rows, width = images.shape
    text_count = texts.shape[0]
    out_shape = [
        jax.ShapeDtypeStruct(images.shape, jnp.bfloat16),
        jax.ShapeDtypeStruct(texts.shape, jnp.bfloat16),
    ]
    smem = pl.BlockSpec(memory_space=pltpu.SMEM)
    vmem = pl.BlockSpec(memory_space=pltpu.VMEM)
    pairs = image_count * text_count * rows * rows
    return pl.pallas_call(
        functools.partial(pairs_kernel, image_count, text_count, rows, 2),
        out_shape=out_shape,
        in_specs=[smem, smem, vmem, vmem, smem],
        out_specs=[vmem] * len(out_shape),
        scratch_shapes=[
            pltpu.VMEM((image_count * rows, width), jnp.bfloat16),
            pltpu.VMEM((image_count * rows, width), jnp.float32),
        ],
        compiler_params=pltpu.CompilerParams(vmem_limit_bytes=VMEM_LIMIT),
        cost_estimate=pl.CostEstimate(
            flops=6 * pairs * width,
            bytes_accessed=4 * (image_count + text_count) * rows * width,
            transcendentals=2 * pairs,
        ),
        name="pair_terms",
    )(scale, bias, images, texts, jnp.stack([image_at, text_at]))


def finish_kernel(image_count, text_count, image_ref, text_ref, *refs):
    image_parts = [refs[0].at[a] for a in range(image_count)]
    text_parts = [refs[1].at[c] for c in range(text_count)]
    outs = refs[2:]
    for raw, parts, out in ((image_ref, image_parts, outs[0]), (text_ref, text_parts, outs[1])):
        unit, factor = unit_rows(raw[...])
        total = parts[0][...].astype(jnp.float32)
        for part in parts[1:]:
            total = total + part[...].astype(jnp.float32)
        along = jnp.sum(unit * total, axis=-1, keepdims=True)
        out[...] = factor * (total - unit * along)


def finish(images, texts, image_parts, text_parts):
    out = jax.ShapeDtypeStruct(images.shape, jnp.float32)
    vmem = pl.BlockSpec(memory_space=pltpu.VMEM)
    count = image_parts.shape[0] + text_parts.shape[0]
    return pl.pallas_call(
        functools.partial(finish_kernel, image_parts.shape[0], text_parts.shape[0]),
        out_shape=(out, out),
        in_specs=[vmem] * 4,
        out_specs=(vmem, vmem),
        compiler_params=pltpu.CompilerParams(vmem_limit_bytes=VMEM_LIMIT),
        cost_estimate=pl.CostEstimate(
            flops=10 * count * images.size, bytes_accessed=3 * count * images.size,
            transcendentals=0,
        ),
        name="finish",
    )(images, texts, image_parts, text_parts)


def plan(grp_count, dev_count):
    options = [n for n in range(1, dev_count + 1) if dev_count % n == 0]
    near = min(options, key=lambda n: (dev_count // n + grp_count * n, -n))
    return dev_count // near, near


def solution(mesh):
    grp_count, dev_count = mesh.shape["grp"], mesh.shape["dev"]
    far_count, near_count = plan(grp_count, dev_count)
    image_groups = [
        [(g * far_count + f) * near_count + n for f in range(far_count)]
        for g in range(grp_count) for n in range(near_count)
    ]
    text_groups = [
        [(g * far_count + f) * near_count + n for g in range(grp_count) for n in range(near_count)]
        for f in range(far_count)
    ]

    def swap(value, groups):
        return lax.all_to_all(value, AXES, 0, 0, axis_index_groups=groups, tiled=True)

    def on_device(images, texts, logit_scale, logit_bias):
        group_at, dev_at = lax.axis_index("grp"), lax.axis_index("dev")
        image_at = dev_at // near_count
        text_at = group_at * near_count + dev_at % near_count
        image_rows = swap(jnp.broadcast_to(images, (far_count,) + images.shape), image_groups)
        text_rows = swap(
            jnp.broadcast_to(texts, (grp_count * near_count,) + texts.shape), text_groups
        )
        image_parts, text_parts = pair_terms(
            image_rows, text_rows, logit_scale, logit_bias, image_at, text_at
        )
        return finish(
            images, texts, swap(image_parts, image_groups), swap(text_parts, text_groups)
        )

    in_specs = (P(AXES, None), P(AXES, None), P(), P())
    out_specs = (P(AXES, None), P(AXES, None))
    return jax.shard_map(
        on_device, mesh=mesh, in_specs=in_specs, out_specs=out_specs, check_vma=False
    )
```

```python
import functools

import jax
import jax.numpy as jnp
from jax import lax
from jax.experimental import pallas as pl
from jax.experimental.pallas import tpu as pltpu
from jax.sharding import PartitionSpec as P

AXES = ("grp", "dev")
VMEM_LIMIT = 50 * 1024 * 1024
SPAN = 256
EARLY = 10
VMEM = pl.BlockSpec(memory_space=pltpu.VMEM)


def unit_rows(raw):
    wide = raw.astype(jnp.float32)
    factor = lax.rsqrt(jnp.sum(wide * wide, axis=-1, keepdims=True) + 1e-06)
    return wide * factor, factor


def call(kernel, out_shape, operands, scratch=(), flops=0, transcendentals=0, name=None):
    touched = sum(x.size * x.dtype.itemsize for x in list(operands) + list(out_shape))
    outs = pl.pallas_call(
        kernel,
        out_shape=out_shape,
        in_specs=[VMEM] * len(operands),
        out_specs=[VMEM] * len(out_shape),
        scratch_shapes=scratch,
        compiler_params=pltpu.CompilerParams(vmem_limit_bytes=VMEM_LIMIT),
        cost_estimate=pl.CostEstimate(
            flops=flops, bytes_accessed=touched, transcendentals=transcendentals
        ),
        name=name,
    )(*operands)
    return tuple(outs)


def stack_units_kernel(*refs):
    out = refs[-1]
    rows = refs[0].shape[0]
    for at, ref in enumerate(refs[:-1]):
        out[at * rows:(at + 1) * rows, :] = unit_rows(ref[...])[0].astype(out.dtype)


def stack_units(blocks):
    rows, width = blocks[0].shape
    out = jax.ShapeDtypeStruct((len(blocks) * rows, width), jnp.bfloat16)
    return call(stack_units_kernel, [out], blocks, flops=4 * out.size, name="stack_units")[0]


def pairs(vi, temper, offset, text_ref, text_out, own):
    held = text_ref.shape[0]
    total = None
    for first in range(0, held, SPAN):
        last = min(first + SPAN, held)
        vt = text_ref[first:last, :]
        logits = temper * lax.dot_general(
            vi, vt, (((1,), (1,)), ((), ())), preferred_element_type=jnp.float32
        ) + offset
        chance = 1.0 / (1.0 + jnp.exp(-logits))
        if own and first == 0:
            row = lax.broadcasted_iota(jnp.int32, chance.shape, 0)
            column = lax.broadcasted_iota(jnp.int32, chance.shape, 1)
            same = (row == column) & (row < own)
            chance = chance - same.astype(jnp.float32)
        coefficient = (temper * chance).astype(jnp.bfloat16)
        text_out[first:last, :] = lax.dot_general(
            coefficient, vi, (((0,), (0,)), ((), ())), preferred_element_type=jnp.float32
        ).astype(text_out.dtype)
        part = jnp.dot(coefficient, vt, preferred_element_type=jnp.float32)
        total = part if total is None else total + part
    return total


def own_pairs_kernel(params_ref, text_ref, *refs):
    image_refs, (text_out, units_out, total_out) = refs[:-3], refs[-3:]
    rows = image_refs[0].shape[0]
    for a, ref in enumerate(image_refs):
        units_out[a * rows:(a + 1) * rows, :] = unit_rows(ref[...])[0].astype(jnp.bfloat16)
    temper, offset = params_ref[0:1, 0:1], params_ref[1:2, 0:1]
    total_out[...] = pairs(units_out[...], temper, offset, text_ref, text_out, rows)


def other_pairs_kernel(text_count, params_ref, units_ref, total_ref, *refs):
    text_refs, outs = refs[:text_count], refs[text_count:]
    text_out, image_out = outs[:text_count], outs[text_count:]
    rows = image_out[0].shape[0]
    vi = units_ref[...]
    temper, offset = params_ref[0:1, 0:1], params_ref[1:2, 0:1]
    total = total_ref[...]
    for t in range(text_count):
        total = total + pairs(vi, temper, offset, text_refs[t], text_out[t], 0)
    for a, ref in enumerate(image_out):
        ref[...] = total[a * rows:(a + 1) * rows, :].astype(ref.dtype)


def pair_terms(params, images, texts):
    rows, width = images[0].shape
    image_rows = rows * len(images)

    def cost(text_rows):
        return dict(
            flops=6 * image_rows * text_rows * width, transcendentals=2 * image_rows * text_rows
        )

    own_out, units, total = call(
        own_pairs_kernel,
        [
            jax.ShapeDtypeStruct(texts[0].shape, jnp.float32),
            jax.ShapeDtypeStruct((image_rows, width), jnp.bfloat16),
            jax.ShapeDtypeStruct((image_rows, width), jnp.float32),
        ],
        [params, texts[0], *images],
        name="own_pairs",
        **cost(EARLY * texts[0].shape[0]),
    )
    others = texts[1:]
    outs = call(
        functools.partial(other_pairs_kernel, len(others)),
        [jax.ShapeDtypeStruct(t.shape, jnp.bfloat16) for t in others]
        + [jax.ShapeDtypeStruct((rows, width), jnp.float32)]
        + [jax.ShapeDtypeStruct((rows, width), jnp.bfloat16)] * (len(images) - 1),
        [params, units, total, *others],
        name="other_pairs",
        **cost(sum(t.shape[0] for t in others)),
    )
    return outs[len(others):], (own_out,) + outs[:len(others)]


def add_stacks_kernel(part_count, *refs):
    parts, outs = refs[:part_count], refs[part_count:]
    rows = outs[0].shape[0]
    for at, out in enumerate(outs):
        total = parts[0][at * rows:(at + 1) * rows, :]
        for part in parts[1:]:
            total = total + part[at * rows:(at + 1) * rows, :].astype(jnp.float32)
        out[...] = total.astype(out.dtype)


def add_stacks(parts, count):
    shape = (parts[0].shape[0] // count, parts[0].shape[1])
    types = [jnp.float32] + [jnp.bfloat16] * (count - 1)
    return call(
        functools.partial(add_stacks_kernel, len(parts)),
        [jax.ShapeDtypeStruct(shape, t) for t in types],
        parts,
        flops=len(parts) * parts[0].size,
        name="add_stacks",
    )


def finish_kernel(image_count, text_count, image_ref, text_ref, *refs):
    image_parts = refs[:image_count]
    text_parts = refs[image_count:image_count + text_count]
    outs = refs[image_count + text_count:]
    for raw, parts, out in ((image_ref, image_parts, outs[0]), (text_ref, text_parts, outs[1])):
        unit, factor = unit_rows(raw[...])
        total = parts[0][...].astype(jnp.float32)
        for part in parts[1:]:
            total = total + part[...].astype(jnp.float32)
        along = jnp.sum(unit * total, axis=-1, keepdims=True)
        out[...] = factor * (total - unit * along)


def finish(images, texts, image_parts, text_parts):
    out = jax.ShapeDtypeStruct(images.shape, jnp.float32)
    count = len(image_parts) + len(text_parts)
    return call(
        functools.partial(finish_kernel, len(image_parts), len(text_parts)),
        [out, out],
        [images, texts, *image_parts, *text_parts],
        flops=10 * count * images.size,
        name="finish",
    )


def plan(grp_count, dev_count):
    options = [n for n in range(1, dev_count + 1) if dev_count % n == 0]
    near = min(options, key=lambda n: (dev_count // n + grp_count * n, -n))
    return dev_count // near, near


def step_to(at, by, count):
    if count & (count - 1) == 0:
        return at ^ abs(by)
    return (at + by) % count


def solution(mesh):
    grp_count, dev_count = mesh.shape["grp"], mesh.shape["dev"]
    far_count, near_count = plan(grp_count, dev_count)

    def move(value, by_grp=0, by_far=0, by_near=0):
        perm = []
        for g in range(grp_count):
            for f in range(far_count):
                for n in range(near_count):
                    g2 = step_to(g, by_grp, grp_count)
                    f2 = step_to(f, by_far, far_count)
                    n2 = step_to(n, by_near, near_count)
                    source = (g * far_count + f) * near_count + n
                    perm.append((source, (g2 * far_count + f2) * near_count + n2))
        return lax.ppermute(value, AXES, perm)

    def on_device(images, texts, logit_scale, logit_bias):
        params = jnp.concatenate(
            [jnp.broadcast_to(logit_scale, (1, 128)), jnp.broadcast_to(logit_bias, (1, 128))]
        )
        image_rows = [images] + [move(images, by_far=f) for f in range(1, far_count)]
        near_rows = [texts] + [move(texts, by_near=n) for n in range(1, near_count)]
        own_stack = stack_units(near_rows)
        stacks = [own_stack] + [move(own_stack, by_grp=g) for g in range(1, grp_count)]
        image_parts, text_parts = pair_terms(params, image_rows, stacks)
        image_parts = [image_parts[0]] + [
            move(part, by_far=-f) for f, part in enumerate(image_parts) if f
        ]
        text_parts = [text_parts[0]] + [
            move(part, by_grp=-g) for g, part in enumerate(text_parts) if g
        ]
        near_parts = add_stacks(text_parts, near_count)
        near_parts = [near_parts[0]] + [
            move(part, by_near=-n) for n, part in enumerate(near_parts) if n
        ]
        return finish(images, texts, image_parts, near_parts)

    in_specs = (P(AXES, None), P(AXES, None), P(), P())
    out_specs = (P(AXES, None), P(AXES, None))
    return jax.shard_map(
        on_device, mesh=mesh, in_specs=in_specs, out_specs=out_specs, check_vma=False
    )
```

```python
import functools

import jax
import jax.numpy as jnp
from jax import lax
from jax.experimental import pallas as pl
from jax.experimental.pallas import tpu as pltpu
from jax.sharding import PartitionSpec as P

AXES = ("grp", "dev")
VMEM_LIMIT = 50 * 1024 * 1024
SPAN = 256
EARLY = 10
VMEM = pl.BlockSpec(memory_space=pltpu.VMEM)


def unit_rows(raw):
    wide = raw.astype(jnp.float32)
    factor = lax.rsqrt(jnp.sum(wide * wide, axis=-1, keepdims=True) + 1e-06)
    return wide * factor, factor


def call(kernel, out_shape, operands, scratch=(), flops=0, transcendentals=0, name=None):
    touched = sum(x.size * x.dtype.itemsize for x in list(operands) + list(out_shape))
    outs = pl.pallas_call(
        kernel,
        out_shape=out_shape,
        in_specs=[VMEM] * len(operands),
        out_specs=[VMEM] * len(out_shape),
        scratch_shapes=scratch,
        compiler_params=pltpu.CompilerParams(vmem_limit_bytes=VMEM_LIMIT),
        cost_estimate=pl.CostEstimate(
            flops=flops, bytes_accessed=touched, transcendentals=transcendentals
        ),
        name=name,
    )(*operands)
    return tuple(outs)


def own_units_kernel(ref, out):
    out[...] = unit_rows(ref[...])[0].astype(out.dtype)


def own_units(raw):
    out = jax.ShapeDtypeStruct(raw.shape, jnp.bfloat16)
    return call(own_units_kernel, [out], [raw], flops=4 * raw.size, name="own_units")[0]


def stack_units_kernel(*refs):
    out = refs[-1]
    rows = refs[0].shape[0]
    out[:rows, :] = refs[0][...]
    for at, ref in enumerate(refs[1:-1], 1):
        out[at * rows:(at + 1) * rows, :] = unit_rows(ref[...])[0].astype(out.dtype)


def stack_units(blocks):
    rows, width = blocks[0].shape
    out = jax.ShapeDtypeStruct((len(blocks) * rows, width), jnp.bfloat16)
    return call(stack_units_kernel, [out], blocks, flops=4 * out.size, name="stack_units")[0]


def pairs(vi, temper, offset, text_ref, text_out, own):
    held = text_ref.shape[0]
    total = None
    for first in range(0, held, SPAN):
        last = min(first + SPAN, held)
        vt = text_ref[first:last, :]
        logits = temper * lax.dot_general(
            vi, vt, (((1,), (1,)), ((), ())), preferred_element_type=jnp.float32
        ) + offset
        chance = 1.0 / (1.0 + jnp.exp(-logits))
        if own and first == 0:
            row = lax.broadcasted_iota(jnp.int32, chance.shape, 0)
            column = lax.broadcasted_iota(jnp.int32, chance.shape, 1)
            same = (row == column) & (row < own)
            chance = chance - same.astype(jnp.float32)
        coefficient = (temper * chance).astype(jnp.bfloat16)
        text_out[first:last, :] = lax.dot_general(
            coefficient, vi, (((0,), (0,)), ((), ())), preferred_element_type=jnp.float32
        ).astype(text_out.dtype)
        part = jnp.dot(coefficient, vt, preferred_element_type=jnp.float32)
        total = part if total is None else total + part
    return total


def own_pairs_kernel(params_ref, text_ref, *refs):
    image_refs, (text_out, units_out, total_out) = refs[:-3], refs[-3:]
    rows = image_refs[0].shape[0]
    for a, ref in enumerate(image_refs):
        units_out[a * rows:(a + 1) * rows, :] = unit_rows(ref[...])[0].astype(jnp.bfloat16)
    temper, offset = params_ref[0:1, 0:1], params_ref[1:2, 0:1]
    total_out[...] = pairs(units_out[...], temper, offset, text_ref, text_out, rows)


def other_pairs_kernel(text_count, params_ref, units_ref, total_ref, *refs):
    text_refs, outs = refs[:text_count], refs[text_count:]
    text_out, image_out = outs[:text_count], outs[text_count:]
    rows = image_out[0].shape[0]
    vi = units_ref[...]
    temper, offset = params_ref[0:1, 0:1], params_ref[1:2, 0:1]
    total = total_ref[...]
    for t in range(text_count):
        total = total + pairs(vi, temper, offset, text_refs[t], text_out[t], 0)
    for a, ref in enumerate(image_out):
        ref[...] = total[a * rows:(a + 1) * rows, :].astype(ref.dtype)


def pair_terms(params, images, texts):
    rows, width = images[0].shape
    image_rows = rows * len(images)

    def cost(text_rows):
        return dict(
            flops=6 * image_rows * text_rows * width, transcendentals=2 * image_rows * text_rows
        )

    own_out, units, total = call(
        own_pairs_kernel,
        [
            jax.ShapeDtypeStruct(texts[0].shape, jnp.float32),
            jax.ShapeDtypeStruct((image_rows, width), jnp.bfloat16),
            jax.ShapeDtypeStruct((image_rows, width), jnp.float32),
        ],
        [params, texts[0], *images],
        name="own_pairs",
        **cost(EARLY * texts[0].shape[0]),
    )
    others = texts[1:]
    outs = call(
        functools.partial(other_pairs_kernel, len(others)),
        [jax.ShapeDtypeStruct(t.shape, jnp.bfloat16) for t in others]
        + [jax.ShapeDtypeStruct((rows, width), jnp.float32)]
        + [jax.ShapeDtypeStruct((rows, width), jnp.bfloat16)] * (len(images) - 1),
        [params, units, total, *others],
        name="other_pairs",
        **cost(sum(t.shape[0] for t in others)),
    )
    return outs[len(others):], (own_out,) + outs[:len(others)]


def add_stacks_kernel(part_count, *refs):
    parts, outs = refs[:part_count], refs[part_count:]
    rows = outs[0].shape[0]
    for at, out in enumerate(outs):
        total = parts[0][at * rows:(at + 1) * rows, :]
        for part in parts[1:]:
            total = total + part[at * rows:(at + 1) * rows, :].astype(jnp.float32)
        out[...] = total.astype(out.dtype)


def add_stacks(parts, count):
    shape = (parts[0].shape[0] // count, parts[0].shape[1])
    types = [jnp.float32] + [jnp.bfloat16] * (count - 1)
    return call(
        functools.partial(add_stacks_kernel, len(parts)),
        [jax.ShapeDtypeStruct(shape, t) for t in types],
        parts,
        flops=len(parts) * parts[0].size,
        name="add_stacks",
    )


def finish_kernel(image_count, text_count, image_ref, text_ref, *refs):
    image_parts = refs[:image_count]
    text_parts = refs[image_count:image_count + text_count]
    outs = refs[image_count + text_count:]
    for raw, parts, out in ((image_ref, image_parts, outs[0]), (text_ref, text_parts, outs[1])):
        unit, factor = unit_rows(raw[...])
        total = parts[0][...].astype(jnp.float32)
        for part in parts[1:]:
            total = total + part[...].astype(jnp.float32)
        along = jnp.sum(unit * total, axis=-1, keepdims=True)
        out[...] = factor * (total - unit * along)


def finish(images, texts, image_parts, text_parts):
    out = jax.ShapeDtypeStruct(images.shape, jnp.float32)
    count = len(image_parts) + len(text_parts)
    return call(
        functools.partial(finish_kernel, len(image_parts), len(text_parts)),
        [out, out],
        [images, texts, *image_parts, *text_parts],
        flops=10 * count * images.size,
        name="finish",
    )


def plan(grp_count, dev_count):
    options = [n for n in range(1, dev_count + 1) if dev_count % n == 0]
    near = min(options, key=lambda n: (dev_count // n + grp_count * n, -n))
    return dev_count // near, near


def step_to(at, by, count):
    if count & (count - 1) == 0:
        return at ^ abs(by)
    return (at + by) % count


def solution(mesh):
    grp_count, dev_count = mesh.shape["grp"], mesh.shape["dev"]
    far_count, near_count = plan(grp_count, dev_count)
    low_count = 2 if far_count % 2 == 0 else 1
    high_count = far_count // low_count

    def move(value, grp=0, high=0, low=0, near=0):
        perm = []
        for g in range(grp_count):
            for h in range(high_count):
                for w in range(low_count):
                    for n in range(near_count):
                        source = ((g * high_count + h) * low_count + w) * near_count + n
                        g2 = step_to(g, grp, grp_count)
                        h2 = step_to(h, high, high_count)
                        w2 = step_to(w, low, low_count)
                        n2 = step_to(n, near, near_count)
                        target = ((g2 * high_count + h2) * low_count + w2) * near_count + n2
                        perm.append((source, target))
        return lax.ppermute(value, AXES, perm)

    far_steps = [(h, w) for h in range(high_count) for w in range(low_count)]

    def gather_far(rows):
        held = {(0, 0): rows}
        for h in range(1, high_count):
            held[h, 0] = move(rows, high=h)
        for h in range(high_count):
            for w in range(1, low_count):
                held[h, w] = move(held[h, 0], low=w)
        return [held[step] for step in far_steps]

    def on_device(images, texts, logit_scale, logit_bias):
        params = jnp.concatenate(
            [jnp.broadcast_to(logit_scale, (1, 128)), jnp.broadcast_to(logit_bias, (1, 128))]
        )
        image_rows = gather_far(images)
        near_rows = [own_units(texts)] + [move(texts, near=n) for n in range(1, near_count)]
        own_stack = stack_units(near_rows)
        stacks = [own_stack] + [move(own_stack, grp=g) for g in range(1, grp_count)]
        image_parts, text_parts = pair_terms(params, image_rows, stacks)
        image_parts = [image_parts[0]] + [
            move(part, high=-h, low=-w) for (h, w), part in zip(far_steps, image_parts) if h or w
        ]
        text_parts = [text_parts[0]] + [
            move(part, grp=-g) for g, part in enumerate(text_parts) if g
        ]
        near_parts = add_stacks(text_parts, near_count)
        near_parts = [near_parts[0]] + [
            move(part, near=-n) for n, part in enumerate(near_parts) if n
        ]
        return finish(images, texts, image_parts, near_parts)

    in_specs = (P(AXES, None), P(AXES, None), P(), P())
    out_specs = (P(AXES, None), P(AXES, None))
    return jax.shard_map(
        on_device, mesh=mesh, in_specs=in_specs, out_specs=out_specs, check_vma=False
    )
```

```python
import functools

import jax
import jax.numpy as jnp
from jax import lax
from jax.experimental import pallas as pl
from jax.experimental.pallas import tpu as pltpu
from jax.sharding import PartitionSpec as P

AXES = ("grp", "dev")
VMEM_LIMIT = 50 * 1024 * 1024
SPAN = 256
EARLY = 10
VMEM = pl.BlockSpec(memory_space=pltpu.VMEM)


def unit_rows(raw):
    wide = raw.astype(jnp.float32)
    factor = lax.rsqrt(jnp.sum(wide * wide, axis=-1, keepdims=True) + 1e-06)
    return wide * factor, factor


def call(kernel, out_shape, operands, scratch=(), flops=0, transcendentals=0, name=None):
    touched = sum(x.size * x.dtype.itemsize for x in list(operands) + list(out_shape))
    outs = pl.pallas_call(
        kernel,
        out_shape=out_shape,
        in_specs=[VMEM] * len(operands),
        out_specs=[VMEM] * len(out_shape),
        scratch_shapes=scratch,
        compiler_params=pltpu.CompilerParams(vmem_limit_bytes=VMEM_LIMIT),
        cost_estimate=pl.CostEstimate(
            flops=flops, bytes_accessed=touched, transcendentals=transcendentals
        ),
        name=name,
    )(*operands)
    return tuple(outs)


def prepare_kernel(text_ref, scale_ref, bias_ref, units, params, raw, scalars, sems):
    copies = [
        pltpu.make_async_copy(text_ref, raw, sems.at[0]),
        pltpu.make_async_copy(scale_ref, scalars.at[0], sems.at[1]),
        pltpu.make_async_copy(bias_ref, scalars.at[1], sems.at[2]),
    ]
    for copy in copies:
        copy.start()
    for copy in copies:
        copy.wait()
    units[...] = unit_rows(raw[...])[0].astype(units.dtype)
    params[0:1, :] = jnp.full((1, 128), scalars[0, 0], jnp.float32)
    params[1:2, :] = jnp.full((1, 128), scalars[1, 0], jnp.float32)


def prepare(texts, scale, bias):
    return pl.pallas_call(
        prepare_kernel,
        out_shape=(
            jax.ShapeDtypeStruct(texts.shape, jnp.bfloat16),
            jax.ShapeDtypeStruct((2, 128), jnp.float32),
        ),
        in_specs=[pl.BlockSpec(memory_space=pltpu.HBM)] * 3,
        out_specs=(VMEM, VMEM),
        scratch_shapes=[
            pltpu.VMEM(texts.shape, texts.dtype),
            pltpu.SMEM((2, 1), jnp.float32),
            pltpu.SemaphoreType.DMA((3,)),
        ],
        compiler_params=pltpu.CompilerParams(vmem_limit_bytes=VMEM_LIMIT),
        cost_estimate=pl.CostEstimate(
            flops=4 * texts.size, bytes_accessed=4 * texts.size, transcendentals=0
        ),
        name="prepare",
    )(texts, scale, bias)


def stack_units_kernel(*refs):
    out = refs[-1]
    rows = refs[0].shape[0]
    out[:rows, :] = refs[0][...]
    for at, ref in enumerate(refs[1:-1], 1):
        out[at * rows:(at + 1) * rows, :] = unit_rows(ref[...])[0].astype(out.dtype)


def stack_units(blocks):
    rows, width = blocks[0].shape
    out = jax.ShapeDtypeStruct((len(blocks) * rows, width), jnp.bfloat16)
    return call(stack_units_kernel, [out], blocks, flops=4 * out.size, name="stack_units")[0]


def pairs(vi, temper, offset, text_ref, text_out, own):
    held = text_ref.shape[0]
    total = None
    for first in range(0, held, SPAN):
        last = min(first + SPAN, held)
        vt = text_ref[first:last, :]
        logits = temper * lax.dot_general(
            vi, vt, (((1,), (1,)), ((), ())), preferred_element_type=jnp.float32
        ) + offset
        chance = 1.0 / (1.0 + jnp.exp(-logits))
        if own and first == 0:
            row = lax.broadcasted_iota(jnp.int32, chance.shape, 0)
            column = lax.broadcasted_iota(jnp.int32, chance.shape, 1)
            same = (row == column) & (row < own)
            chance = chance - same.astype(jnp.float32)
        coefficient = (temper * chance).astype(jnp.bfloat16)
        text_out[first:last, :] = lax.dot_general(
            coefficient, vi, (((0,), (0,)), ((), ())), preferred_element_type=jnp.float32
        ).astype(text_out.dtype)
        part = jnp.dot(coefficient, vt, preferred_element_type=jnp.float32)
        total = part if total is None else total + part
    return total


def own_pairs_kernel(params_ref, text_ref, *refs):
    image_refs, (text_out, units_out, total_out) = refs[:-3], refs[-3:]
    rows = image_refs[0].shape[0]
    for a, ref in enumerate(image_refs):
        units_out[a * rows:(a + 1) * rows, :] = unit_rows(ref[...])[0].astype(jnp.bfloat16)
    temper, offset = params_ref[0:1, 0:1], params_ref[1:2, 0:1]
    total_out[...] = pairs(units_out[...], temper, offset, text_ref, text_out, rows)


def other_pairs_kernel(text_count, params_ref, units_ref, total_ref, *refs):
    text_refs, outs = refs[:text_count], refs[text_count:]
    text_out, image_out = outs[:text_count], outs[text_count:]
    rows = image_out[0].shape[0]
    vi = units_ref[...]
    temper, offset = params_ref[0:1, 0:1], params_ref[1:2, 0:1]
    total = total_ref[...]
    for t in range(text_count):
        total = total + pairs(vi, temper, offset, text_refs[t], text_out[t], 0)
    for a, ref in enumerate(image_out):
        ref[...] = total[a * rows:(a + 1) * rows, :].astype(ref.dtype)


def pair_terms(params, images, texts, image_types):
    rows, width = images[0].shape
    image_rows = rows * len(images)

    def cost(text_rows):
        return dict(
            flops=6 * image_rows * text_rows * width, transcendentals=2 * image_rows * text_rows
        )

    own_out, units, total = call(
        own_pairs_kernel,
        [
            jax.ShapeDtypeStruct(texts[0].shape, jnp.float32),
            jax.ShapeDtypeStruct((image_rows, width), jnp.bfloat16),
            jax.ShapeDtypeStruct((image_rows, width), jnp.float32),
        ],
        [params, texts[0], *images],
        name="own_pairs",
        **cost(EARLY * texts[0].shape[0]),
    )
    others = texts[1:]
    outs = call(
        functools.partial(other_pairs_kernel, len(others)),
        [jax.ShapeDtypeStruct(t.shape, jnp.bfloat16) for t in others]
        + [jax.ShapeDtypeStruct((rows, width), t) for t in image_types],
        [params, units, total, *others],
        name="other_pairs",
        **cost(sum(t.shape[0] for t in others)),
    )
    return outs[len(others):], (own_out,) + outs[:len(others)]


def add_stacks_kernel(part_count, *refs):
    parts, outs = refs[:part_count], refs[part_count:]
    rows = outs[0].shape[0]
    for at, out in enumerate(outs):
        total = parts[0][at * rows:(at + 1) * rows, :]
        for part in parts[1:]:
            total = total + part[at * rows:(at + 1) * rows, :].astype(jnp.float32)
        out[...] = total.astype(out.dtype)


def add_stacks(parts, count):
    shape = (parts[0].shape[0] // count, parts[0].shape[1])
    types = [jnp.float32] + [jnp.bfloat16] * (count - 1)
    return call(
        functools.partial(add_stacks_kernel, len(parts)),
        [jax.ShapeDtypeStruct(shape, t) for t in types],
        parts,
        flops=len(parts) * parts[0].size,
        name="add_stacks",
    )


def add_parts_kernel(*refs):
    total = refs[0][...].astype(jnp.float32)
    for part in refs[1:-1]:
        total = total + part[...].astype(jnp.float32)
    refs[-1][...] = total.astype(refs[-1].dtype)


def add_parts(parts):
    out = jax.ShapeDtypeStruct(parts[0].shape, jnp.bfloat16)
    return call(
        add_parts_kernel, [out], parts, flops=len(parts) * out.size, name="add_parts"
    )[0]


def finish_kernel(image_count, text_count, image_ref, text_ref, *refs):
    image_parts = refs[:image_count]
    text_parts = refs[image_count:image_count + text_count]
    outs = refs[image_count + text_count:]
    for raw, parts, out in ((image_ref, image_parts, outs[0]), (text_ref, text_parts, outs[1])):
        unit, factor = unit_rows(raw[...])
        total = parts[0][...].astype(jnp.float32)
        for part in parts[1:]:
            total = total + part[...].astype(jnp.float32)
        along = jnp.sum(unit * total, axis=-1, keepdims=True)
        out[...] = factor * (total - unit * along)


def finish(images, texts, image_parts, text_parts):
    out = jax.ShapeDtypeStruct(images.shape, jnp.float32)
    count = len(image_parts) + len(text_parts)
    return call(
        functools.partial(finish_kernel, len(image_parts), len(text_parts)),
        [out, out],
        [images, texts, *image_parts, *text_parts],
        flops=10 * count * images.size,
        name="finish",
    )


def plan(grp_count, dev_count):
    options = [n for n in range(1, dev_count + 1) if dev_count % n == 0]
    near = min(options, key=lambda n: (dev_count // n + grp_count * n, -n))
    return dev_count // near, near


def step_to(at, by, count):
    if count & (count - 1) == 0:
        return at ^ abs(by)
    return (at + by) % count


def solution(mesh):
    grp_count, dev_count = mesh.shape["grp"], mesh.shape["dev"]
    far_count, near_count = plan(grp_count, dev_count)
    low_count = 2 if far_count % 2 == 0 else 1
    high_count = far_count // low_count

    def move(value, grp=0, high=0, low=0, near=0):
        perm = []
        for g in range(grp_count):
            for h in range(high_count):
                for w in range(low_count):
                    for n in range(near_count):
                        source = ((g * high_count + h) * low_count + w) * near_count + n
                        g2 = step_to(g, grp, grp_count)
                        h2 = step_to(h, high, high_count)
                        w2 = step_to(w, low, low_count)
                        n2 = step_to(n, near, near_count)
                        target = ((g2 * high_count + h2) * low_count + w2) * near_count + n2
                        perm.append((source, target))
        return lax.ppermute(value, AXES, perm)

    far_steps = [(h, w) for h in range(high_count) for w in range(low_count)]

    def gather_far(rows):
        held = {(0, 0): rows}
        for h in range(1, high_count):
            held[h, 0] = move(rows, high=h)
        for w in range(1, low_count):
            held[0, w] = move(rows, low=w)
        for h in range(1, high_count):
            for w in range(1, low_count):
                block, held[0, w] = lax.optimization_barrier((held[h, 0], held[0, w]))
                held[h, w] = move(block, low=w)
        return [held[step] for step in far_steps]

    def return_far(parts):
        came = {
            (h, w): move(parts[h, w], low=-w)
            for h in reversed(range(high_count)) for w in range(1, low_count)
        }
        owned = [parts[0, 0]] + [came[0, w] for w in range(1, low_count)]
        for h in range(1, high_count):
            both = add_parts([parts[h, 0]] + [came[h, w] for w in range(1, low_count)])
            owned.append(move(both, high=-h))
        return owned

    def on_device(images, texts, logit_scale, logit_bias):
        own_texts, params = prepare(texts, logit_scale, logit_bias)
        image_rows = gather_far(images)
        near_rows = [own_texts] + [move(texts, near=n) for n in range(1, near_count)]
        own_stack = stack_units(near_rows)
        stacks = [own_stack] + [move(own_stack, grp=g) for g in range(1, grp_count)]
        image_types = [jnp.bfloat16 if w else jnp.float32 for _, w in far_steps]
        image_parts, text_parts = pair_terms(params, image_rows, stacks, image_types)
        text_parts = [text_parts[0]] + [
            move(part, grp=-g) for g, part in enumerate(text_parts) if g
        ]
        image_parts = return_far(dict(zip(far_steps, image_parts)))
        near_parts = add_stacks(text_parts, near_count)
        near_parts = [near_parts[0]] + [
            move(part, near=-n) for n, part in enumerate(near_parts) if n
        ]
        return finish(images, texts, image_parts, near_parts)

    in_specs = (P(AXES, None), P(AXES, None), P(), P())
    out_specs = (P(AXES, None), P(AXES, None))
    return jax.shard_map(
        on_device, mesh=mesh, in_specs=in_specs, out_specs=out_specs, check_vma=False
    )
```

```python
import functools

import jax
import jax.numpy as jnp
from jax import lax
from jax.experimental import pallas as pl
from jax.experimental.pallas import tpu as pltpu
from jax.sharding import PartitionSpec as P

AXES = ("grp", "dev")
VMEM_LIMIT = 50 * 1024 * 1024
SPAN = 256
LATE = 40
VMEM = pl.BlockSpec(memory_space=pltpu.VMEM)


def unit_rows(raw):
    wide = raw.astype(jnp.float32)
    factor = lax.rsqrt(jnp.sum(wide * wide, axis=-1, keepdims=True) + 1e-06)
    return wide * factor, factor


def call(kernel, out_shape, operands, scratch=(), flops=0, transcendentals=0, name=None):
    touched = sum(x.size * x.dtype.itemsize for x in list(operands) + list(out_shape))
    outs = pl.pallas_call(
        kernel,
        out_shape=out_shape,
        in_specs=[VMEM] * len(operands),
        out_specs=[VMEM] * len(out_shape),
        scratch_shapes=scratch,
        compiler_params=pltpu.CompilerParams(vmem_limit_bytes=VMEM_LIMIT),
        cost_estimate=pl.CostEstimate(
            flops=flops, bytes_accessed=touched, transcendentals=transcendentals
        ),
        name=name,
    )(*operands)
    return tuple(outs)


def prepare_kernel(text_ref, scale_ref, bias_ref, units, params, raw, scalars, sems):
    copies = [
        pltpu.make_async_copy(text_ref, raw, sems.at[0]),
        pltpu.make_async_copy(scale_ref, scalars.at[0], sems.at[1]),
        pltpu.make_async_copy(bias_ref, scalars.at[1], sems.at[2]),
    ]
    for copy in copies:
        copy.start()
    for copy in copies:
        copy.wait()
    units[...] = unit_rows(raw[...])[0].astype(units.dtype)
    params[0:1, :] = jnp.full((1, 128), scalars[0, 0], jnp.float32)
    params[1:2, :] = jnp.full((1, 128), scalars[1, 0], jnp.float32)


def prepare(texts, scale, bias):
    return pl.pallas_call(
        prepare_kernel,
        out_shape=(
            jax.ShapeDtypeStruct(texts.shape, jnp.bfloat16),
            jax.ShapeDtypeStruct((2, 128), jnp.float32),
        ),
        in_specs=[pl.BlockSpec(memory_space=pltpu.HBM)] * 3,
        out_specs=(VMEM, VMEM),
        scratch_shapes=[
            pltpu.VMEM(texts.shape, texts.dtype),
            pltpu.SMEM((2, 1), jnp.float32),
            pltpu.SemaphoreType.DMA((3,)),
        ],
        compiler_params=pltpu.CompilerParams(vmem_limit_bytes=VMEM_LIMIT),
        cost_estimate=pl.CostEstimate(
            flops=4 * texts.size, bytes_accessed=4 * texts.size, transcendentals=0
        ),
        name="prepare",
    )(texts, scale, bias)


def stack_units_kernel(*refs):
    out = refs[-1]
    rows = refs[0].shape[0]
    out[:rows, :] = refs[0][...]
    for at, ref in enumerate(refs[1:-1], 1):
        out[at * rows:(at + 1) * rows, :] = unit_rows(ref[...])[0].astype(out.dtype)


def stack_units(blocks):
    rows, width = blocks[0].shape
    out = jax.ShapeDtypeStruct((len(blocks) * rows, width), jnp.bfloat16)
    return call(stack_units_kernel, [out], blocks, flops=4 * out.size, name="stack_units")[0]


def pairs(vi, temper, offset, text_ref, text_out, own):
    held = text_ref.shape[0]
    total = None
    for first in range(0, held, SPAN):
        last = min(first + SPAN, held)
        vt = text_ref[first:last, :]
        logits = temper * lax.dot_general(
            vi, vt, (((1,), (1,)), ((), ())), preferred_element_type=jnp.float32
        ) + offset
        chance = 1.0 / (1.0 + jnp.exp(-logits))
        if own and first == 0:
            row = lax.broadcasted_iota(jnp.int32, chance.shape, 0)
            column = lax.broadcasted_iota(jnp.int32, chance.shape, 1)
            same = (row == column) & (row < own)
            chance = chance - same.astype(jnp.float32)
        coefficient = (temper * chance).astype(jnp.bfloat16)
        text_out[first:last, :] = lax.dot_general(
            coefficient, vi, (((0,), (0,)), ((), ())), preferred_element_type=jnp.float32
        ).astype(text_out.dtype)
        part = jnp.dot(coefficient, vt, preferred_element_type=jnp.float32)
        total = part if total is None else total + part
    return total


def own_pairs_kernel(has_own, params_ref, text_ref, *refs):
    image_refs, (text_out, units_out, total_out) = refs[:-3], refs[-3:]
    rows = image_refs[0].shape[0]
    for a, ref in enumerate(image_refs):
        units_out[a * rows:(a + 1) * rows, :] = unit_rows(ref[...])[0].astype(jnp.bfloat16)
    temper, offset = params_ref[0:1, 0:1], params_ref[1:2, 0:1]
    own = rows if has_own else 0
    total_out[...] = pairs(units_out[...], temper, offset, text_ref, text_out, own)


def own_pairs(params, text, images, has_own, weight, name):
    rows, width = images[0].shape
    image_rows = rows * len(images)
    return call(
        functools.partial(own_pairs_kernel, has_own),
        [
            jax.ShapeDtypeStruct(text.shape, jnp.float32),
            jax.ShapeDtypeStruct((image_rows, width), jnp.bfloat16),
            jax.ShapeDtypeStruct((image_rows, width), jnp.float32),
        ],
        [params, text, *images],
        flops=6 * weight * image_rows * text.shape[0] * width,
        transcendentals=2 * weight * image_rows * text.shape[0],
        name=name,
    )


def other_pairs_kernel(part_count, text_count, params_ref, *refs):
    units_refs, total_refs = refs[:part_count], refs[part_count:2 * part_count]
    text_refs = refs[2 * part_count:2 * part_count + text_count]
    outs = refs[2 * part_count + text_count:]
    text_out, image_out = outs[:text_count], outs[text_count:]
    rows = image_out[0].shape[0]
    vi = jnp.concatenate([ref[...] for ref in units_refs], axis=0)
    temper, offset = params_ref[0:1, 0:1], params_ref[1:2, 0:1]
    total = jnp.concatenate([ref[...] for ref in total_refs], axis=0)
    for t in range(text_count):
        total = total + pairs(vi, temper, offset, text_refs[t], text_out[t], 0)
    for a, ref in enumerate(image_out):
        ref[...] = total[a * rows:(a + 1) * rows, :].astype(ref.dtype)


def pair_terms(params, early, late, texts):
    rows, width = early[0].shape
    held = []
    for images, weight, name in ((early, 1, "early_pairs"), (late, LATE, "late_pairs")):
        if images:
            held.append(own_pairs(params, texts[0], images, images is early, weight, name))
    count = len(early) + len(late)
    others = texts[1:]
    text_rows = sum(t.shape[0] for t in others)
    outs = call(
        functools.partial(other_pairs_kernel, len(held), len(others)),
        [jax.ShapeDtypeStruct(t.shape, jnp.bfloat16) for t in others]
        + [jax.ShapeDtypeStruct((rows, width), jnp.float32)]
        + [jax.ShapeDtypeStruct((rows, width), jnp.bfloat16)] * (count - 1),
        [params, *[h[1] for h in held], *[h[2] for h in held], *others],
        flops=6 * count * rows * text_rows * width,
        transcendentals=2 * count * rows * text_rows,
        name="other_pairs",
    )
    return outs[len(others):], [h[0] for h in held], outs[:len(others)]


def add_stacks_kernel(part_count, *refs):
    parts, outs = refs[:part_count], refs[part_count:]
    rows = outs[0].shape[0]
    for at, out in enumerate(outs):
        total = parts[0][at * rows:(at + 1) * rows, :].astype(jnp.float32)
        for part in parts[1:]:
            total = total + part[at * rows:(at + 1) * rows, :].astype(jnp.float32)
        out[...] = total.astype(out.dtype)


def add_stacks(parts, count):
    shape = (parts[0].shape[0] // count, parts[0].shape[1])
    types = [jnp.float32] + [jnp.bfloat16] * (count - 1)
    return call(
        functools.partial(add_stacks_kernel, len(parts)),
        [jax.ShapeDtypeStruct(shape, t) for t in types],
        parts,
        flops=len(parts) * parts[0].size,
        name="add_stacks",
    )


def finish_kernel(sides, image_ref, text_ref, *refs):
    outs = refs[len(sides):]
    for side, (raw, out) in enumerate(zip((image_ref, text_ref), outs)):
        unit, factor = unit_rows(raw[...])
        total = sum(ref[...].astype(jnp.float32) for at, ref in zip(sides, refs) if at == side)
        along = jnp.sum(unit * total, axis=-1, keepdims=True)
        out[...] = factor * (total - unit * along)


def finish(images, texts, parts):
    out = jax.ShapeDtypeStruct(images.shape, jnp.float32)
    return call(
        functools.partial(finish_kernel, [side for side, _ in parts]),
        [out, out],
        [images, texts, *[part for _, part in parts]],
        flops=10 * len(parts) * images.size,
        name="finish",
    )


def plan(grp_count, dev_count):
    options = [n for n in range(1, dev_count + 1) if dev_count % n == 0]
    near = min(options, key=lambda n: (dev_count // n + grp_count * n, -n))
    return dev_count // near, near


def step_to(at, by, count):
    if count & (count - 1) == 0:
        return at ^ abs(by)
    return (at + by) % count


def solution(mesh):
    grp_count, dev_count = mesh.shape["grp"], mesh.shape["dev"]
    far_count, near_count = plan(grp_count, dev_count)
    low_count = 2 if far_count % 2 == 0 else 1
    high_count = far_count // low_count

    def move(value, grp=0, high=0, low=0, near=0):
        perm = []
        for g in range(grp_count):
            for h in range(high_count):
                for w in range(low_count):
                    for n in range(near_count):
                        source = ((g * high_count + h) * low_count + w) * near_count + n
                        g2 = step_to(g, grp, grp_count)
                        h2 = step_to(h, high, high_count)
                        w2 = step_to(w, low, low_count)
                        n2 = step_to(n, near, near_count)
                        target = ((g2 * high_count + h2) * low_count + w2) * near_count + n2
                        perm.append((source, target))
        return lax.ppermute(value, AXES, perm)

    def on_device(images, texts, logit_scale, logit_bias):
        own_texts, params = prepare(texts, logit_scale, logit_bias)
        early = {(0, 0): images}
        for h in range(1, high_count):
            early[h, 0] = move(images, high=h)
        for w in range(1, low_count):
            early[0, w] = move(images, low=w)
        late = {}
        for h in range(1, high_count):
            block, own_texts, params = lax.optimization_barrier((early[h, 0], own_texts, params))
            for w in range(1, low_count):
                late[h, w] = move(block, low=w)
        near_rows = [own_texts] + [move(texts, near=n) for n in range(1, near_count)]
        own_stack = stack_units(near_rows)
        stacks = [own_stack] + [move(own_stack, grp=g) for g in range(1, grp_count)]
        image_parts, own_parts, other_parts = pair_terms(
            params, list(early.values()), list(late.values()), stacks
        )
        far_parts = dict(zip([*early, *late], image_parts))
        came = [move(part, grp=-g) for g, part in enumerate(other_parts, 1)]
        low_parts = [move(p, low=-w) for (h, w), p in far_parts.items() if w and not h]
        high_parts = [move(p, high=-h, low=-w) for (h, w), p in far_parts.items() if h]
        near_parts = add_stacks([*own_parts, *came], near_count)
        near_parts = [near_parts[0]] + [
            move(part, near=-n) for n, part in enumerate(near_parts) if n
        ]
        return finish(
            images,
            texts,
            [(0, part) for part in [far_parts[0, 0]] + low_parts + high_parts]
            + [(1, part) for part in near_parts],
        )

    in_specs = (P(AXES, None), P(AXES, None), P(), P())
    out_specs = (P(AXES, None), P(AXES, None))
    return jax.shard_map(
        on_device, mesh=mesh, in_specs=in_specs, out_specs=out_specs, check_vma=False
    )
```

```python
import functools
import math

import jax
import jax.numpy as jnp
from jax import lax
from jax.experimental import pallas as pl
from jax.experimental.pallas import tpu as pltpu
from jax.sharding import PartitionSpec as P

AXES = ("grp", "dev")
VMEM_LIMIT = 32 * 1024 * 1024
SPAN = 256
LATE = 30000
LOG2_E = math.log2(math.e)
VMEM = pl.BlockSpec(memory_space=pltpu.VMEM)


def unit_rows(raw):
    wide = raw.astype(jnp.float32)
    factor = lax.rsqrt(jnp.sum(wide * wide, axis=-1, keepdims=True) + 1e-06)
    return wide * factor, factor


def call(kernel, out_shape, operands, scratch=(), flops=0, transcendentals=0, name=None):
    touched = sum(x.size * x.dtype.itemsize for x in list(operands) + list(out_shape))
    outs = pl.pallas_call(
        kernel,
        out_shape=out_shape,
        in_specs=[VMEM] * len(operands),
        out_specs=[VMEM] * len(out_shape),
        scratch_shapes=scratch,
        compiler_params=pltpu.CompilerParams(vmem_limit_bytes=VMEM_LIMIT),
        cost_estimate=pl.CostEstimate(
            flops=flops, bytes_accessed=touched, transcendentals=transcendentals
        ),
        name=name,
    )(*operands)
    return tuple(outs)


def units_kernel(*refs):
    rows = refs[0].shape[0]
    for at, ref in enumerate(refs[:-1]):
        refs[-1][at * rows:(at + 1) * rows, :] = unit_rows(ref[...])[0].astype(refs[-1].dtype)


def units(blocks, name, weight=1):
    rows, width = blocks[0].shape
    out = jax.ShapeDtypeStruct((len(blocks) * rows, width), jnp.bfloat16)
    return call(units_kernel, [out], blocks, flops=4 * weight * out.size, name=name)[0]


def stack_units_kernel(*refs):
    out = refs[-1]
    rows = refs[0].shape[0]
    out[:rows, :] = refs[0][...]
    for at, ref in enumerate(refs[1:-1], 1):
        out[at * rows:(at + 1) * rows, :] = unit_rows(ref[...])[0].astype(out.dtype)


def stack_units(blocks):
    rows, width = blocks[0].shape
    out = jax.ShapeDtypeStruct((len(blocks) * rows, width), jnp.bfloat16)
    return call(stack_units_kernel, [out], blocks, flops=4 * out.size, name="stack_units")[0]


def pairs(vi, params_ref, text_ref, text_out, own=0, text_add=None):
    slope, shift, temper = (params_ref[0:1, at:at + 1] for at in range(3))
    held = text_ref.shape[0]
    total = None
    for first in range(0, held, SPAN):
        last = min(first + SPAN, held)
        vt = text_ref[first:last, :]
        dots = lax.dot_general(
            vi, vt, (((1,), (1,)), ((), ())), preferred_element_type=jnp.float32
        )
        e = jnp.exp2(slope * dots + shift)
        chance = pl.reciprocal(1.0 + e, approx=True)
        if own and first == 0:
            row = lax.broadcasted_iota(jnp.int32, chance.shape, 0)
            column = lax.broadcasted_iota(jnp.int32, chance.shape, 1)
            same = (row == column) & (row < own)
            chance = jnp.where(same, -e * chance, chance)
        coefficient = (temper * chance).astype(jnp.bfloat16)
        text_part = lax.dot_general(
            coefficient, vi, (((0,), (0,)), ((), ())), preferred_element_type=jnp.float32
        )
        if text_add is not None:
            text_part = text_add[first:last, :] + text_part
        text_out[first:last, :] = text_part.astype(text_out.dtype)
        part = jnp.dot(coefficient, vt, preferred_element_type=jnp.float32)
        total = part if total is None else total + part
    return total


def early_pairs_kernel(params_ref, text_ref, *refs):
    image_refs, (text_out, units_out, total_out) = refs[:-3], refs[-3:]
    rows = image_refs[0].shape[0]
    for a, ref in enumerate(image_refs):
        units_out[a * rows:(a + 1) * rows, :] = unit_rows(ref[...])[0].astype(jnp.bfloat16)
    total_out[...] = pairs(units_out[...], params_ref, text_ref, text_out, own=rows)


def rest_pairs_kernel(
    count, params_ref, early_ref, total_ref, own_text_ref, own_add_ref, late_ref, *refs
):
    text_refs, own_out = refs[:count], refs[count]
    other_out, image_out = refs[count + 1:2 * count + 1], refs[2 * count + 1:]
    rows = image_out[0].shape[0]
    early, late = early_ref[...], late_ref[...]
    total = jnp.concatenate(
        [
            total_ref[...],
            pairs(late, params_ref, own_text_ref, own_out, text_add=own_add_ref),
        ],
        axis=0,
    )
    vi = jnp.concatenate([early, late], axis=0)
    for text_ref, out in zip(text_refs, other_out):
        total = total + pairs(vi, params_ref, text_ref, out)
    for a, ref in enumerate(image_out):
        ref[...] = total[a * rows:(a + 1) * rows, :].astype(ref.dtype)


def pair_terms(params, early, late, texts):
    rows, width = early[0].shape
    early_rows, late_rows = rows * len(early), rows * len(late)
    own, others = texts[0], texts[1:]
    other_rows = sum(t.shape[0] for t in others)

    def cost(pair_count):
        return dict(flops=6 * pair_count * width, transcendentals=2 * pair_count)

    own_add, early_units, total = call(
        early_pairs_kernel,
        [
            jax.ShapeDtypeStruct(own.shape, jnp.float32),
            jax.ShapeDtypeStruct((early_rows, width), jnp.bfloat16),
            jax.ShapeDtypeStruct((early_rows, width), jnp.float32),
        ],
        [params, own, *early],
        name="early_pairs",
        **cost(early_rows * own.shape[0]),
    )
    late_units = units(late, "late_units", LATE)
    outs = call(
        functools.partial(rest_pairs_kernel, len(others)),
        [jax.ShapeDtypeStruct(own.shape, jnp.float32)]
        + [jax.ShapeDtypeStruct(t.shape, jnp.bfloat16) for t in others]
        + [jax.ShapeDtypeStruct((rows, width), jnp.float32)]
        + [jax.ShapeDtypeStruct((rows, width), jnp.bfloat16)] * (len(early) + len(late) - 1),
        [params, early_units, total, own, own_add, late_units, *others],
        name="rest_pairs",
        **cost(late_rows * own.shape[0] + (early_rows + late_rows) * other_rows),
    )
    count = 1 + len(others)
    return outs[count:], outs[:count]


def add_stacks_kernel(part_count, *refs):
    parts, outs = refs[:part_count], refs[part_count:]
    rows = outs[0].shape[0]
    for at, out in enumerate(outs):
        total = parts[0][at * rows:(at + 1) * rows, :].astype(jnp.float32)
        for part in parts[1:]:
            total = total + part[at * rows:(at + 1) * rows, :].astype(jnp.float32)
        out[...] = total.astype(out.dtype)


def add_stacks(parts, count):
    shape = (parts[0].shape[0] // count, parts[0].shape[1])
    types = [jnp.float32] + [jnp.bfloat16] * (count - 1)
    return call(
        functools.partial(add_stacks_kernel, len(parts)),
        [jax.ShapeDtypeStruct(shape, t) for t in types],
        parts,
        flops=len(parts) * parts[0].size,
        name="add_stacks",
    )


def finish_kernel(sides, image_ref, text_ref, *refs):
    parts, outs = refs[:len(sides)], refs[len(sides):len(sides) + 2]
    staged, sems = refs[len(sides) + 2:]
    copies = []
    for side, raw in enumerate((image_ref, text_ref)):
        unit, factor = unit_rows(raw[...])
        total = sum(ref[...].astype(jnp.float32) for at, ref in zip(sides, parts) if at == side)
        along = jnp.sum(unit * total, axis=-1, keepdims=True)
        staged[side] = factor * (total - unit * along)
        copies.append(pltpu.make_async_copy(staged.at[side], outs[side], sems.at[side]))
        copies[-1].start()
    for copy in copies:
        copy.wait()


def finish(images, texts, parts):
    out = jax.ShapeDtypeStruct(images.shape, jnp.float32)
    return pl.pallas_call(
        functools.partial(finish_kernel, [side for side, _ in parts]),
        out_shape=(out, out),
        in_specs=[VMEM] * (2 + len(parts)),
        out_specs=[pl.BlockSpec(memory_space=pl.ANY)] * 2,
        scratch_shapes=[
            pltpu.VMEM((2,) + images.shape, jnp.float32),
            pltpu.SemaphoreType.DMA((2,)),
        ],
        compiler_params=pltpu.CompilerParams(vmem_limit_bytes=VMEM_LIMIT),
        cost_estimate=pl.CostEstimate(
            flops=10 * len(parts) * images.size,
            bytes_accessed=3 * len(parts) * images.size,
            transcendentals=0,
        ),
        name="finish",
    )(images, texts, *[part for _, part in parts])


def plan(grp_count, dev_count):
    options = [n for n in range(1, dev_count + 1) if dev_count % n == 0]
    near = min(options, key=lambda n: (dev_count // n + grp_count * n, -n))
    return dev_count // near, near


def step_to(at, by, count):
    if count & (count - 1) == 0:
        return at ^ abs(by)
    return (at + by) % count


def solution(mesh):
    grp_count, dev_count = mesh.shape["grp"], mesh.shape["dev"]
    far_count, near_count = plan(grp_count, dev_count)
    low_count = 2 if far_count % 2 == 0 else 1
    high_count = far_count // low_count

    def move(value, grp=0, high=0, low=0, near=0):
        perm = []
        for g in range(grp_count):
            for h in range(high_count):
                for w in range(low_count):
                    for n in range(near_count):
                        source = ((g * high_count + h) * low_count + w) * near_count + n
                        g2 = step_to(g, grp, grp_count)
                        h2 = step_to(h, high, high_count)
                        w2 = step_to(w, low, low_count)
                        n2 = step_to(n, near, near_count)
                        target = ((g2 * high_count + h2) * low_count + w2) * near_count + n2
                        perm.append((source, target))
        return lax.ppermute(value, AXES, perm)

    def on_device(images, texts, logit_scale, logit_bias):
        params = jnp.concatenate(
            [logit_scale * -LOG2_E, logit_bias * -LOG2_E, logit_scale]
        ).reshape(1, 3)
        early = {(0, 0): images}
        for h in range(1, high_count):
            early[h, 0] = move(images, high=h)
        for w in range(1, low_count):
            early[0, w] = move(images, low=w)
        late = {}
        for h in range(1, high_count):
            block, params = lax.optimization_barrier((early[h, 0], params))
            for w in range(1, low_count):
                late[h, w] = move(block, low=w)
        near_rows = [units([texts], "own_units")] + [move(texts, near=n) for n in range(1, near_count)]
        own_stack = stack_units(near_rows)
        stacks = [own_stack] + [move(own_stack, grp=g) for g in range(1, grp_count)]
        image_parts, text_parts = pair_terms(
            params, list(early.values()), list(late.values()), stacks
        )
        far_parts = dict(zip([*early, *late], image_parts))
        came = [move(part, grp=-g) for g, part in enumerate(text_parts) if g]
        low_parts = [move(p, low=-w) for (h, w), p in far_parts.items() if w and not h]
        high_parts = [move(p, high=-h, low=-w) for (h, w), p in far_parts.items() if h]
        near_parts = add_stacks([text_parts[0], *came], near_count)
        near_parts = [near_parts[0]] + [
            move(part, near=-n) for n, part in enumerate(near_parts) if n
        ]
        return finish(
            images,
            texts,
            [(0, part) for part in [far_parts[0, 0]] + low_parts + high_parts]
            + [(1, part) for part in near_parts],
        )

    in_specs = (P(AXES, None), P(AXES, None), P(), P())
    out_specs = (P(AXES, None), P(AXES, None))
    return jax.shard_map(
        on_device, mesh=mesh, in_specs=in_specs, out_specs=out_specs, check_vma=False
    )
```

```python
import functools
import math

import jax
import jax.numpy as jnp
from jax import lax
from jax.experimental import pallas as pl
from jax.experimental.pallas import tpu as pltpu
from jax.sharding import PartitionSpec as P

AXES = ("grp", "dev")
VMEM_LIMIT = 32 * 1024 * 1024
SPAN = 256
PIECE = 32
LATE = 30000
LOG2_E = math.log2(math.e)
VMEM = pl.BlockSpec(memory_space=pltpu.VMEM)


def unit_rows(raw):
    wide = raw.astype(jnp.float32)
    factor = lax.rsqrt(jnp.sum(wide * wide, axis=-1, keepdims=True) + 1e-06)
    return wide * factor, factor


def call(kernel, out_shape, operands, scratch=(), flops=0, transcendentals=0, name=None):
    touched = sum(x.size * x.dtype.itemsize for x in list(operands) + list(out_shape))
    outs = pl.pallas_call(
        kernel,
        out_shape=out_shape,
        in_specs=[VMEM] * len(operands),
        out_specs=[VMEM] * len(out_shape),
        scratch_shapes=scratch,
        compiler_params=pltpu.CompilerParams(vmem_limit_bytes=VMEM_LIMIT),
        cost_estimate=pl.CostEstimate(
            flops=flops, bytes_accessed=touched, transcendentals=transcendentals
        ),
        name=name,
    )(*operands)
    return tuple(outs)


def units_kernel(*refs):
    rows = refs[0].shape[0]
    for at, ref in enumerate(refs[:-1]):
        refs[-1][at * rows:(at + 1) * rows, :] = unit_rows(ref[...])[0].astype(refs[-1].dtype)


def units(blocks, name, weight=1):
    rows, width = blocks[0].shape
    out = jax.ShapeDtypeStruct((len(blocks) * rows, width), jnp.bfloat16)
    return call(units_kernel, [out], blocks, flops=4 * weight * out.size, name=name)[0]


def stack_units_kernel(*refs):
    out = refs[-1]
    rows = refs[0].shape[0]
    out[:rows, :] = refs[0][...]
    for at, ref in enumerate(refs[1:-1], 1):
        out[at * rows:(at + 1) * rows, :] = unit_rows(ref[...])[0].astype(out.dtype)


def stack_units(blocks):
    rows, width = blocks[0].shape
    out = jax.ShapeDtypeStruct((len(blocks) * rows, width), jnp.bfloat16)
    return call(stack_units_kernel, [out], blocks, flops=4 * out.size, name="stack_units")[0]


def pairs(vi, params_ref, text_ref, text_out, own=0, text_add=None):
    slope, shift, temper = (params_ref[0:1, at:at + 1] for at in range(3))
    held = text_ref.shape[0]
    total = None

    def dots_of(first):
        return lax.dot_general(
            vi,
            text_ref[first:min(first + SPAN, held), :],
            (((1,), (1,)), ((), ())),
            preferred_element_type=jnp.float32,
        )

    coming = dots_of(0)
    for first in range(0, held, SPAN):
        last = min(first + SPAN, held)
        dots, coming = coming, dots_of(last) if last < held else None
        vt = text_ref[first:last, :]
        e = jnp.exp2(slope * dots + shift)
        chance = pl.reciprocal(1.0 + e, approx=True)
        if own and first == 0:
            row = lax.broadcasted_iota(jnp.int32, chance.shape, 0)
            column = lax.broadcasted_iota(jnp.int32, chance.shape, 1)
            same = (row == column) & (row < own)
            chance = jnp.where(same, -e * chance, chance)
        coefficient = (temper * chance).astype(jnp.bfloat16)
        text_part = lax.dot_general(
            coefficient, vi, (((0,), (0,)), ((), ())), preferred_element_type=jnp.float32
        )
        if text_add is not None:
            text_part = text_add[first:last, :] + text_part
        text_out[first:last, :] = text_part.astype(text_out.dtype)
        part = jnp.dot(coefficient, vt, preferred_element_type=jnp.float32)
        total = part if total is None else total + part
    return total


def early_pairs_kernel(params_ref, text_ref, *refs):
    image_refs, (text_out, units_out, total_out) = refs[:-3], refs[-3:]
    rows = image_refs[0].shape[0]
    for a, ref in enumerate(image_refs):
        units_out[a * rows:(a + 1) * rows, :] = unit_rows(ref[...])[0].astype(jnp.bfloat16)
    total_out[...] = pairs(units_out[...], params_ref, text_ref, text_out, own=rows)


def rest_pairs_kernel(
    count, params_ref, early_ref, total_ref, own_text_ref, own_add_ref, late_ref, *refs
):
    text_refs, own_out = refs[:count], refs[count]
    other_out, image_out = refs[count + 1:2 * count + 1], refs[2 * count + 1:]
    rows = image_out[0].shape[0]
    early, late = early_ref[...], late_ref[...]
    total = jnp.concatenate(
        [
            total_ref[...],
            pairs(late, params_ref, own_text_ref, own_out, text_add=own_add_ref),
        ],
        axis=0,
    )
    vi = jnp.concatenate([early, late], axis=0)
    for text_ref, out in zip(text_refs, other_out):
        total = total + pairs(vi, params_ref, text_ref, out)
    for a, ref in enumerate(image_out):
        ref[...] = total[a * rows:(a + 1) * rows, :].astype(ref.dtype)


def pair_terms(params, early, late, texts):
    rows, width = early[0].shape
    early_rows, late_rows = rows * len(early), rows * len(late)
    own, others = texts[0], texts[1:]
    other_rows = sum(t.shape[0] for t in others)

    def cost(pair_count):
        return dict(flops=6 * pair_count * width, transcendentals=2 * pair_count)

    own_add, early_units, total = call(
        early_pairs_kernel,
        [
            jax.ShapeDtypeStruct(own.shape, jnp.float32),
            jax.ShapeDtypeStruct((early_rows, width), jnp.bfloat16),
            jax.ShapeDtypeStruct((early_rows, width), jnp.float32),
        ],
        [params, own, *early],
        name="early_pairs",
        **cost(early_rows * own.shape[0]),
    )
    late_units = units(late, "late_units", LATE)
    outs = call(
        functools.partial(rest_pairs_kernel, len(others)),
        [jax.ShapeDtypeStruct(own.shape, jnp.float32)]
        + [jax.ShapeDtypeStruct(t.shape, jnp.bfloat16) for t in others]
        + [jax.ShapeDtypeStruct((rows, width), jnp.float32)]
        + [jax.ShapeDtypeStruct((rows, width), jnp.bfloat16)] * (len(early) + len(late) - 1),
        [params, early_units, total, own, own_add, late_units, *others],
        name="rest_pairs",
        **cost(late_rows * own.shape[0] + (early_rows + late_rows) * other_rows),
    )
    count = 1 + len(others)
    return outs[count:], outs[:count]


def add_stacks_kernel(part_count, *refs):
    parts, outs = refs[:part_count], refs[part_count:]
    rows = outs[0].shape[0]
    for at, out in enumerate(outs):
        total = parts[0][at * rows:(at + 1) * rows, :].astype(jnp.float32)
        for part in parts[1:]:
            total = total + part[at * rows:(at + 1) * rows, :].astype(jnp.float32)
        out[...] = total.astype(out.dtype)


def add_stacks(parts, count):
    shape = (parts[0].shape[0] // count, parts[0].shape[1])
    types = [jnp.float32] + [jnp.bfloat16] * (count - 1)
    return call(
        functools.partial(add_stacks_kernel, len(parts)),
        [jax.ShapeDtypeStruct(shape, t) for t in types],
        parts,
        flops=len(parts) * parts[0].size,
        name="add_stacks",
    )


def finish_kernel(sides, image_ref, text_ref, *refs):
    parts, outs = refs[:len(sides)], refs[len(sides):len(sides) + 2]
    staged, sems = refs[len(sides) + 2:]
    rows = image_ref.shape[0]
    piece = math.gcd(rows, PIECE)
    copies = []
    for side, raw in enumerate((image_ref, text_ref)):
        for first in range(0, rows, piece):
            here = pl.ds(first, piece)
            unit, factor = unit_rows(raw[here, :])
            total = sum(
                ref[here, :].astype(jnp.float32) for at, ref in zip(sides, parts) if at == side
            )
            along = jnp.sum(unit * total, axis=-1, keepdims=True)
            staged[side, here, :] = factor * (total - unit * along)
            copies.append(
                pltpu.make_async_copy(
                    staged.at[side, here, :], outs[side].at[here, :], sems.at[len(copies)]
                )
            )
            copies[-1].start()
    for copy in copies:
        copy.wait()


def finish(images, texts, parts):
    out = jax.ShapeDtypeStruct(images.shape, jnp.float32)
    return pl.pallas_call(
        functools.partial(finish_kernel, [side for side, _ in parts]),
        out_shape=(out, out),
        in_specs=[VMEM] * (2 + len(parts)),
        out_specs=[pl.BlockSpec(memory_space=pl.ANY)] * 2,
        scratch_shapes=[
            pltpu.VMEM((2,) + images.shape, jnp.float32),
            pltpu.SemaphoreType.DMA((2 * (images.shape[0] // math.gcd(images.shape[0], PIECE)),)),
        ],
        compiler_params=pltpu.CompilerParams(vmem_limit_bytes=VMEM_LIMIT),
        cost_estimate=pl.CostEstimate(
            flops=10 * len(parts) * images.size,
            bytes_accessed=3 * len(parts) * images.size,
            transcendentals=0,
        ),
        name="finish",
    )(images, texts, *[part for _, part in parts])


def plan(grp_count, dev_count):
    options = [n for n in range(1, dev_count + 1) if dev_count % n == 0]
    near = min(options, key=lambda n: (dev_count // n + grp_count * n, -n))
    return dev_count // near, near


def step_to(at, by, count):
    if count & (count - 1) == 0:
        return at ^ abs(by)
    return (at + by) % count


def solution(mesh):
    grp_count, dev_count = mesh.shape["grp"], mesh.shape["dev"]
    far_count, near_count = plan(grp_count, dev_count)
    low_count = 2 if far_count % 2 == 0 else 1
    high_count = far_count // low_count

    def move(value, grp=0, high=0, low=0, near=0):
        perm = []
        for g in range(grp_count):
            for h in range(high_count):
                for w in range(low_count):
                    for n in range(near_count):
                        source = ((g * high_count + h) * low_count + w) * near_count + n
                        g2 = step_to(g, grp, grp_count)
                        h2 = step_to(h, high, high_count)
                        w2 = step_to(w, low, low_count)
                        n2 = step_to(n, near, near_count)
                        target = ((g2 * high_count + h2) * low_count + w2) * near_count + n2
                        perm.append((source, target))
        return lax.ppermute(value, AXES, perm)

    def on_device(images, texts, logit_scale, logit_bias):
        params = jnp.concatenate(
            [logit_scale * -LOG2_E, logit_bias * -LOG2_E, logit_scale]
        ).reshape(1, 3)
        early = {(0, 0): images}
        for h in range(1, high_count):
            early[h, 0] = move(images, high=h)
        for w in range(1, low_count):
            early[0, w] = move(images, low=w)
        late = {}
        for h in range(1, high_count):
            block, params = lax.optimization_barrier((early[h, 0], params))
            for w in range(1, low_count):
                late[h, w] = move(block, low=w)
        near_rows = [units([texts], "own_units")] + [move(texts, near=n) for n in range(1, near_count)]
        own_stack = stack_units(near_rows)
        stacks = [own_stack] + [move(own_stack, grp=g) for g in range(1, grp_count)]
        image_parts, text_parts = pair_terms(
            params, list(early.values()), list(late.values()), stacks
        )
        far_parts = dict(zip([*early, *late], image_parts))
        came = [move(part, grp=-g) for g, part in enumerate(text_parts) if g]
        far_order = [step for step in early if step[0]] + [step for step in early if step[1]] + list(late)
        far_came = [move(far_parts[h, w], high=-h, low=-w) for h, w in far_order]
        near_parts = add_stacks([text_parts[0], *came], near_count)
        near_parts = [near_parts[0]] + [
            move(part, near=-n) for n, part in enumerate(near_parts) if n
        ]
        return finish(
            images,
            texts,
            [(0, part) for part in [far_parts[0, 0]] + far_came]
            + [(1, part) for part in near_parts],
        )

    in_specs = (P(AXES, None), P(AXES, None), P(), P())
    out_specs = (P(AXES, None), P(AXES, None))
    return jax.shard_map(
        on_device, mesh=mesh, in_specs=in_specs, out_specs=out_specs, check_vma=False
    )
```

```python
import functools
import math

import jax
import jax.numpy as jnp
from jax import lax
from jax.experimental import pallas as pl
from jax.experimental.pallas import tpu as pltpu
from jax.sharding import PartitionSpec as P

AXES = ("grp", "dev")
VMEM_LIMIT = 32 * 1024 * 1024
SPAN = 256
PIECE = 32
LATE = 30000
LOG2_E = math.log2(math.e)
VMEM = pl.BlockSpec(memory_space=pltpu.VMEM)


def unit_rows(raw):
    wide = raw.astype(jnp.float32)
    factor = lax.rsqrt(jnp.sum(wide * wide, axis=-1, keepdims=True) + 1e-06)
    return wide * factor, factor


def call(kernel, out_shape, operands, scratch=(), flops=0, transcendentals=0, name=None):
    touched = sum(x.size * x.dtype.itemsize for x in list(operands) + list(out_shape))
    outs = pl.pallas_call(
        kernel,
        out_shape=out_shape,
        in_specs=[VMEM] * len(operands),
        out_specs=[VMEM] * len(out_shape),
        scratch_shapes=scratch,
        compiler_params=pltpu.CompilerParams(vmem_limit_bytes=VMEM_LIMIT),
        cost_estimate=pl.CostEstimate(
            flops=flops, bytes_accessed=touched, transcendentals=transcendentals
        ),
        name=name,
    )(*operands)
    return tuple(outs)


def units_kernel(*refs):
    rows = refs[0].shape[0]
    for at, ref in enumerate(refs[:-1]):
        refs[-1][at * rows:(at + 1) * rows, :] = unit_rows(ref[...])[0].astype(refs[-1].dtype)


def units(blocks, name, weight=1):
    rows, width = blocks[0].shape
    out = jax.ShapeDtypeStruct((len(blocks) * rows, width), jnp.bfloat16)
    return call(units_kernel, [out], blocks, flops=4 * weight * out.size, name=name)[0]


def stack_units_kernel(*refs):
    out = refs[-1]
    rows = refs[0].shape[0]
    out[:rows, :] = refs[0][...]
    for at, ref in enumerate(refs[1:-1], 1):
        out[at * rows:(at + 1) * rows, :] = unit_rows(ref[...])[0].astype(out.dtype)


def stack_units(blocks):
    rows, width = blocks[0].shape
    out = jax.ShapeDtypeStruct((len(blocks) * rows, width), jnp.bfloat16)
    return call(stack_units_kernel, [out], blocks, flops=4 * out.size, name="stack_units")[0]


def pairs(vi, params_ref, text_ref, text_out, own=0, text_add=None):
    slope, shift, temper = (params_ref[0:1, at:at + 1] for at in range(3))
    held = text_ref.shape[0]
    total = None

    def dots_of(first):
        return lax.dot_general(
            vi,
            text_ref[first:min(first + SPAN, held), :],
            (((1,), (1,)), ((), ())),
            preferred_element_type=jnp.float32,
        )

    coming = dots_of(0)
    for first in range(0, held, SPAN):
        last = min(first + SPAN, held)
        dots, coming = coming, dots_of(last) if last < held else None
        vt = text_ref[first:last, :]
        e = jnp.exp2(slope * dots + shift)
        chance = pl.reciprocal(1.0 + e, approx=True)
        if own and first == 0:
            row = lax.broadcasted_iota(jnp.int32, chance.shape, 0)
            column = lax.broadcasted_iota(jnp.int32, chance.shape, 1)
            same = (row == column) & (row < own)
            chance = jnp.where(same, -e * chance, chance)
        coefficient = (temper * chance).astype(jnp.bfloat16)
        text_part = lax.dot_general(
            coefficient, vi, (((0,), (0,)), ((), ())), preferred_element_type=jnp.float32
        )
        if text_add is not None:
            text_part = text_add[first:last, :] + text_part
        text_out[first:last, :] = text_part.astype(text_out.dtype)
        part = jnp.dot(coefficient, vt, preferred_element_type=jnp.float32)
        total = part if total is None else total + part
    return total


def early_pairs_kernel(params_ref, text_ref, *refs):
    image_refs, (text_out, units_out, total_out) = refs[:-3], refs[-3:]
    rows = image_refs[0].shape[0]
    for a, ref in enumerate(image_refs):
        units_out[a * rows:(a + 1) * rows, :] = unit_rows(ref[...])[0].astype(jnp.bfloat16)
    total_out[...] = pairs(units_out[...], params_ref, text_ref, text_out, own=rows)


def rest_pairs_kernel(
    count, params_ref, early_ref, total_ref, own_text_ref, own_add_ref, late_ref, *refs
):
    text_refs, own_out = refs[:count], refs[count]
    other_out, image_out = refs[count + 1:2 * count + 1], refs[2 * count + 1:]
    rows = image_out[0].shape[0]
    early, late = early_ref[...], late_ref[...]
    total = jnp.concatenate(
        [
            total_ref[...],
            pairs(late, params_ref, own_text_ref, own_out, text_add=own_add_ref),
        ],
        axis=0,
    )
    vi = jnp.concatenate([early, late], axis=0)
    for text_ref, out in zip(text_refs, other_out):
        total = total + pairs(vi, params_ref, text_ref, out)
    for a, ref in enumerate(image_out):
        ref[...] = total[a * rows:(a + 1) * rows, :].astype(ref.dtype)


def pair_terms(params, early, late, texts):
    rows, width = early[0].shape
    early_rows, late_rows = rows * len(early), rows * len(late)
    own, others = texts[0], texts[1:]
    other_rows = sum(t.shape[0] for t in others)

    def cost(pair_count):
        return dict(flops=6 * pair_count * width, transcendentals=2 * pair_count)

    own_add, early_units, total = call(
        early_pairs_kernel,
        [
            jax.ShapeDtypeStruct(own.shape, jnp.float32),
            jax.ShapeDtypeStruct((early_rows, width), jnp.bfloat16),
            jax.ShapeDtypeStruct((early_rows, width), jnp.float32),
        ],
        [params, own, *early],
        name="early_pairs",
        **cost(early_rows * own.shape[0]),
    )
    late_units = units(late, "late_units", LATE)
    outs = call(
        functools.partial(rest_pairs_kernel, len(others)),
        [jax.ShapeDtypeStruct(own.shape, jnp.float32)]
        + [jax.ShapeDtypeStruct(t.shape, jnp.bfloat16) for t in others]
        + [jax.ShapeDtypeStruct((rows, width), jnp.float32)]
        + [jax.ShapeDtypeStruct((rows, width), jnp.bfloat16)] * (len(early) + len(late) - 1),
        [params, early_units, total, own, own_add, late_units, *others],
        name="rest_pairs",
        **cost(late_rows * own.shape[0] + (early_rows + late_rows) * other_rows),
    )
    count = 1 + len(others)
    return outs[count:], outs[:count]


def add_stacks_kernel(part_count, *refs):
    parts, outs = refs[:part_count], refs[part_count:]
    rows = outs[0].shape[0]
    for at, out in enumerate(outs):
        total = parts[0][at * rows:(at + 1) * rows, :].astype(jnp.float32)
        for part in parts[1:]:
            total = total + part[at * rows:(at + 1) * rows, :].astype(jnp.float32)
        out[...] = total.astype(out.dtype)


def add_stacks(parts, count):
    shape = (parts[0].shape[0] // count, parts[0].shape[1])
    types = [jnp.float32] + [jnp.bfloat16] * (count - 1)
    return call(
        functools.partial(add_stacks_kernel, len(parts)),
        [jax.ShapeDtypeStruct(shape, t) for t in types],
        parts,
        flops=len(parts) * parts[0].size,
        name="add_stacks",
    )


def finish_kernel(sides, image_ref, text_ref, at_ref, low_ref, *refs):
    parts, outs = refs[:len(sides)], refs[len(sides):len(sides) + 2]
    staged, sems = refs[len(sides) + 2:]
    rows = image_ref.shape[0]
    at, low_count = at_ref[0], low_ref.shape[0]
    neighbour = [low_ref.at[lax.rem(at + w, low_count)] for w in range(1, low_count)]
    sides = sides + [0] * len(neighbour)
    parts = list(parts) + neighbour
    piece = math.gcd(rows, PIECE)
    copies = []
    for side, raw in enumerate((image_ref, text_ref)):
        for first in range(0, rows, piece):
            here = pl.ds(first, piece)
            unit, factor = unit_rows(raw[here, :])
            total = sum(
                ref[here, :].astype(jnp.float32) for own, ref in zip(sides, parts) if own == side
            )
            along = jnp.sum(unit * total, axis=-1, keepdims=True)
            staged[side, here, :] = factor * (total - unit * along)
            copies.append(
                pltpu.make_async_copy(
                    staged.at[side, here, :], outs[side].at[here, :], sems.at[len(copies)]
                )
            )
            copies[-1].start()
    for copy in copies:
        copy.wait()


def finish(images, texts, low_at, low_parts, parts):
    out = jax.ShapeDtypeStruct(images.shape, jnp.float32)
    return pl.pallas_call(
        functools.partial(finish_kernel, [side for side, _ in parts]),
        out_shape=(out, out),
        in_specs=[VMEM] * 2 + [pl.BlockSpec(memory_space=pltpu.SMEM)] + [VMEM] * (1 + len(parts)),
        out_specs=[pl.BlockSpec(memory_space=pl.ANY)] * 2,
        scratch_shapes=[
            pltpu.VMEM((2,) + images.shape, jnp.float32),
            pltpu.SemaphoreType.DMA((2 * (images.shape[0] // math.gcd(images.shape[0], PIECE)),)),
        ],
        compiler_params=pltpu.CompilerParams(vmem_limit_bytes=VMEM_LIMIT),
        cost_estimate=pl.CostEstimate(
            flops=10 * len(parts) * images.size,
            bytes_accessed=3 * len(parts) * images.size,
            transcendentals=0,
        ),
        name="finish",
    )(images, texts, low_at, low_parts, *[part for _, part in parts])


def plan(grp_count, dev_count):
    options = [n for n in range(1, dev_count + 1) if dev_count % n == 0]
    near = min(options, key=lambda n: (dev_count // n + grp_count * n, -n))
    return dev_count // near, near


def step_to(at, by, count):
    if count & (count - 1) == 0:
        return at ^ abs(by)
    return (at + by) % count


def solution(mesh):
    grp_count, dev_count = mesh.shape["grp"], mesh.shape["dev"]
    far_count, near_count = plan(grp_count, dev_count)
    low_count = 2 if far_count % 2 == 0 else 1
    high_count = far_count // low_count

    def move(value, grp=0, high=0, low=0, near=0):
        perm = []
        for g in range(grp_count):
            for h in range(high_count):
                for w in range(low_count):
                    for n in range(near_count):
                        source = ((g * high_count + h) * low_count + w) * near_count + n
                        g2 = step_to(g, grp, grp_count)
                        h2 = step_to(h, high, high_count)
                        w2 = step_to(w, low, low_count)
                        n2 = step_to(n, near, near_count)
                        target = ((g2 * high_count + h2) * low_count + w2) * near_count + n2
                        perm.append((source, target))
        return lax.ppermute(value, AXES, perm)

    low_groups = [
        [((g * high_count + h) * low_count + w) * near_count + n for w in range(low_count)]
        for g in range(grp_count) for h in range(high_count) for n in range(near_count)
    ]

    def on_device(images, texts, logit_scale, logit_bias):
        params = jnp.concatenate(
            [logit_scale * -LOG2_E, logit_bias * -LOG2_E, logit_scale]
        ).reshape(1, 3)
        early = {(0, 0): images}
        for h in range(1, high_count):
            early[h, 0] = move(images, high=h)
        for w in range(1, low_count):
            early[0, w] = move(images, low=w)
        late = {}
        for h in range(1, high_count):
            block, params = lax.optimization_barrier((early[h, 0], params))
            for w in range(1, low_count):
                late[h, w] = move(block, low=w)
        near_rows = [units([texts], "own_units")] + [move(texts, near=n) for n in range(1, near_count)]
        own_stack = stack_units(near_rows)
        stacks = [own_stack] + [move(own_stack, grp=g) for g in range(1, grp_count)]
        image_parts, text_parts = pair_terms(
            params, list(early.values()), list(late.values()), stacks
        )
        far_parts = dict(zip([*early, *late], image_parts))
        came = [move(part, grp=-g) for g, part in enumerate(text_parts) if g]
        far_came = [move(p, high=-h, low=-w) for (h, w), p in far_parts.items() if h]
        near_parts = add_stacks([text_parts[0], *came], near_count)
        near_parts = [near_parts[0]] + [
            move(part, near=-n) for n, part in enumerate(near_parts) if n
        ]
        low_part = far_parts[0, low_count - 1]
        low_parts = lax.all_to_all(
            jnp.broadcast_to(low_part, (low_count,) + low_part.shape),
            AXES, 0, 0, axis_index_groups=low_groups, tiled=True,
        )
        low_at = lax.axis_index("dev") // near_count % low_count
        return finish(
            images,
            texts,
            low_at.reshape(1),
            low_parts,
            [(0, part) for part in [far_parts[0, 0]] + far_came]
            + [(1, part) for part in near_parts],
        )

    in_specs = (P(AXES, None), P(AXES, None), P(), P())
    out_specs = (P(AXES, None), P(AXES, None))
    return jax.shard_map(
        on_device, mesh=mesh, in_specs=in_specs, out_specs=out_specs, check_vma=False
    )
```

```python
import functools
import math

import jax
import jax.numpy as jnp
from jax import lax
from jax.experimental import pallas as pl
from jax.experimental.pallas import tpu as pltpu
from jax.sharding import PartitionSpec as P

AXES = ("grp", "dev")
VMEM_LIMIT = 32 * 1024 * 1024
SPAN = 256
PIECE = 32
LATE = 30000
LOG2_E = math.log2(math.e)
VMEM = pl.BlockSpec(memory_space=pltpu.VMEM)


def unit_rows(raw):
    wide = raw.astype(jnp.float32)
    factor = lax.rsqrt(jnp.sum(wide * wide, axis=-1, keepdims=True) + 1e-06)
    return wide * factor, factor


def call(kernel, out_shape, operands, scratch=(), flops=0, transcendentals=0, name=None):
    touched = sum(x.size * x.dtype.itemsize for x in list(operands) + list(out_shape))
    outs = pl.pallas_call(
        kernel,
        out_shape=out_shape,
        in_specs=[VMEM] * len(operands),
        out_specs=[VMEM] * len(out_shape),
        scratch_shapes=scratch,
        compiler_params=pltpu.CompilerParams(vmem_limit_bytes=VMEM_LIMIT),
        cost_estimate=pl.CostEstimate(
            flops=flops, bytes_accessed=touched, transcendentals=transcendentals
        ),
        name=name,
    )(*operands)
    return tuple(outs)


def units_kernel(*refs):
    rows = refs[0].shape[0]
    for at, ref in enumerate(refs[:-1]):
        refs[-1][at * rows:(at + 1) * rows, :] = unit_rows(ref[...])[0].astype(refs[-1].dtype)


def units(blocks, name, weight=1):
    rows, width = blocks[0].shape
    out = jax.ShapeDtypeStruct((len(blocks) * rows, width), jnp.bfloat16)
    return call(units_kernel, [out], blocks, flops=4 * weight * out.size, name=name)[0]


def stack_units_kernel(*refs):
    out = refs[-1]
    rows = refs[0].shape[0]
    out[:rows, :] = refs[0][...]
    for at, ref in enumerate(refs[1:-1], 1):
        out[at * rows:(at + 1) * rows, :] = unit_rows(ref[...])[0].astype(out.dtype)


def stack_units(blocks):
    rows, width = blocks[0].shape
    out = jax.ShapeDtypeStruct((len(blocks) * rows, width), jnp.bfloat16)
    return call(stack_units_kernel, [out], blocks, flops=4 * out.size, name="stack_units")[0]


def pairs(vi, params_ref, text_ref, text_out, own=0, text_add=None):
    slope, shift, temper = (params_ref[0:1, at:at + 1] for at in range(3))
    held = text_ref.shape[0]
    total = None

    def dots_of(first):
        return lax.dot_general(
            vi,
            text_ref[first:min(first + SPAN, held), :],
            (((1,), (1,)), ((), ())),
            preferred_element_type=jnp.float32,
        )

    coming = dots_of(0)
    for first in range(0, held, SPAN):
        last = min(first + SPAN, held)
        dots, coming = coming, dots_of(last) if last < held else None
        vt = text_ref[first:last, :]
        e = jnp.exp2(slope * dots + shift)
        chance = pl.reciprocal(1.0 + e, approx=True)
        if own and first == 0:
            row = lax.broadcasted_iota(jnp.int32, chance.shape, 0)
            column = lax.broadcasted_iota(jnp.int32, chance.shape, 1)
            same = (row == column) & (row < own)
            chance = jnp.where(same, -e * chance, chance)
        coefficient = (temper * chance).astype(jnp.bfloat16)
        text_part = lax.dot_general(
            coefficient, vi, (((0,), (0,)), ((), ())), preferred_element_type=jnp.float32
        )
        if text_add is not None:
            text_part = text_add[first:last, :] + text_part
        text_out[first:last, :] = text_part.astype(text_out.dtype)
        part = jnp.dot(coefficient, vt, preferred_element_type=jnp.float32)
        total = part if total is None else total + part
    return total


def early_pairs_kernel(params_ref, text_ref, *refs):
    image_refs, (text_out, units_out, total_out) = refs[:-3], refs[-3:]
    rows = image_refs[0].shape[0]
    for a, ref in enumerate(image_refs):
        units_out[a * rows:(a + 1) * rows, :] = unit_rows(ref[...])[0].astype(jnp.bfloat16)
    total_out[...] = pairs(units_out[...], params_ref, text_ref, text_out, own=rows)


def rest_pairs_kernel(
    count, params_ref, early_ref, total_ref, own_text_ref, own_add_ref, late_ref, *refs
):
    text_refs, own_out = refs[:count], refs[count]
    other_out, image_out = refs[count + 1:2 * count + 1], refs[2 * count + 1:]
    rows = image_out[0].shape[0]
    early, late = early_ref[...], late_ref[...]
    total = jnp.concatenate(
        [
            total_ref[...],
            pairs(late, params_ref, own_text_ref, own_out, text_add=own_add_ref),
        ],
        axis=0,
    )
    vi = jnp.concatenate([early, late], axis=0)
    for text_ref, out in zip(text_refs, other_out):
        total = total + pairs(vi, params_ref, text_ref, out)
    for a, ref in enumerate(image_out):
        ref[...] = total[a * rows:(a + 1) * rows, :].astype(ref.dtype)


def pair_terms(params, early, late, texts):
    rows, width = early[0].shape
    early_rows, late_rows = rows * len(early), rows * len(late)
    own, others = texts[0], texts[1:]
    other_rows = sum(t.shape[0] for t in others)

    def cost(pair_count):
        return dict(flops=6 * pair_count * width, transcendentals=2 * pair_count)

    own_add, early_units, total = call(
        early_pairs_kernel,
        [
            jax.ShapeDtypeStruct(own.shape, jnp.float32),
            jax.ShapeDtypeStruct((early_rows, width), jnp.bfloat16),
            jax.ShapeDtypeStruct((early_rows, width), jnp.float32),
        ],
        [params, own, *early],
        name="early_pairs",
        **cost(early_rows * own.shape[0]),
    )
    late_units = units(late, "late_units", LATE)
    outs = call(
        functools.partial(rest_pairs_kernel, len(others)),
        [jax.ShapeDtypeStruct(own.shape, jnp.float32)]
        + [jax.ShapeDtypeStruct(t.shape, jnp.bfloat16) for t in others]
        + [jax.ShapeDtypeStruct((rows, width), jnp.float32)]
        + [jax.ShapeDtypeStruct((rows, width), jnp.bfloat16)] * (len(early) + len(late) - 1),
        [params, early_units, total, own, own_add, late_units, *others],
        name="rest_pairs",
        **cost(late_rows * own.shape[0] + (early_rows + late_rows) * other_rows),
    )
    count = 1 + len(others)
    return outs[count:], outs[:count]


def add_stacks_kernel(part_count, *refs):
    parts, outs = refs[:part_count], refs[part_count:]
    rows = outs[0].shape[0]
    for at, out in enumerate(outs):
        total = parts[0][at * rows:(at + 1) * rows, :].astype(jnp.float32)
        for part in parts[1:]:
            total = total + part[at * rows:(at + 1) * rows, :].astype(jnp.float32)
        out[...] = total.astype(out.dtype)


def add_stacks(parts, count):
    shape = (parts[0].shape[0] // count, parts[0].shape[1])
    types = [jnp.float32] + [jnp.bfloat16] * (count - 1)
    return call(
        functools.partial(add_stacks_kernel, len(parts)),
        [jax.ShapeDtypeStruct(shape, t) for t in types],
        parts,
        flops=len(parts) * parts[0].size,
        name="add_stacks",
    )


def finish_kernel(sides, image_ref, text_ref, *refs):
    parts, outs = refs[:len(sides)], refs[len(sides):len(sides) + 2]
    staged, sems = refs[len(sides) + 2:]
    rows = image_ref.shape[0]
    piece = math.gcd(rows, PIECE)
    copies = []
    for side, raw in enumerate((image_ref, text_ref)):
        for first in range(0, rows, piece):
            here = pl.ds(first, piece)
            unit, factor = unit_rows(raw[here, :])
            total = sum(
                ref[here, :].astype(jnp.float32) for at, ref in zip(sides, parts) if at == side
            )
            along = jnp.sum(unit * total, axis=-1, keepdims=True)
            staged[side, here, :] = factor * (total - unit * along)
            copies.append(
                pltpu.make_async_copy(
                    staged.at[side, here, :], outs[side].at[here, :], sems.at[len(copies)]
                )
            )
            copies[-1].start()
    for copy in copies:
        copy.wait()


def finish(images, texts, parts):
    out = jax.ShapeDtypeStruct(images.shape, jnp.float32)
    return pl.pallas_call(
        functools.partial(finish_kernel, [side for side, _ in parts]),
        out_shape=(out, out),
        in_specs=[VMEM] * (2 + len(parts)),
        out_specs=[pl.BlockSpec(memory_space=pl.ANY)] * 2,
        scratch_shapes=[
            pltpu.VMEM((2,) + images.shape, jnp.float32),
            pltpu.SemaphoreType.DMA((2 * (images.shape[0] // math.gcd(images.shape[0], PIECE)),)),
        ],
        compiler_params=pltpu.CompilerParams(vmem_limit_bytes=VMEM_LIMIT),
        cost_estimate=pl.CostEstimate(
            flops=10 * len(parts) * images.size,
            bytes_accessed=3 * len(parts) * images.size,
            transcendentals=0,
        ),
        name="finish",
    )(images, texts, *[part for _, part in parts])


def plan(grp_count, dev_count):
    options = [n for n in range(1, dev_count + 1) if dev_count % n == 0]
    near = min(options, key=lambda n: (dev_count // n + grp_count * n, -n))
    return dev_count // near, near


def step_to(at, by, count):
    if count & (count - 1) == 0:
        return at ^ abs(by)
    return (at + by) % count


def solution(mesh):
    grp_count, dev_count = mesh.shape["grp"], mesh.shape["dev"]
    far_count, near_count = plan(grp_count, dev_count)
    low_count = 2 if far_count % 2 == 0 else 1
    high_count = far_count // low_count

    def move(value, grp=0, high=0, low=0, near=0):
        perm = []
        for g in range(grp_count):
            for h in range(high_count):
                for w in range(low_count):
                    for n in range(near_count):
                        source = ((g * high_count + h) * low_count + w) * near_count + n
                        g2 = step_to(g, grp, grp_count)
                        h2 = step_to(h, high, high_count)
                        w2 = step_to(w, low, low_count)
                        n2 = step_to(n, near, near_count)
                        target = ((g2 * high_count + h2) * low_count + w2) * near_count + n2
                        perm.append((source, target))
        return lax.ppermute(value, AXES, perm)

    def on_device(images, texts, logit_scale, logit_bias):
        params = jnp.concatenate(
            [logit_scale * -LOG2_E, logit_bias * -LOG2_E, logit_scale]
        ).reshape(1, 3)
        early = {(0, 0): images}
        for h in range(1, high_count):
            early[h, 0] = move(images, high=h)
        for w in range(1, low_count):
            early[0, w] = move(images, low=w)
        late = {}
        for h in range(1, high_count):
            block, params = lax.optimization_barrier((early[h, 0], params))
            for w in range(1, low_count):
                late[h, w] = move(block, low=w)
        near_rows = [units([texts], "own_units")] + [move(texts, near=n) for n in range(1, near_count)]
        own_stack = stack_units(near_rows)
        stacks = [own_stack] + [move(own_stack, grp=g) for g in range(1, grp_count)]
        image_parts, text_parts = pair_terms(
            params, list(early.values()), list(late.values()), stacks
        )
        far_parts = dict(zip([*early, *late], image_parts))
        came = [move(part, grp=-g) for g, part in enumerate(text_parts) if g]
        far_came = [move(p, high=-h, low=-w) for (h, w), p in far_parts.items() if h]
        near_parts = add_stacks([text_parts[0], *came], near_count)
        near_parts = [near_parts[0]] + [
            move(part, near=-n) for n, part in enumerate(near_parts) if n
        ]
        low_parts = [p for (h, w), p in far_parts.items() if w and not h]
        low_parts, far_came[:1], near_parts[:2] = lax.optimization_barrier(
            (low_parts, far_came[:1], near_parts[:2])
        )
        far_came += [move(part, low=-w) for w, part in enumerate(low_parts, 1)]
        return finish(
            images,
            texts,
            [(0, part) for part in [far_parts[0, 0]] + far_came]
            + [(1, part) for part in near_parts],
        )

    in_specs = (P(AXES, None), P(AXES, None), P(), P())
    out_specs = (P(AXES, None), P(AXES, None))
    return jax.shard_map(
        on_device, mesh=mesh, in_specs=in_specs, out_specs=out_specs, check_vma=False
    )
```

```python
import functools
import math

import jax
import jax.numpy as jnp
from jax import lax
from jax.experimental import pallas as pl
from jax.experimental.pallas import tpu as pltpu
from jax.sharding import PartitionSpec as P

AXES = ("grp", "dev")
VMEM_LIMIT = 32 * 1024 * 1024
SPAN = 256
PIECE = 32
LATE = 30000
LOG2_E = math.log2(math.e)
VMEM = pl.BlockSpec(memory_space=pltpu.VMEM)


def unit_rows(raw):
    wide = raw.astype(jnp.float32)
    factor = lax.rsqrt(jnp.sum(wide * wide, axis=-1, keepdims=True) + 1e-06)
    return wide * factor, factor


def call(kernel, out_shape, operands, scratch=(), flops=0, transcendentals=0, name=None):
    touched = sum(x.size * x.dtype.itemsize for x in list(operands) + list(out_shape))
    outs = pl.pallas_call(
        kernel,
        out_shape=out_shape,
        in_specs=[VMEM] * len(operands),
        out_specs=[VMEM] * len(out_shape),
        scratch_shapes=scratch,
        compiler_params=pltpu.CompilerParams(vmem_limit_bytes=VMEM_LIMIT),
        cost_estimate=pl.CostEstimate(
            flops=flops, bytes_accessed=touched, transcendentals=transcendentals
        ),
        name=name,
    )(*operands)
    return tuple(outs)


def units_kernel(*refs):
    rows = refs[0].shape[0]
    for at, ref in enumerate(refs[:-1]):
        refs[-1][at * rows:(at + 1) * rows, :] = unit_rows(ref[...])[0].astype(refs[-1].dtype)


def units(blocks, name, weight=1):
    rows, width = blocks[0].shape
    out = jax.ShapeDtypeStruct((len(blocks) * rows, width), jnp.bfloat16)
    return call(units_kernel, [out], blocks, flops=4 * weight * out.size, name=name)[0]


def stack_units_kernel(*refs):
    out = refs[-1]
    rows = refs[0].shape[0]
    out[:rows, :] = refs[0][...]
    for at, ref in enumerate(refs[1:-1], 1):
        out[at * rows:(at + 1) * rows, :] = unit_rows(ref[...])[0].astype(out.dtype)


def stack_units(blocks):
    rows, width = blocks[0].shape
    out = jax.ShapeDtypeStruct((len(blocks) * rows, width), jnp.bfloat16)
    return call(stack_units_kernel, [out], blocks, flops=4 * out.size, name="stack_units")[0]


def pairs(vi, params_ref, text_ref, text_out, own=0, text_add=None):
    slope, shift, temper = (params_ref[0:1, at:at + 1] for at in range(3))
    held = text_ref.shape[0]
    total = None

    def dots_of(first):
        return lax.dot_general(
            vi,
            text_ref[first:min(first + SPAN, held), :],
            (((1,), (1,)), ((), ())),
            preferred_element_type=jnp.float32,
        )

    coming = dots_of(0)
    for first in range(0, held, SPAN):
        last = min(first + SPAN, held)
        dots, coming = coming, dots_of(last) if last < held else None
        vt = text_ref[first:last, :]
        e = jnp.exp2(slope * dots + shift)
        chance = pl.reciprocal(1.0 + e, approx=True)
        if own and first == 0:
            row = lax.broadcasted_iota(jnp.int32, chance.shape, 0)
            column = lax.broadcasted_iota(jnp.int32, chance.shape, 1)
            same = (row == column) & (row < own)
            chance = jnp.where(same, -e * chance, chance)
        coefficient = (temper * chance).astype(jnp.bfloat16)
        text_part = lax.dot_general(
            coefficient, vi, (((0,), (0,)), ((), ())), preferred_element_type=jnp.float32
        )
        if text_add is not None:
            text_part = text_add[first:last, :] + text_part
        text_out[first:last, :] = text_part.astype(text_out.dtype)
        part = jnp.dot(coefficient, vt, preferred_element_type=jnp.float32)
        total = part if total is None else total + part
    return total


def early_pairs_kernel(params_ref, text_ref, *refs):
    image_refs, (text_out, units_out, total_out) = refs[:-3], refs[-3:]
    rows = image_refs[0].shape[0]
    for a, ref in enumerate(image_refs):
        units_out[a * rows:(a + 1) * rows, :] = unit_rows(ref[...])[0].astype(jnp.bfloat16)
    total_out[...] = pairs(units_out[...], params_ref, text_ref, text_out, own=rows)


def rest_pairs_kernel(
    count, params_ref, early_ref, total_ref, own_text_ref, own_add_ref, late_ref, *refs
):
    text_refs, own_out = refs[:count], refs[count]
    other_out, image_out = refs[count + 1:2 * count + 1], refs[2 * count + 1:]
    rows = image_out[0].shape[0]
    early, late = early_ref[...], late_ref[...]
    total = jnp.concatenate(
        [
            total_ref[...],
            pairs(late, params_ref, own_text_ref, own_out, text_add=own_add_ref),
        ],
        axis=0,
    )
    vi = jnp.concatenate([early, late], axis=0)
    for text_ref, out in zip(text_refs, other_out):
        total = total + pairs(vi, params_ref, text_ref, out)
    for a, ref in enumerate(image_out):
        ref[...] = total[a * rows:(a + 1) * rows, :].astype(ref.dtype)


def pair_terms(params, early, late, texts, image_types):
    rows, width = early[0].shape
    early_rows, late_rows = rows * len(early), rows * len(late)
    own, others = texts[0], texts[1:]
    other_rows = sum(t.shape[0] for t in others)

    def cost(pair_count):
        return dict(flops=6 * pair_count * width, transcendentals=2 * pair_count)

    own_add, early_units, total = call(
        early_pairs_kernel,
        [
            jax.ShapeDtypeStruct(own.shape, jnp.float32),
            jax.ShapeDtypeStruct((early_rows, width), jnp.bfloat16),
            jax.ShapeDtypeStruct((early_rows, width), jnp.float32),
        ],
        [params, own, *early],
        name="early_pairs",
        **cost(early_rows * own.shape[0]),
    )
    late_units = units(late, "late_units", LATE)
    outs = call(
        functools.partial(rest_pairs_kernel, len(others)),
        [jax.ShapeDtypeStruct(own.shape, jnp.float32)]
        + [jax.ShapeDtypeStruct(t.shape, jnp.bfloat16) for t in others]
        + [jax.ShapeDtypeStruct((rows, width), t) for t in image_types],
        [params, early_units, total, own, own_add, late_units, *others],
        name="rest_pairs",
        **cost(late_rows * own.shape[0] + (early_rows + late_rows) * other_rows),
    )
    count = 1 + len(others)
    return outs[count:], outs[:count]


def add_stacks_kernel(part_count, *refs):
    parts, outs = refs[:part_count], refs[part_count:]
    rows = outs[0].shape[0]
    for at, out in enumerate(outs):
        total = parts[0][at * rows:(at + 1) * rows, :].astype(jnp.float32)
        for part in parts[1:]:
            total = total + part[at * rows:(at + 1) * rows, :].astype(jnp.float32)
        out[...] = total.astype(out.dtype)


def add_stacks(parts, count):
    shape = (parts[0].shape[0] // count, parts[0].shape[1])
    types = [jnp.float32] + [jnp.bfloat16] * (count - 1)
    return call(
        functools.partial(add_stacks_kernel, len(parts)),
        [jax.ShapeDtypeStruct(shape, t) for t in types],
        parts,
        flops=len(parts) * parts[0].size,
        name="add_stacks",
    )


def add_parts_kernel(*refs):
    total = refs[0][...].astype(jnp.float32)
    for part in refs[1:-1]:
        total = total + part[...].astype(jnp.float32)
    refs[-1][...] = total.astype(refs[-1].dtype)


def add_parts(parts):
    out = jax.ShapeDtypeStruct(parts[0].shape, jnp.bfloat16)
    return call(
        add_parts_kernel, [out], parts, flops=len(parts) * out.size, name="add_parts"
    )[0]


def finish_kernel(sides, image_ref, text_ref, *refs):
    parts, outs = refs[:len(sides)], refs[len(sides):len(sides) + 2]
    staged, sems = refs[len(sides) + 2:]
    rows = image_ref.shape[0]
    piece = math.gcd(rows, PIECE)
    copies = []
    for side, raw in enumerate((image_ref, text_ref)):
        for first in range(0, rows, piece):
            here = pl.ds(first, piece)
            unit, factor = unit_rows(raw[here, :])
            total = sum(
                ref[here, :].astype(jnp.float32) for at, ref in zip(sides, parts) if at == side
            )
            along = jnp.sum(unit * total, axis=-1, keepdims=True)
            staged[side, here, :] = factor * (total - unit * along)
            copies.append(
                pltpu.make_async_copy(
                    staged.at[side, here, :], outs[side].at[here, :], sems.at[len(copies)]
                )
            )
            copies[-1].start()
    for copy in copies:
        copy.wait()


def finish(images, texts, parts):
    out = jax.ShapeDtypeStruct(images.shape, jnp.float32)
    return pl.pallas_call(
        functools.partial(finish_kernel, [side for side, _ in parts]),
        out_shape=(out, out),
        in_specs=[VMEM] * (2 + len(parts)),
        out_specs=[pl.BlockSpec(memory_space=pl.ANY)] * 2,
        scratch_shapes=[
            pltpu.VMEM((2,) + images.shape, jnp.float32),
            pltpu.SemaphoreType.DMA((2 * (images.shape[0] // math.gcd(images.shape[0], PIECE)),)),
        ],
        compiler_params=pltpu.CompilerParams(vmem_limit_bytes=VMEM_LIMIT),
        cost_estimate=pl.CostEstimate(
            flops=10 * len(parts) * images.size,
            bytes_accessed=3 * len(parts) * images.size,
            transcendentals=0,
        ),
        name="finish",
    )(images, texts, *[part for _, part in parts])


def plan(grp_count, dev_count):
    options = [n for n in range(1, dev_count + 1) if dev_count % n == 0]
    near = min(options, key=lambda n: (dev_count // n + grp_count * n, -n))
    return dev_count // near, near


def step_to(at, by, count):
    if count & (count - 1) == 0:
        return at ^ abs(by)
    return (at + by) % count


def solution(mesh):
    grp_count, dev_count = mesh.shape["grp"], mesh.shape["dev"]
    far_count, near_count = plan(grp_count, dev_count)
    low_count = 2 if far_count % 2 == 0 else 1
    high_count = far_count // low_count

    def move(value, grp=0, high=0, low=0, near=0):
        perm = []
        for g in range(grp_count):
            for h in range(high_count):
                for w in range(low_count):
                    for n in range(near_count):
                        source = ((g * high_count + h) * low_count + w) * near_count + n
                        g2 = step_to(g, grp, grp_count)
                        h2 = step_to(h, high, high_count)
                        w2 = step_to(w, low, low_count)
                        n2 = step_to(n, near, near_count)
                        target = ((g2 * high_count + h2) * low_count + w2) * near_count + n2
                        perm.append((source, target))
        return lax.ppermute(value, AXES, perm)

    def on_device(images, texts, logit_scale, logit_bias):
        params = jnp.concatenate(
            [logit_scale * -LOG2_E, logit_bias * -LOG2_E, logit_scale]
        ).reshape(1, 3)
        early = {(0, 0): images}
        for h in range(1, high_count):
            early[h, 0] = move(images, high=h)
        for w in range(1, low_count):
            early[0, w] = move(images, low=w)
        late = {}
        for h in range(1, high_count):
            block, params = lax.optimization_barrier((early[h, 0], params))
            for w in range(1, low_count):
                late[h, w] = move(block, low=w)
        near_rows = [units([texts], "own_units")] + [move(texts, near=n) for n in range(1, near_count)]
        own_stack = stack_units(near_rows)
        stacks = [own_stack] + [move(own_stack, grp=g) for g in range(1, grp_count)]
        far_steps = [*early, *late]
        image_types = [jnp.bfloat16 if w else jnp.float32 for _, w in far_steps]
        image_parts, text_parts = pair_terms(
            params, list(early.values()), list(late.values()), stacks, image_types
        )
        far_parts = dict(zip(far_steps, image_parts))
        passed = {
            h: [move(far_parts[h, w], low=-w) for w in range(1, low_count)]
            for h in range(1, high_count)
        }
        came = [move(part, grp=-g) for g, part in enumerate(text_parts) if g]
        near_parts = list(add_stacks([text_parts[0], *came], near_count))
        high_parts = []
        for h in range(1, high_count):
            passed[h], near_parts[0] = lax.optimization_barrier((passed[h], near_parts[0]))
            high_parts.append(move(add_parts([far_parts[h, 0], *passed[h]]), high=-h))
        near_parts = [near_parts[0]] + [
            move(part, near=-n) for n, part in enumerate(near_parts) if n
        ]
        low_parts = [far_parts[0, w] for w in range(1, low_count)]
        low_parts, near_parts[:2] = lax.optimization_barrier((low_parts, near_parts[:2]))
        low_parts = [move(part, low=-w) for w, part in enumerate(low_parts, 1)]
        return finish(
            images,
            texts,
            [(0, far_parts[0, 0])]
            + [(1, part) for part in near_parts[:3]]
            + [(0, part) for part in high_parts]
            + [(1, part) for part in near_parts[3:]]
            + [(0, part) for part in low_parts],
        )

    in_specs = (P(AXES, None), P(AXES, None), P(), P())
    out_specs = (P(AXES, None), P(AXES, None))
    return jax.shard_map(
        on_device, mesh=mesh, in_specs=in_specs, out_specs=out_specs, check_vma=False
    )
```

```python
import functools
import math

import jax
import jax.numpy as jnp
from jax import lax
from jax.experimental import pallas as pl
from jax.experimental.pallas import tpu as pltpu
from jax.sharding import PartitionSpec as P

AXES = ("grp", "dev")
VMEM_LIMIT = 32 * 1024 * 1024
SPAN = 256
PIECE = 32
LATE = 30000
LOG2_E = math.log2(math.e)
VMEM = pl.BlockSpec(memory_space=pltpu.VMEM)


def unit_rows(raw):
    wide = raw.astype(jnp.float32)
    factor = lax.rsqrt(jnp.sum(wide * wide, axis=-1, keepdims=True) + 1e-06)
    return wide * factor, factor


def call(kernel, out_shape, operands, scratch=(), flops=0, transcendentals=0, name=None):
    touched = sum(x.size * x.dtype.itemsize for x in list(operands) + list(out_shape))
    outs = pl.pallas_call(
        kernel,
        out_shape=out_shape,
        in_specs=[VMEM] * len(operands),
        out_specs=[VMEM] * len(out_shape),
        scratch_shapes=scratch,
        compiler_params=pltpu.CompilerParams(vmem_limit_bytes=VMEM_LIMIT),
        cost_estimate=pl.CostEstimate(
            flops=flops, bytes_accessed=touched, transcendentals=transcendentals
        ),
        name=name,
    )(*operands)
    return tuple(outs)


def units_kernel(*refs):
    rows = refs[0].shape[0]
    for at, ref in enumerate(refs[:-1]):
        refs[-1][at * rows:(at + 1) * rows, :] = unit_rows(ref[...])[0].astype(refs[-1].dtype)


def units(blocks, name, weight=1):
    rows, width = blocks[0].shape
    out = jax.ShapeDtypeStruct((len(blocks) * rows, width), jnp.bfloat16)
    return call(units_kernel, [out], blocks, flops=4 * weight * out.size, name=name)[0]


def stack_units_kernel(*refs):
    out = refs[-1]
    rows = refs[0].shape[0]
    out[:rows, :] = refs[0][...]
    for at, ref in enumerate(refs[1:-1], 1):
        out[at * rows:(at + 1) * rows, :] = unit_rows(ref[...])[0].astype(out.dtype)


def stack_units(blocks):
    rows, width = blocks[0].shape
    out = jax.ShapeDtypeStruct((len(blocks) * rows, width), jnp.bfloat16)
    return call(stack_units_kernel, [out], blocks, flops=4 * out.size, name="stack_units")[0]


def pairs(vi, params_ref, text_ref, text_out, own=0, text_add=None):
    slope, shift, temper = (params_ref[0:1, at:at + 1] for at in range(3))
    held = text_ref.shape[0]
    total = None

    def dots_of(first):
        return lax.dot_general(
            vi,
            text_ref[first:min(first + SPAN, held), :],
            (((1,), (1,)), ((), ())),
            preferred_element_type=jnp.float32,
        )

    coming = dots_of(0)
    for first in range(0, held, SPAN):
        last = min(first + SPAN, held)
        dots, coming = coming, dots_of(last) if last < held else None
        vt = text_ref[first:last, :]
        e = jnp.exp2(slope * dots + shift)
        chance = pl.reciprocal(1.0 + e, approx=True)
        if own and first == 0:
            row = lax.broadcasted_iota(jnp.int32, chance.shape, 0)
            column = lax.broadcasted_iota(jnp.int32, chance.shape, 1)
            same = (row == column) & (row < own)
            chance = jnp.where(same, -e * chance, chance)
        coefficient = (temper * chance).astype(jnp.bfloat16)
        text_part = lax.dot_general(
            coefficient, vi, (((0,), (0,)), ((), ())), preferred_element_type=jnp.float32
        )
        if text_add is not None:
            text_part = text_add[first:last, :] + text_part
        text_out[first:last, :] = text_part.astype(text_out.dtype)
        part = jnp.dot(coefficient, vt, preferred_element_type=jnp.float32)
        total = part if total is None else total + part
    return total


def early_pairs_kernel(params_ref, text_ref, *refs):
    image_refs, (text_out, units_out, total_out) = refs[:-3], refs[-3:]
    rows = image_refs[0].shape[0]
    for a, ref in enumerate(image_refs):
        units_out[a * rows:(a + 1) * rows, :] = unit_rows(ref[...])[0].astype(jnp.bfloat16)
    total_out[...] = pairs(units_out[...], params_ref, text_ref, text_out, own=rows)


def rest_pairs_kernel(
    count, params_ref, early_ref, total_ref, own_text_ref, own_add_ref, late_ref, *refs
):
    text_refs, own_out = refs[:count], refs[count]
    other_out, image_out = refs[count + 1:2 * count + 1], refs[2 * count + 1:]
    rows = image_out[0].shape[0]
    early, late = early_ref[...], late_ref[...]
    total = jnp.concatenate(
        [
            total_ref[...],
            pairs(late, params_ref, own_text_ref, own_out, text_add=own_add_ref),
        ],
        axis=0,
    )
    vi = jnp.concatenate([early, late], axis=0)
    for text_ref, out in zip(text_refs, other_out):
        total = total + pairs(vi, params_ref, text_ref, out)
    for a, ref in enumerate(image_out):
        ref[...] = total[a * rows:(a + 1) * rows, :].astype(ref.dtype)


def pair_terms(params, early, late, texts):
    rows, width = early[0].shape
    early_rows, late_rows = rows * len(early), rows * len(late)
    own, others = texts[0], texts[1:]
    other_rows = sum(t.shape[0] for t in others)

    def cost(pair_count):
        return dict(flops=6 * pair_count * width, transcendentals=2 * pair_count)

    own_add, early_units, total = call(
        early_pairs_kernel,
        [
            jax.ShapeDtypeStruct(own.shape, jnp.float32),
            jax.ShapeDtypeStruct((early_rows, width), jnp.bfloat16),
            jax.ShapeDtypeStruct((early_rows, width), jnp.float32),
        ],
        [params, own, *early],
        name="early_pairs",
        **cost(early_rows * own.shape[0]),
    )
    late_units = units(late, "late_units", LATE)
    outs = call(
        functools.partial(rest_pairs_kernel, len(others)),
        [jax.ShapeDtypeStruct(own.shape, jnp.float32)]
        + [jax.ShapeDtypeStruct(t.shape, jnp.bfloat16) for t in others]
        + [jax.ShapeDtypeStruct((rows, width), jnp.float32)]
        + [jax.ShapeDtypeStruct((rows, width), jnp.bfloat16)] * (len(early) + len(late) - 1),
        [params, early_units, total, own, own_add, late_units, *others],
        name="rest_pairs",
        **cost(late_rows * own.shape[0] + (early_rows + late_rows) * other_rows),
    )
    count = 1 + len(others)
    return outs[count:], outs[:count]


def add_stacks_kernel(part_count, *refs):
    parts, outs = refs[:part_count], refs[part_count:]
    rows = outs[0].shape[0]
    for at, out in enumerate(outs):
        total = parts[0][at * rows:(at + 1) * rows, :].astype(jnp.float32)
        for part in parts[1:]:
            total = total + part[at * rows:(at + 1) * rows, :].astype(jnp.float32)
        out[...] = total.astype(out.dtype)


def add_stacks(parts, count):
    shape = (parts[0].shape[0] // count, parts[0].shape[1])
    types = [jnp.float32] + [jnp.bfloat16] * (count - 1)
    return call(
        functools.partial(add_stacks_kernel, len(parts)),
        [jax.ShapeDtypeStruct(shape, t) for t in types],
        parts,
        flops=len(parts) * parts[0].size,
        name="add_stacks",
    )


def finish_kernel(sides, image_ref, text_ref, *refs):
    parts, outs = refs[:len(sides)], refs[len(sides):len(sides) + 2]
    staged, sems = refs[len(sides) + 2:]
    rows = image_ref.shape[0]
    piece = math.gcd(rows, PIECE)
    copies = []
    for side, raw in enumerate((image_ref, text_ref)):
        for first in range(0, rows, piece):
            here = pl.ds(first, piece)
            unit, factor = unit_rows(raw[here, :])
            total = sum(
                ref[here, :].astype(jnp.float32) for at, ref in zip(sides, parts) if at == side
            )
            along = jnp.sum(unit * total, axis=-1, keepdims=True)
            staged[side, here, :] = factor * (total - unit * along)
            copies.append(
                pltpu.make_async_copy(
                    staged.at[side, here, :], outs[side].at[here, :], sems.at[len(copies)]
                )
            )
            copies[-1].start()
    for copy in copies:
        copy.wait()


def finish(images, texts, parts):
    out = jax.ShapeDtypeStruct(images.shape, jnp.float32)
    return pl.pallas_call(
        functools.partial(finish_kernel, [side for side, _ in parts]),
        out_shape=(out, out),
        in_specs=[VMEM] * (2 + len(parts)),
        out_specs=[pl.BlockSpec(memory_space=pl.ANY)] * 2,
        scratch_shapes=[
            pltpu.VMEM((2,) + images.shape, jnp.float32),
            pltpu.SemaphoreType.DMA((2 * (images.shape[0] // math.gcd(images.shape[0], PIECE)),)),
        ],
        compiler_params=pltpu.CompilerParams(vmem_limit_bytes=VMEM_LIMIT),
        cost_estimate=pl.CostEstimate(
            flops=10 * len(parts) * images.size,
            bytes_accessed=3 * len(parts) * images.size,
            transcendentals=0,
        ),
        name="finish",
    )(images, texts, *[part for _, part in parts])


def plan(grp_count, dev_count):
    options = [n for n in range(1, dev_count + 1) if dev_count % n == 0]
    near = min(options, key=lambda n: (dev_count // n + grp_count * n, -n))
    return dev_count // near, near


def step_to(at, by, count):
    if count & (count - 1) == 0:
        return at ^ abs(by)
    return (at + by) % count


def solution(mesh):
    grp_count, dev_count = mesh.shape["grp"], mesh.shape["dev"]
    far_count, near_count = plan(grp_count, dev_count)
    low_count = 2 if far_count % 2 == 0 else 1
    high_count = far_count // low_count

    def move(value, grp=0, high=0, low=0, near=0):
        perm = []
        for g in range(grp_count):
            for h in range(high_count):
                for w in range(low_count):
                    for n in range(near_count):
                        source = ((g * high_count + h) * low_count + w) * near_count + n
                        g2 = step_to(g, grp, grp_count)
                        h2 = step_to(h, high, high_count)
                        w2 = step_to(w, low, low_count)
                        n2 = step_to(n, near, near_count)
                        target = ((g2 * high_count + h2) * low_count + w2) * near_count + n2
                        perm.append((source, target))
        return lax.ppermute(value, AXES, perm)

    def on_device(images, texts, logit_scale, logit_bias):
        params = jnp.concatenate(
            [logit_scale * -LOG2_E, logit_bias * -LOG2_E, logit_scale]
        ).reshape(1, 3)
        early = {(0, 0): images}
        for h in range(1, high_count):
            early[h, 0] = move(images, high=h)
        for w in range(1, low_count):
            early[0, w] = move(images, low=w)
        late = {}
        for h in range(1, high_count):
            block, params = lax.optimization_barrier((early[h, 0], params))
            for w in range(1, low_count):
                late[h, w] = move(block, low=w)
        near_rows = [units([texts], "own_units")] + [move(texts, near=n) for n in range(1, near_count)]
        own_stack = stack_units(near_rows)
        stacks = [own_stack] + [move(own_stack, grp=g) for g in range(1, grp_count)]
        image_parts, text_parts = pair_terms(
            params, list(early.values()), list(late.values()), stacks
        )
        far_parts = dict(zip([*early, *late], image_parts))
        came = [move(part, grp=-g) for g, part in enumerate(text_parts) if g]
        far_order = sorted((step for step in far_parts if step != (0, 0)), key=lambda step: step[0])
        far_came = [move(far_parts[h, w], high=-h, low=-w) for h, w in far_order]
        near_parts = add_stacks([text_parts[0], *came], near_count)
        near_parts = [near_parts[0]] + [
            move(part, near=-n) for n, part in enumerate(near_parts) if n
        ]
        return finish(
            images,
            texts,
            [(0, part) for part in [far_parts[0, 0]] + far_came]
            + [(1, part) for part in near_parts],
        )

    in_specs = (P(AXES, None), P(AXES, None), P(), P())
    out_specs = (P(AXES, None), P(AXES, None))
    return jax.shard_map(
        on_device, mesh=mesh, in_specs=in_specs, out_specs=out_specs, check_vma=False
    )
```

```python
import functools
import math

import jax
import jax.numpy as jnp
from jax import lax
from jax.experimental import pallas as pl
from jax.experimental.pallas import tpu as pltpu
from jax.sharding import PartitionSpec as P

AXES = ("grp", "dev")
VMEM_LIMIT = 32 * 1024 * 1024
SPAN = 256
PIECE = 32
LATE = 30000
FAR = 60000
LOG2_E = math.log2(math.e)
VMEM = pl.BlockSpec(memory_space=pltpu.VMEM)


def unit_rows(raw):
    wide = raw.astype(jnp.float32)
    factor = lax.rsqrt(jnp.sum(wide * wide, axis=-1, keepdims=True) + 1e-06)
    return wide * factor, factor


def call(kernel, out_shape, operands, scratch=(), flops=0, transcendentals=0, name=None):
    touched = sum(x.size * x.dtype.itemsize for x in list(operands) + list(out_shape))
    outs = pl.pallas_call(
        kernel,
        out_shape=out_shape,
        in_specs=[VMEM] * len(operands),
        out_specs=[VMEM] * len(out_shape),
        scratch_shapes=scratch,
        compiler_params=pltpu.CompilerParams(vmem_limit_bytes=VMEM_LIMIT),
        cost_estimate=pl.CostEstimate(
            flops=flops, bytes_accessed=touched, transcendentals=transcendentals
        ),
        name=name,
    )(*operands)
    return tuple(outs)


def units_kernel(*refs):
    rows = refs[0].shape[0]
    for at, ref in enumerate(refs[:-1]):
        refs[-1][at * rows:(at + 1) * rows, :] = unit_rows(ref[...])[0].astype(refs[-1].dtype)


def units(blocks, name, weight=1):
    rows, width = blocks[0].shape
    out = jax.ShapeDtypeStruct((len(blocks) * rows, width), jnp.bfloat16)
    return call(units_kernel, [out], blocks, flops=4 * weight * out.size, name=name)[0]


def stack_units_kernel(*refs):
    out = refs[-1]
    rows = refs[0].shape[0]
    out[:rows, :] = refs[0][...]
    for at, ref in enumerate(refs[1:-1], 1):
        out[at * rows:(at + 1) * rows, :] = unit_rows(ref[...])[0].astype(out.dtype)


def stack_units(blocks):
    rows, width = blocks[0].shape
    out = jax.ShapeDtypeStruct((len(blocks) * rows, width), jnp.bfloat16)
    return call(stack_units_kernel, [out], blocks, flops=4 * out.size, name="stack_units")[0]


def pairs(vi, params_ref, text_ref, text_out, own=0, text_add=None):
    slope, shift, temper = (params_ref[0:1, at:at + 1] for at in range(3))
    held = text_ref.shape[0]
    total = None

    def dots_of(first):
        return lax.dot_general(
            vi,
            text_ref[first:min(first + SPAN, held), :],
            (((1,), (1,)), ((), ())),
            preferred_element_type=jnp.float32,
        )

    coming = dots_of(0)
    for first in range(0, held, SPAN):
        last = min(first + SPAN, held)
        dots, coming = coming, dots_of(last) if last < held else None
        vt = text_ref[first:last, :]
        e = jnp.exp2(slope * dots + shift)
        chance = pl.reciprocal(1.0 + e, approx=True)
        if own and first == 0:
            row = lax.broadcasted_iota(jnp.int32, chance.shape, 0)
            column = lax.broadcasted_iota(jnp.int32, chance.shape, 1)
            same = (row == column) & (row < own)
            chance = jnp.where(same, -e * chance, chance)
        coefficient = (temper * chance).astype(jnp.bfloat16)
        text_part = lax.dot_general(
            coefficient, vi, (((0,), (0,)), ((), ())), preferred_element_type=jnp.float32
        )
        if text_add is not None:
            text_part = text_add[first:last, :] + text_part
        text_out[first:last, :] = text_part.astype(text_out.dtype)
        part = jnp.dot(coefficient, vt, preferred_element_type=jnp.float32)
        total = part if total is None else total + part
    return total


def early_pairs_kernel(params_ref, text_ref, *refs):
    image_refs, (text_out, units_out, total_out) = refs[:-3], refs[-3:]
    rows = image_refs[0].shape[0]
    for a, ref in enumerate(image_refs):
        units_out[a * rows:(a + 1) * rows, :] = unit_rows(ref[...])[0].astype(jnp.bfloat16)
    total_out[...] = pairs(units_out[...], params_ref, text_ref, text_out, own=rows)


def early_rest_kernel(count, params_ref, units_ref, total_ref, *refs):
    text_refs, text_out, image_out = refs[:count], refs[count:2 * count], refs[2 * count:]
    rows = image_out[0].shape[0]
    vi, total = units_ref[...], total_ref[...]
    for text_ref, out in zip(text_refs, text_out):
        total = total + pairs(vi, params_ref, text_ref, out)
    for a, ref in enumerate(image_out):
        ref[...] = total[a * rows:(a + 1) * rows, :].astype(ref.dtype)


def late_pairs_kernel(count, params_ref, units_ref, *refs):
    text_refs, add_refs = refs[:count], refs[count:2 * count]
    text_out, image_out = refs[2 * count:3 * count], refs[3 * count:]
    rows = image_out[0].shape[0]
    total = sum(
        pairs(units_ref[...], params_ref, text_ref, out, text_add=add)
        for text_ref, add, out in zip(text_refs, add_refs, text_out)
    )
    for a, ref in enumerate(image_out):
        ref[...] = total[a * rows:(a + 1) * rows, :].astype(ref.dtype)


def pair_terms(params, early, late, texts):
    rows, width = early[0].shape
    early_rows, late_rows = rows * len(early), rows * len(late)
    own, others = texts[0], texts[1:]
    other_rows = sum(t.shape[0] for t in others)
    part = jax.ShapeDtypeStruct((rows, width), jnp.bfloat16)

    def cost(pair_count):
        return dict(flops=6 * pair_count * width, transcendentals=2 * pair_count)

    def text_sums(stacks, dtype):
        return [jax.ShapeDtypeStruct(t.shape, dtype) for t in stacks]

    own_add, early_units, total = call(
        early_pairs_kernel,
        [
            *text_sums([own], jnp.float32),
            jax.ShapeDtypeStruct((early_rows, width), jnp.bfloat16),
            jax.ShapeDtypeStruct((early_rows, width), jnp.float32),
        ],
        [params, own, *early],
        name="early_pairs",
        **cost(early_rows * own.shape[0]),
    )
    late_units = units(late, "late_units", LATE)
    late_units, total = lax.optimization_barrier((late_units, total))
    outs = call(
        functools.partial(early_rest_kernel, len(others)),
        text_sums(others, jnp.float32)
        + [jax.ShapeDtypeStruct((rows, width), jnp.float32)]
        + [part] * (len(early) - 1),
        [params, early_units, total, *others],
        name="early_rest",
        **cost(early_rows * other_rows),
    )
    other_adds, early_parts = outs[:len(others)], outs[len(others):]
    outs = call(
        functools.partial(late_pairs_kernel, len(texts)),
        text_sums([own], jnp.float32) + text_sums(others, jnp.bfloat16) + [part] * len(late),
        [params, late_units, *texts, own_add, *other_adds],
        name="late_pairs",
        **cost(late_rows * (own.shape[0] + other_rows)),
    )
    return early_parts, outs[len(texts):], outs[:len(texts)]


def add_stacks_kernel(part_count, *refs):
    parts, outs = refs[:part_count], refs[part_count:]
    rows = outs[0].shape[0]
    for at, out in enumerate(outs):
        total = parts[0][at * rows:(at + 1) * rows, :].astype(jnp.float32)
        for part in parts[1:]:
            total = total + part[at * rows:(at + 1) * rows, :].astype(jnp.float32)
        out[...] = total.astype(out.dtype)


def add_stacks(parts, count):
    shape = (parts[0].shape[0] // count, parts[0].shape[1])
    types = [jnp.float32] + [jnp.bfloat16] * (count - 1)
    return call(
        functools.partial(add_stacks_kernel, len(parts)),
        [jax.ShapeDtypeStruct(shape, t) for t in types],
        parts,
        flops=len(parts) * parts[0].size,
        name="add_stacks",
    )


def add_far_kernel(*refs):
    refs[-1][...] = sum(ref[...].astype(jnp.float32) for ref in refs[:-1])


def add_far(parts):
    out = jax.ShapeDtypeStruct(parts[0].shape, jnp.float32)
    return call(
        add_far_kernel, [out], parts, flops=FAR * len(parts) * out.size, name="add_far"
    )[0]


def finish_kernel(sides, image_ref, text_ref, *refs):
    parts, outs = refs[:len(sides)], refs[len(sides):len(sides) + 2]
    staged, sems = refs[len(sides) + 2:]
    rows = image_ref.shape[0]
    piece = math.gcd(rows, PIECE)
    copies = []
    for side, raw in enumerate((image_ref, text_ref)):
        for first in range(0, rows, piece):
            here = pl.ds(first, piece)
            unit, factor = unit_rows(raw[here, :])
            total = sum(
                ref[here, :].astype(jnp.float32) for at, ref in zip(sides, parts) if at == side
            )
            along = jnp.sum(unit * total, axis=-1, keepdims=True)
            staged[side, here, :] = factor * (total - unit * along)
            copies.append(
                pltpu.make_async_copy(
                    staged.at[side, here, :], outs[side].at[here, :], sems.at[len(copies)]
                )
            )
            copies[-1].start()
    for copy in copies:
        copy.wait()


def finish(images, texts, parts):
    out = jax.ShapeDtypeStruct(images.shape, jnp.float32)
    return pl.pallas_call(
        functools.partial(finish_kernel, [side for side, _ in parts]),
        out_shape=(out, out),
        in_specs=[VMEM] * (2 + len(parts)),
        out_specs=[pl.BlockSpec(memory_space=pl.ANY)] * 2,
        scratch_shapes=[
            pltpu.VMEM((2,) + images.shape, jnp.float32),
            pltpu.SemaphoreType.DMA((2 * (images.shape[0] // math.gcd(images.shape[0], PIECE)),)),
        ],
        compiler_params=pltpu.CompilerParams(vmem_limit_bytes=VMEM_LIMIT),
        cost_estimate=pl.CostEstimate(
            flops=10 * len(parts) * images.size,
            bytes_accessed=3 * len(parts) * images.size,
            transcendentals=0,
        ),
        name="finish",
    )(images, texts, *[part for _, part in parts])


def plan(grp_count, dev_count):
    options = [n for n in range(1, dev_count + 1) if dev_count % n == 0]
    near = min(options, key=lambda n: (dev_count // n + grp_count * n, -n))
    return dev_count // near, near


def step_to(at, by, count):
    if count & (count - 1) == 0:
        return at ^ abs(by)
    return (at + by) % count


def solution(mesh):
    grp_count, dev_count = mesh.shape["grp"], mesh.shape["dev"]
    far_count, near_count = plan(grp_count, dev_count)
    low_count = 2 if far_count % 2 == 0 else 1
    high_count = far_count // low_count

    def move(value, grp=0, high=0, low=0, near=0):
        perm = []
        for g in range(grp_count):
            for h in range(high_count):
                for w in range(low_count):
                    for n in range(near_count):
                        source = ((g * high_count + h) * low_count + w) * near_count + n
                        g2 = step_to(g, grp, grp_count)
                        h2 = step_to(h, high, high_count)
                        w2 = step_to(w, low, low_count)
                        n2 = step_to(n, near, near_count)
                        target = ((g2 * high_count + h2) * low_count + w2) * near_count + n2
                        perm.append((source, target))
        return lax.ppermute(value, AXES, perm)

    def on_device(images, texts, logit_scale, logit_bias):
        params = jnp.concatenate(
            [logit_scale * -LOG2_E, logit_bias * -LOG2_E, logit_scale]
        ).reshape(1, 3)
        early = {(0, 0): images}
        for h in range(1, high_count):
            early[h, 0] = move(images, high=h)
        for w in range(1, low_count):
            early[0, w] = move(images, low=w)
        late = {}
        for h in range(1, high_count):
            block, params = lax.optimization_barrier((early[h, 0], params))
            for w in range(1, low_count):
                late[h, w] = move(block, low=w)
        near_rows = [units([texts], "own_units")] + [move(texts, near=n) for n in range(1, near_count)]
        own_stack = stack_units(near_rows)
        stacks = [own_stack] + [move(own_stack, grp=g) for g in range(1, grp_count)]
        early_parts, late_parts, text_parts = pair_terms(
            params, list(early.values()), list(late.values()), stacks
        )
        far_parts = dict(zip([*early, *late], [*early_parts, *late_parts]))

        def give_back(h, w):
            return move(far_parts[h, w], high=-h, low=-w)

        came = [move(part, grp=-g) for g, part in enumerate(text_parts) if g]
        far_sum = add_far(
            [far_parts[0, 0]] + [give_back(h, w) for h, w in early if h]
        )
        far_sum, own_text = lax.optimization_barrier((far_sum, text_parts[0]))
        far_came = [give_back(h, w) for h, w in late] + [give_back(h, w) for h, w in early if w]
        near_parts = add_stacks([own_text, *came], near_count)
        near_parts = [near_parts[0]] + [
            move(part, near=-n) for n, part in enumerate(near_parts) if n
        ]
        return finish(
            images,
            texts,
            [(0, part) for part in [far_sum] + far_came] + [(1, part) for part in near_parts],
        )

    in_specs = (P(AXES, None), P(AXES, None), P(), P())
    out_specs = (P(AXES, None), P(AXES, None))
    return jax.shard_map(
        on_device, mesh=mesh, in_specs=in_specs, out_specs=out_specs, check_vma=False
    )
```

```python
import functools
import math

import jax
import jax.numpy as jnp
from jax import lax
from jax.experimental import pallas as pl
from jax.experimental.pallas import tpu as pltpu
from jax.sharding import PartitionSpec as P

AXES = ("grp", "dev")
VMEM_LIMIT = 32 * 1024 * 1024
SPAN = 256
PIECE = 32
LATE = 16500
LOG2_E = math.log2(math.e)
VMEM = pl.BlockSpec(memory_space=pltpu.VMEM)


def unit_rows(raw):
    wide = raw.astype(jnp.float32)
    factor = lax.rsqrt(jnp.sum(wide * wide, axis=-1, keepdims=True) + 1e-06)
    return wide * factor, factor


def call(kernel, out_shape, operands, scratch=(), flops=0, transcendentals=0, name=None):
    touched = sum(x.size * x.dtype.itemsize for x in list(operands) + list(out_shape))
    outs = pl.pallas_call(
        kernel,
        out_shape=out_shape,
        in_specs=[VMEM] * len(operands),
        out_specs=[VMEM] * len(out_shape),
        scratch_shapes=scratch,
        compiler_params=pltpu.CompilerParams(vmem_limit_bytes=VMEM_LIMIT),
        cost_estimate=pl.CostEstimate(
            flops=flops, bytes_accessed=touched, transcendentals=transcendentals
        ),
        name=name,
    )(*operands)
    return tuple(outs)


def units_kernel(*refs):
    rows = refs[0].shape[0]
    for at, ref in enumerate(refs[:-1]):
        refs[-1][at * rows:(at + 1) * rows, :] = unit_rows(ref[...])[0].astype(refs[-1].dtype)


def units(blocks, name, weight=1):
    rows, width = blocks[0].shape
    out = jax.ShapeDtypeStruct((len(blocks) * rows, width), jnp.bfloat16)
    return call(units_kernel, [out], blocks, flops=4 * weight * out.size, name=name)[0]


def stack_units_kernel(*refs):
    out = refs[-1]
    rows = refs[0].shape[0]
    out[:rows, :] = refs[0][...]
    for at, ref in enumerate(refs[1:-1], 1):
        out[at * rows:(at + 1) * rows, :] = unit_rows(ref[...])[0].astype(out.dtype)


def stack_units(blocks):
    rows, width = blocks[0].shape
    out = jax.ShapeDtypeStruct((len(blocks) * rows, width), jnp.bfloat16)
    return call(stack_units_kernel, [out], blocks, flops=4 * out.size, name="stack_units")[0]


def pairs(vi, params_ref, text_ref, text_out, own=0, text_add=None):
    slope, shift, temper = (params_ref[0:1, at:at + 1] for at in range(3))
    held = text_ref.shape[0]
    total = None

    def dots_of(first):
        return lax.dot_general(
            vi,
            text_ref[first:min(first + SPAN, held), :],
            (((1,), (1,)), ((), ())),
            preferred_element_type=jnp.float32,
        )

    coming = dots_of(0)
    for first in range(0, held, SPAN):
        last = min(first + SPAN, held)
        dots, coming = coming, dots_of(last) if last < held else None
        vt = text_ref[first:last, :]
        e = jnp.exp2(slope * dots + shift)
        chance = pl.reciprocal(1.0 + e, approx=True)
        if own and first == 0:
            row = lax.broadcasted_iota(jnp.int32, chance.shape, 0)
            column = lax.broadcasted_iota(jnp.int32, chance.shape, 1)
            same = (row == column) & (row < own)
            chance = jnp.where(same, -e * chance, chance)
        coefficient = (temper * chance).astype(jnp.bfloat16)
        text_part = lax.dot_general(
            coefficient, vi, (((0,), (0,)), ((), ())), preferred_element_type=jnp.float32
        )
        if text_add is not None:
            text_part = text_add[first:last, :] + text_part
        text_out[first:last, :] = text_part.astype(text_out.dtype)
        part = jnp.dot(coefficient, vt, preferred_element_type=jnp.float32)
        total = part if total is None else total + part
    return total


def early_pairs_kernel(params_ref, text_ref, *refs):
    image_refs, (text_out, units_out, total_out) = refs[:-3], refs[-3:]
    rows = image_refs[0].shape[0]
    for a, ref in enumerate(image_refs):
        units_out[a * rows:(a + 1) * rows, :] = unit_rows(ref[...])[0].astype(jnp.bfloat16)
    total_out[...] = pairs(units_out[...], params_ref, text_ref, text_out, own=rows)


def rest_pairs_kernel(
    count, params_ref, early_ref, total_ref, own_text_ref, own_add_ref, late_ref, *refs
):
    text_refs, own_out = refs[:count], refs[count]
    other_out, image_out = refs[count + 1:2 * count + 1], refs[2 * count + 1:]
    rows = image_out[0].shape[0]
    early, late = early_ref[...], late_ref[...]
    total = jnp.concatenate(
        [
            total_ref[...],
            pairs(late, params_ref, own_text_ref, own_out, text_add=own_add_ref),
        ],
        axis=0,
    )
    vi = jnp.concatenate([early, late], axis=0)
    for text_ref, out in zip(text_refs, other_out):
        total = total + pairs(vi, params_ref, text_ref, out)
    for a, ref in enumerate(image_out):
        ref[...] = total[a * rows:(a + 1) * rows, :].astype(ref.dtype)


def pair_terms(params, early, late, texts):
    rows, width = early[0].shape
    early_rows, late_rows = rows * len(early), rows * len(late)
    own, others = texts[0], texts[1:]
    other_rows = sum(t.shape[0] for t in others)

    def cost(pair_count):
        return dict(flops=6 * pair_count * width, transcendentals=2 * pair_count)

    own_add, early_units, total = call(
        early_pairs_kernel,
        [
            jax.ShapeDtypeStruct(own.shape, jnp.float32),
            jax.ShapeDtypeStruct((early_rows, width), jnp.bfloat16),
            jax.ShapeDtypeStruct((early_rows, width), jnp.float32),
        ],
        [params, own, *early],
        name="early_pairs",
        **cost(early_rows * own.shape[0]),
    )
    late_units = units(late, "late_units", LATE)
    outs = call(
        functools.partial(rest_pairs_kernel, len(others)),
        [jax.ShapeDtypeStruct(own.shape, jnp.float32)]
        + [jax.ShapeDtypeStruct(t.shape, jnp.bfloat16) for t in others]
        + [jax.ShapeDtypeStruct((rows, width), jnp.float32)]
        + [jax.ShapeDtypeStruct((rows, width), jnp.bfloat16)] * (len(early) + len(late) - 1),
        [params, early_units, total, own, own_add, late_units, *others],
        name="rest_pairs",
        **cost(late_rows * own.shape[0] + (early_rows + late_rows) * other_rows),
    )
    count = 1 + len(others)
    return outs[count:], outs[:count]


def add_stacks_kernel(part_count, *refs):
    parts, outs = refs[:part_count], refs[part_count:]
    rows = outs[0].shape[0]
    for at, out in enumerate(outs):
        total = parts[0][at * rows:(at + 1) * rows, :].astype(jnp.float32)
        for part in parts[1:]:
            total = total + part[at * rows:(at + 1) * rows, :].astype(jnp.float32)
        out[...] = total.astype(out.dtype)


def add_stacks(parts, count):
    shape = (parts[0].shape[0] // count, parts[0].shape[1])
    types = [jnp.float32] + [jnp.bfloat16] * (count - 1)
    return call(
        functools.partial(add_stacks_kernel, len(parts)),
        [jax.ShapeDtypeStruct(shape, t) for t in types],
        parts,
        flops=len(parts) * parts[0].size,
        name="add_stacks",
    )


def finish_kernel(sides, image_ref, text_ref, *refs):
    parts, outs = refs[:len(sides)], refs[len(sides):len(sides) + 2]
    staged, sems = refs[len(sides) + 2:]
    rows = image_ref.shape[0]
    piece = math.gcd(rows, PIECE)
    copies = []
    for side, raw in enumerate((image_ref, text_ref)):
        for first in range(0, rows, piece):
            here = pl.ds(first, piece)
            unit, factor = unit_rows(raw[here, :])
            total = sum(
                ref[here, :].astype(jnp.float32) for at, ref in zip(sides, parts) if at == side
            )
            along = jnp.sum(unit * total, axis=-1, keepdims=True)
            staged[side, here, :] = factor * (total - unit * along)
            copies.append(
                pltpu.make_async_copy(
                    staged.at[side, here, :], outs[side].at[here, :], sems.at[len(copies)]
                )
            )
            copies[-1].start()
    for copy in copies:
        copy.wait()


def finish(images, texts, parts):
    out = jax.ShapeDtypeStruct(images.shape, jnp.float32)
    return pl.pallas_call(
        functools.partial(finish_kernel, [side for side, _ in parts]),
        out_shape=(out, out),
        in_specs=[VMEM] * (2 + len(parts)),
        out_specs=[pl.BlockSpec(memory_space=pl.ANY)] * 2,
        scratch_shapes=[
            pltpu.VMEM((2,) + images.shape, jnp.float32),
            pltpu.SemaphoreType.DMA((2 * (images.shape[0] // math.gcd(images.shape[0], PIECE)),)),
        ],
        compiler_params=pltpu.CompilerParams(vmem_limit_bytes=VMEM_LIMIT),
        cost_estimate=pl.CostEstimate(
            flops=10 * len(parts) * images.size,
            bytes_accessed=3 * len(parts) * images.size,
            transcendentals=0,
        ),
        name="finish",
    )(images, texts, *[part for _, part in parts])


def plan(grp_count, dev_count):
    options = [n for n in range(1, dev_count + 1) if dev_count % n == 0]
    near = min(options, key=lambda n: (dev_count // n + grp_count * n, -n))
    return dev_count // near, near


def step_to(at, by, count):
    if count & (count - 1) == 0:
        return at ^ abs(by)
    return (at + by) % count


def solution(mesh):
    grp_count, dev_count = mesh.shape["grp"], mesh.shape["dev"]
    far_count, near_count = plan(grp_count, dev_count)
    low_count = 2 if far_count % 2 == 0 else 1
    high_count = far_count // low_count

    def move(value, grp=0, high=0, low=0, near=0):
        perm = []
        for g in range(grp_count):
            for h in range(high_count):
                for w in range(low_count):
                    for n in range(near_count):
                        source = ((g * high_count + h) * low_count + w) * near_count + n
                        g2 = step_to(g, grp, grp_count)
                        h2 = step_to(h, high, high_count)
                        w2 = step_to(w, low, low_count)
                        n2 = step_to(n, near, near_count)
                        target = ((g2 * high_count + h2) * low_count + w2) * near_count + n2
                        perm.append((source, target))
        return lax.ppermute(value, AXES, perm)

    def on_device(images, texts, logit_scale, logit_bias):
        params = jnp.concatenate(
            [logit_scale * -LOG2_E, logit_bias * -LOG2_E, logit_scale]
        ).reshape(1, 3)
        early = {(0, 0): images}
        for h in range(1, high_count):
            early[h, 0] = move(images, high=h)
        for w in range(1, low_count):
            early[0, w] = move(images, low=w)
        late = {}
        for h in range(1, high_count):
            block, params = lax.optimization_barrier((early[h, 0], params))
            for w in range(1, low_count):
                late[h, w] = move(block, low=w)
        near_rows = [units([texts], "own_units")] + [move(texts, near=n) for n in range(1, near_count)]
        own_stack = stack_units(near_rows)
        stacks = [own_stack] + [move(own_stack, grp=g) for g in range(1, grp_count)]
        image_parts, text_parts = pair_terms(
            params, list(early.values()), list(late.values()), stacks
        )
        far_parts = dict(zip([*early, *late], image_parts))
        came = [move(part, grp=-g) for g, part in enumerate(text_parts) if g]
        far_order = sorted((step for step in far_parts if step != (0, 0)), key=lambda step: step[0])
        far_came = [move(far_parts[h, w], high=-h, low=-w) for h, w in far_order]
        near_parts = add_stacks([text_parts[0], *came], near_count)
        near_parts = [near_parts[0]] + [
            move(part, near=-n) for n, part in enumerate(near_parts) if n
        ]
        return finish(
            images,
            texts,
            [(0, part) for part in [far_parts[0, 0]] + far_came]
            + [(1, part) for part in near_parts],
        )

    in_specs = (P(AXES, None), P(AXES, None), P(), P())
    out_specs = (P(AXES, None), P(AXES, None))
    return jax.shard_map(
        on_device, mesh=mesh, in_specs=in_specs, out_specs=out_specs, check_vma=False
    )
```

```python
import functools
import math

import jax
import jax.numpy as jnp
from jax import lax
from jax.experimental import pallas as pl
from jax.experimental.pallas import tpu as pltpu
from jax.sharding import PartitionSpec as P

AXES = ("grp", "dev")
VMEM_LIMIT = 32 * 1024 * 1024
SPAN = 256
PIECE = 32
LATE = 16500
FAR = 17000
LOG2_E = math.log2(math.e)
VMEM = pl.BlockSpec(memory_space=pltpu.VMEM)


def unit_rows(raw):
    wide = raw.astype(jnp.float32)
    factor = lax.rsqrt(jnp.sum(wide * wide, axis=-1, keepdims=True) + 1e-06)
    return wide * factor, factor


def call(kernel, out_shape, operands, scratch=(), flops=0, transcendentals=0, name=None):
    touched = sum(x.size * x.dtype.itemsize for x in list(operands) + list(out_shape))
    outs = pl.pallas_call(
        kernel,
        out_shape=out_shape,
        in_specs=[VMEM] * len(operands),
        out_specs=[VMEM] * len(out_shape),
        scratch_shapes=scratch,
        compiler_params=pltpu.CompilerParams(vmem_limit_bytes=VMEM_LIMIT),
        cost_estimate=pl.CostEstimate(
            flops=flops, bytes_accessed=touched, transcendentals=transcendentals
        ),
        name=name,
    )(*operands)
    return tuple(outs)


def units_kernel(*refs):
    rows = refs[0].shape[0]
    for at, ref in enumerate(refs[:-1]):
        refs[-1][at * rows:(at + 1) * rows, :] = unit_rows(ref[...])[0].astype(refs[-1].dtype)


def units(blocks, name, weight=1):
    rows, width = blocks[0].shape
    out = jax.ShapeDtypeStruct((len(blocks) * rows, width), jnp.bfloat16)
    return call(units_kernel, [out], blocks, flops=4 * weight * out.size, name=name)[0]


def stack_units_kernel(*refs):
    out = refs[-1]
    rows = refs[0].shape[0]
    out[:rows, :] = refs[0][...]
    for at, ref in enumerate(refs[1:-1], 1):
        out[at * rows:(at + 1) * rows, :] = unit_rows(ref[...])[0].astype(out.dtype)


def stack_units(blocks):
    rows, width = blocks[0].shape
    out = jax.ShapeDtypeStruct((len(blocks) * rows, width), jnp.bfloat16)
    return call(stack_units_kernel, [out], blocks, flops=4 * out.size, name="stack_units")[0]


def pairs(vi, params_ref, text_ref, text_out, own=0, text_add=None):
    slope, shift, temper = (params_ref[0:1, at:at + 1] for at in range(3))
    held = text_ref.shape[0]
    total = None

    def dots_of(first):
        return lax.dot_general(
            vi,
            text_ref[first:min(first + SPAN, held), :],
            (((1,), (1,)), ((), ())),
            preferred_element_type=jnp.float32,
        )

    coming = dots_of(0)
    for first in range(0, held, SPAN):
        last = min(first + SPAN, held)
        dots, coming = coming, dots_of(last) if last < held else None
        vt = text_ref[first:last, :]
        e = jnp.exp2(slope * dots + shift)
        chance = pl.reciprocal(1.0 + e, approx=True)
        if own and first == 0:
            row = lax.broadcasted_iota(jnp.int32, chance.shape, 0)
            column = lax.broadcasted_iota(jnp.int32, chance.shape, 1)
            same = (row == column) & (row < own)
            chance = jnp.where(same, -e * chance, chance)
        coefficient = (temper * chance).astype(jnp.bfloat16)
        text_part = lax.dot_general(
            coefficient, vi, (((0,), (0,)), ((), ())), preferred_element_type=jnp.float32
        )
        if text_add is not None:
            text_part = text_add[first:last, :] + text_part
        text_out[first:last, :] = text_part.astype(text_out.dtype)
        part = jnp.dot(coefficient, vt, preferred_element_type=jnp.float32)
        total = part if total is None else total + part
    return total


def early_pairs_kernel(params_ref, text_ref, *refs):
    image_refs, (text_out, units_out, total_out) = refs[:-3], refs[-3:]
    rows = image_refs[0].shape[0]
    for a, ref in enumerate(image_refs):
        units_out[a * rows:(a + 1) * rows, :] = unit_rows(ref[...])[0].astype(jnp.bfloat16)
    total_out[...] = pairs(units_out[...], params_ref, text_ref, text_out, own=rows)


def rest_pairs_kernel(
    count, params_ref, early_ref, total_ref, own_text_ref, own_add_ref, late_ref, *refs
):
    text_refs, own_out = refs[:count], refs[count]
    other_out, image_out = refs[count + 1:2 * count + 1], refs[2 * count + 1:]
    rows = image_out[0].shape[0]
    early, late = early_ref[...], late_ref[...]
    total = jnp.concatenate(
        [
            total_ref[...],
            pairs(late, params_ref, own_text_ref, own_out, text_add=own_add_ref),
        ],
        axis=0,
    )
    vi = jnp.concatenate([early, late], axis=0)
    for text_ref, out in zip(text_refs, other_out):
        total = total + pairs(vi, params_ref, text_ref, out)
    for a, ref in enumerate(image_out):
        ref[...] = total[a * rows:(a + 1) * rows, :].astype(ref.dtype)


def pair_terms(params, early, late, texts):
    rows, width = early[0].shape
    early_rows, late_rows = rows * len(early), rows * len(late)
    own, others = texts[0], texts[1:]
    other_rows = sum(t.shape[0] for t in others)

    def cost(pair_count):
        return dict(flops=6 * pair_count * width, transcendentals=2 * pair_count)

    own_add, early_units, total = call(
        early_pairs_kernel,
        [
            jax.ShapeDtypeStruct(own.shape, jnp.float32),
            jax.ShapeDtypeStruct((early_rows, width), jnp.bfloat16),
            jax.ShapeDtypeStruct((early_rows, width), jnp.float32),
        ],
        [params, own, *early],
        name="early_pairs",
        **cost(early_rows * own.shape[0]),
    )
    late_units = units(late, "late_units", LATE)
    outs = call(
        functools.partial(rest_pairs_kernel, len(others)),
        [jax.ShapeDtypeStruct(own.shape, jnp.float32)]
        + [jax.ShapeDtypeStruct(t.shape, jnp.bfloat16) for t in others]
        + [jax.ShapeDtypeStruct((rows, width), jnp.float32)]
        + [jax.ShapeDtypeStruct((rows, width), jnp.bfloat16)] * (len(early) + len(late) - 1),
        [params, early_units, total, own, own_add, late_units, *others],
        name="rest_pairs",
        **cost(late_rows * own.shape[0] + (early_rows + late_rows) * other_rows),
    )
    count = 1 + len(others)
    return outs[count:], outs[:count]


def add_stacks_kernel(part_count, *refs):
    parts, outs = refs[:part_count], refs[part_count:]
    rows = outs[0].shape[0]
    for at, out in enumerate(outs):
        total = parts[0][at * rows:(at + 1) * rows, :].astype(jnp.float32)
        for part in parts[1:]:
            total = total + part[at * rows:(at + 1) * rows, :].astype(jnp.float32)
        out[...] = total.astype(out.dtype)


def add_stacks(parts, count):
    shape = (parts[0].shape[0] // count, parts[0].shape[1])
    types = [jnp.float32] + [jnp.bfloat16] * (count - 1)
    return call(
        functools.partial(add_stacks_kernel, len(parts)),
        [jax.ShapeDtypeStruct(shape, t) for t in types],
        parts,
        flops=len(parts) * parts[0].size,
        name="add_stacks",
    )


def add_far_kernel(*refs):
    refs[-1][...] = sum(ref[...].astype(jnp.float32) for ref in refs[:-1])


def add_far(parts):
    out = jax.ShapeDtypeStruct(parts[0].shape, jnp.float32)
    return call(
        add_far_kernel, [out], parts, flops=FAR * len(parts) * out.size, name="add_far"
    )[0]


def finish_kernel(sides, image_ref, text_ref, *refs):
    parts, outs = refs[:len(sides)], refs[len(sides):len(sides) + 2]
    staged, sems = refs[len(sides) + 2:]
    rows = image_ref.shape[0]
    piece = math.gcd(rows, PIECE)
    copies = []
    for side, raw in enumerate((image_ref, text_ref)):
        for first in range(0, rows, piece):
            here = pl.ds(first, piece)
            unit, factor = unit_rows(raw[here, :])
            total = sum(
                ref[here, :].astype(jnp.float32) for at, ref in zip(sides, parts) if at == side
            )
            along = jnp.sum(unit * total, axis=-1, keepdims=True)
            staged[side, here, :] = factor * (total - unit * along)
            copies.append(
                pltpu.make_async_copy(
                    staged.at[side, here, :], outs[side].at[here, :], sems.at[len(copies)]
                )
            )
            copies[-1].start()
    for copy in copies:
        copy.wait()


def finish(images, texts, parts):
    out = jax.ShapeDtypeStruct(images.shape, jnp.float32)
    return pl.pallas_call(
        functools.partial(finish_kernel, [side for side, _ in parts]),
        out_shape=(out, out),
        in_specs=[VMEM] * (2 + len(parts)),
        out_specs=[pl.BlockSpec(memory_space=pl.ANY)] * 2,
        scratch_shapes=[
            pltpu.VMEM((2,) + images.shape, jnp.float32),
            pltpu.SemaphoreType.DMA((2 * (images.shape[0] // math.gcd(images.shape[0], PIECE)),)),
        ],
        compiler_params=pltpu.CompilerParams(vmem_limit_bytes=VMEM_LIMIT),
        cost_estimate=pl.CostEstimate(
            flops=10 * len(parts) * images.size,
            bytes_accessed=3 * len(parts) * images.size,
            transcendentals=0,
        ),
        name="finish",
    )(images, texts, *[part for _, part in parts])


def plan(grp_count, dev_count):
    options = [n for n in range(1, dev_count + 1) if dev_count % n == 0]
    near = min(options, key=lambda n: (dev_count // n + grp_count * n, -n))
    return dev_count // near, near


def step_to(at, by, count):
    if count & (count - 1) == 0:
        return at ^ abs(by)
    return (at + by) % count


def solution(mesh):
    grp_count, dev_count = mesh.shape["grp"], mesh.shape["dev"]
    far_count, near_count = plan(grp_count, dev_count)
    low_count = 2 if far_count % 2 == 0 else 1
    high_count = far_count // low_count
    near_low = 2 if near_count % 2 == 0 else 1

    def move(value, grp=0, high=0, low=0, near=0):
        perm = []
        for g in range(grp_count):
            for h in range(high_count):
                for w in range(low_count):
                    for n in range(near_count):
                        source = ((g * high_count + h) * low_count + w) * near_count + n
                        g2 = step_to(g, grp, grp_count)
                        h2 = step_to(h, high, high_count)
                        w2 = step_to(w, low, low_count)
                        n2 = step_to(n, near, near_count)
                        target = ((g2 * high_count + h2) * low_count + w2) * near_count + n2
                        perm.append((source, target))
        return lax.ppermute(value, AXES, perm)

    def on_device(images, texts, logit_scale, logit_bias):
        params = jnp.concatenate(
            [logit_scale * -LOG2_E, logit_bias * -LOG2_E, logit_scale]
        ).reshape(1, 3)
        early = {(0, 0): images}
        for h in range(1, high_count):
            early[h, 0] = move(images, high=h)
        for w in range(1, low_count):
            early[0, w] = move(images, low=w)
        late = {}
        for h in range(1, high_count):
            block, params = lax.optimization_barrier((early[h, 0], params))
            for w in range(1, low_count):
                late[h, w] = move(block, low=w)
        near_rows = [units([texts], "own_units")] + [move(texts, near=n) for n in range(1, near_count)]
        own_stack = stack_units(near_rows)
        stacks = [own_stack] + [move(own_stack, grp=g) for g in range(1, grp_count)]
        image_parts, text_parts = pair_terms(
            params, list(early.values()), list(late.values()), stacks
        )
        far_parts = dict(zip([*early, *late], image_parts))
        def give_back(h, w):
            return move(far_parts[h, w], high=-h, low=-w)

        came = [move(part, grp=-g) for g, part in enumerate(text_parts) if g]
        own, *sent = add_stacks([text_parts[0], *came], near_count // near_low)
        came = [move(part, near=-n * near_low) for n, part in enumerate(sent, 1)]
        own, *sent = add_stacks([own, *came], near_low)
        far_sum = add_far([far_parts[0, 0]] + [give_back(h, w) for h, w in early if h])
        far_sum, sent = lax.optimization_barrier((far_sum, sent))
        came = [move(part, near=-n) for n, part in enumerate(sent, 1)]
        far_came = [give_back(h, w) for h, w in late] + [give_back(h, w) for h, w in early if w]
        return finish(
            images,
            texts,
            [(0, part) for part in [far_sum] + far_came] + [(1, part) for part in [own] + came],
        )

    in_specs = (P(AXES, None), P(AXES, None), P(), P())
    out_specs = (P(AXES, None), P(AXES, None))
    return jax.shard_map(
        on_device, mesh=mesh, in_specs=in_specs, out_specs=out_specs, check_vma=False
    )
```

```python
import functools
import math

import jax
import jax.numpy as jnp
from jax import lax
from jax.experimental import pallas as pl
from jax.experimental.pallas import tpu as pltpu
from jax.sharding import PartitionSpec as P

AXES = ("grp", "dev")
VMEM_LIMIT = 32 * 1024 * 1024
SPAN = 256
PIECE = 32
LATE = 16500
LOG2_E = math.log2(math.e)
VMEM = pl.BlockSpec(memory_space=pltpu.VMEM)


def unit_rows(raw):
    wide = raw.astype(jnp.float32)
    factor = lax.rsqrt(jnp.sum(wide * wide, axis=-1, keepdims=True) + 1e-06)
    return wide * factor, factor


def call(kernel, out_shape, operands, scratch=(), flops=0, transcendentals=0, name=None):
    touched = sum(x.size * x.dtype.itemsize for x in list(operands) + list(out_shape))
    outs = pl.pallas_call(
        kernel,
        out_shape=out_shape,
        in_specs=[VMEM] * len(operands),
        out_specs=[VMEM] * len(out_shape),
        scratch_shapes=scratch,
        compiler_params=pltpu.CompilerParams(vmem_limit_bytes=VMEM_LIMIT),
        cost_estimate=pl.CostEstimate(
            flops=flops, bytes_accessed=touched, transcendentals=transcendentals
        ),
        name=name,
    )(*operands)
    return tuple(outs)


def units_kernel(*refs):
    rows = refs[0].shape[0]
    for at, ref in enumerate(refs[:-1]):
        refs[-1][at * rows:(at + 1) * rows, :] = unit_rows(ref[...])[0].astype(refs[-1].dtype)


def units(blocks, name, weight=1):
    rows, width = blocks[0].shape
    out = jax.ShapeDtypeStruct((len(blocks) * rows, width), jnp.bfloat16)
    return call(units_kernel, [out], blocks, flops=4 * weight * out.size, name=name)[0]


def stack_units_kernel(*refs):
    out = refs[-1]
    rows = refs[0].shape[0]
    out[:rows, :] = refs[0][...]
    for at, ref in enumerate(refs[1:-1], 1):
        out[at * rows:(at + 1) * rows, :] = unit_rows(ref[...])[0].astype(out.dtype)


def stack_units(blocks):
    rows, width = blocks[0].shape
    out = jax.ShapeDtypeStruct((len(blocks) * rows, width), jnp.bfloat16)
    return call(stack_units_kernel, [out], blocks, flops=4 * out.size, name="stack_units")[0]


def pairs(vi, params_ref, text_ref, text_out, own=0, text_add=None):
    slope, shift, temper = (params_ref[0:1, at:at + 1] for at in range(3))
    held = text_ref.shape[0]
    total = None

    def dots_of(first):
        return lax.dot_general(
            vi,
            text_ref[first:min(first + SPAN, held), :],
            (((1,), (1,)), ((), ())),
            preferred_element_type=jnp.float32,
        )

    coming = dots_of(0)
    for first in range(0, held, SPAN):
        last = min(first + SPAN, held)
        dots, coming = coming, dots_of(last) if last < held else None
        vt = text_ref[first:last, :]
        e = jnp.exp2(slope * dots + shift)
        chance = pl.reciprocal(1.0 + e, approx=True)
        if own and first == 0:
            row = lax.broadcasted_iota(jnp.int32, chance.shape, 0)
            column = lax.broadcasted_iota(jnp.int32, chance.shape, 1)
            same = (row == column) & (row < own)
            chance = jnp.where(same, -e * chance, chance)
        coefficient = (temper * chance).astype(jnp.bfloat16)
        text_part = lax.dot_general(
            coefficient, vi, (((0,), (0,)), ((), ())), preferred_element_type=jnp.float32
        )
        if text_add is not None:
            text_part = text_add[first:last, :] + text_part
        text_out[first:last, :] = text_part.astype(text_out.dtype)
        part = jnp.dot(coefficient, vt, preferred_element_type=jnp.float32)
        total = part if total is None else total + part
    return total


def early_pairs_kernel(params_ref, text_ref, *refs):
    image_refs, (text_out, units_out, total_out) = refs[:-3], refs[-3:]
    rows = image_refs[0].shape[0]
    for a, ref in enumerate(image_refs):
        units_out[a * rows:(a + 1) * rows, :] = unit_rows(ref[...])[0].astype(jnp.bfloat16)
    total_out[...] = pairs(units_out[...], params_ref, text_ref, text_out, own=rows)


def rest_pairs_kernel(
    count, params_ref, early_ref, total_ref, own_text_ref, own_add_ref, late_ref, *refs
):
    text_refs, own_out = refs[:count], refs[count]
    other_out, image_out = refs[count + 1:2 * count + 1], refs[2 * count + 1:]
    rows = image_out[0].shape[0]
    early, late = early_ref[...], late_ref[...]
    total = jnp.concatenate(
        [
            total_ref[...],
            pairs(late, params_ref, own_text_ref, own_out, text_add=own_add_ref),
        ],
        axis=0,
    )
    vi = jnp.concatenate([early, late], axis=0)
    for text_ref, out in zip(text_refs, other_out):
        total = total + pairs(vi, params_ref, text_ref, out)
    for a, ref in enumerate(image_out):
        ref[...] = total[a * rows:(a + 1) * rows, :].astype(ref.dtype)


def pair_terms(params, early, late, texts):
    rows, width = early[0].shape
    early_rows, late_rows = rows * len(early), rows * len(late)
    own, others = texts[0], texts[1:]
    other_rows = sum(t.shape[0] for t in others)

    def cost(pair_count):
        return dict(flops=6 * pair_count * width, transcendentals=2 * pair_count)

    own_add, early_units, total = call(
        early_pairs_kernel,
        [
            jax.ShapeDtypeStruct(own.shape, jnp.float32),
            jax.ShapeDtypeStruct((early_rows, width), jnp.bfloat16),
            jax.ShapeDtypeStruct((early_rows, width), jnp.float32),
        ],
        [params, own, *early],
        name="early_pairs",
        **cost(early_rows * own.shape[0]),
    )
    late_units = units(late, "late_units", LATE)
    outs = call(
        functools.partial(rest_pairs_kernel, len(others)),
        [jax.ShapeDtypeStruct(own.shape, jnp.float32)]
        + [jax.ShapeDtypeStruct(t.shape, jnp.bfloat16) for t in others]
        + [jax.ShapeDtypeStruct((rows, width), jnp.float32)]
        + [jax.ShapeDtypeStruct((rows, width), jnp.bfloat16)] * (len(early) + len(late) - 1),
        [params, early_units, total, own, own_add, late_units, *others],
        name="rest_pairs",
        **cost(late_rows * own.shape[0] + (early_rows + late_rows) * other_rows),
    )
    count = 1 + len(others)
    return outs[count:], outs[:count]


def add_stacks_kernel(part_count, *refs):
    parts, outs = refs[:part_count], refs[part_count:]
    rows = outs[0].shape[0]
    for at, out in enumerate(outs):
        total = parts[0][at * rows:(at + 1) * rows, :].astype(jnp.float32)
        for part in parts[1:]:
            total = total + part[at * rows:(at + 1) * rows, :].astype(jnp.float32)
        out[...] = total.astype(out.dtype)


def add_stacks(parts, count):
    shape = (parts[0].shape[0] // count, parts[0].shape[1])
    types = [jnp.float32] + [jnp.bfloat16] * (count - 1)
    return call(
        functools.partial(add_stacks_kernel, len(parts)),
        [jax.ShapeDtypeStruct(shape, t) for t in types],
        parts,
        flops=len(parts) * parts[0].size,
        name="add_stacks",
    )


def finish_kernel(sides, image_ref, text_ref, *refs):
    parts, outs = refs[:len(sides)], refs[len(sides):len(sides) + 2]
    staged, sems = refs[len(sides) + 2:]
    rows = image_ref.shape[0]
    piece = math.gcd(rows, PIECE)
    copies = []
    for side, raw in enumerate((image_ref, text_ref)):
        for first in range(0, rows, piece):
            here = pl.ds(first, piece)
            unit, factor = unit_rows(raw[here, :])
            total = sum(
                ref[here, :].astype(jnp.float32) for at, ref in zip(sides, parts) if at == side
            )
            along = jnp.sum(unit * total, axis=-1, keepdims=True)
            staged[side, here, :] = factor * (total - unit * along)
            copies.append(
                pltpu.make_async_copy(
                    staged.at[side, here, :], outs[side].at[here, :], sems.at[len(copies)]
                )
            )
            copies[-1].start()
    for copy in copies:
        copy.wait()


def finish(images, texts, parts):
    out = jax.ShapeDtypeStruct(images.shape, jnp.float32)
    return pl.pallas_call(
        functools.partial(finish_kernel, [side for side, _ in parts]),
        out_shape=(out, out),
        in_specs=[VMEM] * (2 + len(parts)),
        out_specs=[pl.BlockSpec(memory_space=pl.ANY)] * 2,
        scratch_shapes=[
            pltpu.VMEM((2,) + images.shape, jnp.float32),
            pltpu.SemaphoreType.DMA((2 * (images.shape[0] // math.gcd(images.shape[0], PIECE)),)),
        ],
        compiler_params=pltpu.CompilerParams(vmem_limit_bytes=VMEM_LIMIT),
        cost_estimate=pl.CostEstimate(
            flops=10 * len(parts) * images.size,
            bytes_accessed=3 * len(parts) * images.size,
            transcendentals=0,
        ),
        name="finish",
    )(images, texts, *[part for _, part in parts])


def plan(grp_count, dev_count):
    options = [n for n in range(1, dev_count + 1) if dev_count % n == 0]
    near = min(options, key=lambda n: (dev_count // n + grp_count * n, -n))
    return dev_count // near, near


def step_to(at, by, count):
    if count & (count - 1) == 0:
        return at ^ abs(by)
    return (at + by) % count


def solution(mesh):
    grp_count, dev_count = mesh.shape["grp"], mesh.shape["dev"]
    far_count, near_count = plan(grp_count, dev_count)
    low_count = 2 if far_count % 2 == 0 else 1
    high_count = far_count // low_count
    near_low = 2 if near_count % 2 == 0 else 1

    def move(value, grp=0, high=0, low=0, near=0):
        perm = []
        for g in range(grp_count):
            for h in range(high_count):
                for w in range(low_count):
                    for n in range(near_count):
                        source = ((g * high_count + h) * low_count + w) * near_count + n
                        g2 = step_to(g, grp, grp_count)
                        h2 = step_to(h, high, high_count)
                        w2 = step_to(w, low, low_count)
                        n2 = step_to(n, near, near_count)
                        target = ((g2 * high_count + h2) * low_count + w2) * near_count + n2
                        perm.append((source, target))
        return lax.ppermute(value, AXES, perm)

    def on_device(images, texts, logit_scale, logit_bias):
        params = jnp.concatenate(
            [logit_scale * -LOG2_E, logit_bias * -LOG2_E, logit_scale]
        ).reshape(1, 3)
        early = {(0, 0): images}
        for h in range(1, high_count):
            early[h, 0] = move(images, high=h)
        for w in range(1, low_count):
            early[0, w] = move(images, low=w)
        late = {}
        for h in range(1, high_count):
            block, params = lax.optimization_barrier((early[h, 0], params))
            for w in range(1, low_count):
                late[h, w] = move(block, low=w)
        near_rows = [units([texts], "own_units")] + [move(texts, near=n) for n in range(1, near_count)]
        own_stack = stack_units(near_rows)
        stacks = [own_stack] + [move(own_stack, grp=g) for g in range(1, grp_count)]
        image_parts, text_parts = pair_terms(
            params, list(early.values()), list(late.values()), stacks
        )
        far_parts = dict(zip([*early, *late], image_parts))
        def give_back(h, w):
            return move(far_parts[h, w], high=-h, low=-w)

        came = [move(part, grp=-g) for g, part in enumerate(text_parts) if g]
        own, *sent = add_stacks([text_parts[0], *came], near_count // near_low)
        came = [move(part, near=-n * near_low) for n, part in enumerate(sent, 1)]
        own, *sent = add_stacks([own, *came], near_low)
        came = [move(part, near=-n) for n, part in enumerate(sent, 1)]
        far_order = sorted((step for step in far_parts if step != (0, 0)), key=lambda step: -step[0])
        far_came = [give_back(h, w) for h, w in far_order]
        return finish(
            images,
            texts,
            [(0, part) for part in [far_parts[0, 0]] + far_came] + [(1, part) for part in [own] + came],
        )

    in_specs = (P(AXES, None), P(AXES, None), P(), P())
    out_specs = (P(AXES, None), P(AXES, None))
    return jax.shard_map(
        on_device, mesh=mesh, in_specs=in_specs, out_specs=out_specs, check_vma=False
    )
```

```python
import functools
import math

import jax
import jax.numpy as jnp
from jax import lax
from jax.experimental import pallas as pl
from jax.experimental.pallas import tpu as pltpu
from jax.sharding import PartitionSpec as P

AXES = ("grp", "dev")
VMEM_LIMIT = 32 * 1024 * 1024
SPAN = 256
OWN = 8
LATE = 16500
LOG2_E = math.log2(math.e)
VMEM = pl.BlockSpec(memory_space=pltpu.VMEM)


def unit_rows(raw):
    wide = raw.astype(jnp.float32)
    factor = lax.rsqrt(jnp.sum(wide * wide, axis=-1, keepdims=True) + 1e-06)
    return wide * factor, factor


def call(kernel, out_shape, operands, scratch=(), flops=0, transcendentals=0, name=None):
    touched = sum(x.size * x.dtype.itemsize for x in list(operands) + list(out_shape))
    outs = pl.pallas_call(
        kernel,
        out_shape=out_shape,
        in_specs=[VMEM] * len(operands),
        out_specs=[VMEM] * len(out_shape),
        scratch_shapes=scratch,
        compiler_params=pltpu.CompilerParams(vmem_limit_bytes=VMEM_LIMIT),
        cost_estimate=pl.CostEstimate(
            flops=flops, bytes_accessed=touched, transcendentals=transcendentals
        ),
        name=name,
    )(*operands)
    return tuple(outs)


def units_kernel(*refs):
    rows = refs[0].shape[0]
    for at, ref in enumerate(refs[:-1]):
        refs[-1][at * rows:(at + 1) * rows, :] = unit_rows(ref[...])[0].astype(refs[-1].dtype)


def units(blocks, name, weight=1):
    rows, width = blocks[0].shape
    out = jax.ShapeDtypeStruct((len(blocks) * rows, width), jnp.bfloat16)
    return call(units_kernel, [out], blocks, flops=4 * weight * out.size, name=name)[0]


def stack_units_kernel(*refs):
    out = refs[-1]
    rows = refs[0].shape[0]
    out[:rows, :] = refs[0][...]
    for at, ref in enumerate(refs[1:-1], 1):
        out[at * rows:(at + 1) * rows, :] = unit_rows(ref[...])[0].astype(out.dtype)


def stack_units(blocks):
    rows, width = blocks[0].shape
    out = jax.ShapeDtypeStruct((len(blocks) * rows, width), jnp.bfloat16)
    return call(stack_units_kernel, [out], blocks, flops=4 * out.size, name="stack_units")[0]


def pairs(vi, params_ref, text_ref, text_out, own=0, text_add=None):
    slope, shift, temper = (params_ref[0:1, at:at + 1] for at in range(3))
    held = text_ref.shape[0]
    total = None

    def dots_of(first):
        return lax.dot_general(
            vi,
            text_ref[first:min(first + SPAN, held), :],
            (((1,), (1,)), ((), ())),
            preferred_element_type=jnp.float32,
        )

    coming = dots_of(0)
    for first in range(0, held, SPAN):
        last = min(first + SPAN, held)
        dots, coming = coming, dots_of(last) if last < held else None
        vt = text_ref[first:last, :]
        e = jnp.exp2(slope * dots + shift)
        chance = pl.reciprocal(1.0 + e, approx=True)
        if own and first == 0:
            row = lax.broadcasted_iota(jnp.int32, chance.shape, 0)
            column = lax.broadcasted_iota(jnp.int32, chance.shape, 1)
            same = (row == column) & (row < own)
            chance = jnp.where(same, -e * chance, chance)
        coefficient = (temper * chance).astype(jnp.bfloat16)
        text_part = lax.dot_general(
            coefficient, vi, (((0,), (0,)), ((), ())), preferred_element_type=jnp.float32
        )
        if text_add is not None:
            text_part = text_add[first:last, :] + text_part
        text_out[first:last, :] = text_part.astype(text_out.dtype)
        part = jnp.dot(coefficient, vt, preferred_element_type=jnp.float32)
        total = part if total is None else total + part
    return total


def early_pairs_kernel(params_ref, text_ref, *refs):
    image_refs, (text_out, units_out, total_out) = refs[:-3], refs[-3:]
    rows = image_refs[0].shape[0]
    for a, ref in enumerate(image_refs):
        units_out[a * rows:(a + 1) * rows, :] = unit_rows(ref[...])[0].astype(jnp.bfloat16)
    total_out[...] = pairs(units_out[...], params_ref, text_ref, text_out, own=rows)


def rest_pairs_kernel(
    count, params_ref, early_ref, total_ref, own_text_ref, own_add_ref, late_ref, *refs
):
    text_refs, own_out = refs[:count], refs[count]
    other_out, image_out = refs[count + 1:2 * count + 1], refs[2 * count + 1:]
    rows = image_out[0].shape[0]
    early, late = early_ref[...], late_ref[...]
    total = jnp.concatenate(
        [
            total_ref[...],
            pairs(late, params_ref, own_text_ref, own_out, text_add=own_add_ref),
        ],
        axis=0,
    )
    vi = jnp.concatenate([early, late], axis=0)
    for text_ref, out in zip(text_refs, other_out):
        total = total + pairs(vi, params_ref, text_ref, out)
    for a, ref in enumerate(image_out):
        ref[...] = total[a * rows:(a + 1) * rows, :].astype(ref.dtype)


def pair_terms(params, early, late, texts):
    rows, width = early[0].shape
    early_rows, late_rows = rows * len(early), rows * len(late)
    own, others = texts[0], texts[1:]
    other_rows = sum(t.shape[0] for t in others)

    def cost(pair_count):
        return dict(flops=6 * pair_count * width, transcendentals=2 * pair_count)

    own_add, early_units, total = call(
        early_pairs_kernel,
        [
            jax.ShapeDtypeStruct(own.shape, jnp.float32),
            jax.ShapeDtypeStruct((early_rows, width), jnp.bfloat16),
            jax.ShapeDtypeStruct((early_rows, width), jnp.float32),
        ],
        [params, own, *early],
        name="early_pairs",
        **cost(early_rows * own.shape[0]),
    )
    late_units = units(late, "late_units", LATE)
    outs = call(
        functools.partial(rest_pairs_kernel, len(others)),
        [jax.ShapeDtypeStruct(own.shape, jnp.float32)]
        + [jax.ShapeDtypeStruct(t.shape, jnp.bfloat16) for t in others]
        + [jax.ShapeDtypeStruct((rows, width), jnp.float32)]
        + [jax.ShapeDtypeStruct((rows, width), jnp.bfloat16)] * (len(early) + len(late) - 1),
        [params, early_units, total, own, own_add, late_units, *others],
        name="rest_pairs",
        **cost(late_rows * own.shape[0] + (early_rows + late_rows) * other_rows),
    )
    count = 1 + len(others)
    return outs[count:], outs[:count]


def add_stacks_kernel(part_count, *refs):
    parts, outs = refs[:part_count], refs[part_count:]
    rows = outs[0].shape[0]
    for at, out in enumerate(outs):
        total = parts[0][at * rows:(at + 1) * rows, :].astype(jnp.float32)
        for part in parts[1:]:
            total = total + part[at * rows:(at + 1) * rows, :].astype(jnp.float32)
        out[...] = total.astype(out.dtype)


def add_stacks(parts, count):
    shape = (parts[0].shape[0] // count, parts[0].shape[1])
    types = [jnp.float32] + [jnp.bfloat16] * (count - 1)
    return call(
        functools.partial(add_stacks_kernel, len(parts)),
        [jax.ShapeDtypeStruct(shape, t) for t in types],
        parts,
        flops=len(parts) * parts[0].size,
        name="add_stacks",
    )


def own_rows_kernel(*refs):
    half = len(refs) // 3
    for raw, unit_out, factor_out in zip(refs[:half], refs[half::2], refs[half + 1::2]):
        unit, factor = unit_rows(raw[...])
        unit_out[...] = unit
        factor_out[...] = jnp.broadcast_to(factor, factor_out.shape)


def own_rows(arrays):
    out = []
    for x in arrays:
        out.append(jax.ShapeDtypeStruct(x.shape, jnp.float32))
        out.append(jax.ShapeDtypeStruct((x.shape[0], 128), jnp.float32))
    outs = call(own_rows_kernel, out, arrays, flops=OWN * arrays[0].size, name="own_rows")
    return list(zip(outs[::2], outs[1::2]))


def finish_kernel(sides, *refs):
    own, parts = refs[:4], refs[4:4 + len(sides)]
    outs, (staged, sems) = refs[4 + len(sides):6 + len(sides)], refs[6 + len(sides):]
    copies = []
    for side, (unit_ref, factor_ref, out) in enumerate(zip(own[::2], own[1::2], outs)):
        total = sum(ref[...].astype(jnp.float32) for at, ref in zip(sides, parts) if at == side)
        unit = unit_ref[...]
        along = jnp.sum(unit * total, axis=-1, keepdims=True)
        staged[side] = factor_ref[:, 0:1] * (total - unit * along)
        copies.append(pltpu.make_async_copy(staged.at[side], out, sems.at[side]))
        copies[-1].start()
    for copy in copies:
        copy.wait()


def finish(own, parts):
    shape = own[0][0].shape
    out = jax.ShapeDtypeStruct(shape, jnp.float32)
    count = len(parts)
    return pl.pallas_call(
        functools.partial(finish_kernel, [side for side, _ in parts]),
        out_shape=(out, out),
        in_specs=[VMEM] * (4 + count),
        out_specs=[pl.BlockSpec(memory_space=pl.ANY)] * 2,
        scratch_shapes=[
            pltpu.VMEM((2,) + shape, jnp.float32),
            pltpu.SemaphoreType.DMA((2,)),
        ],
        compiler_params=pltpu.CompilerParams(vmem_limit_bytes=VMEM_LIMIT),
        cost_estimate=pl.CostEstimate(
            flops=10 * count * out.size, bytes_accessed=3 * count * out.size, transcendentals=0
        ),
        name="finish",
    )(*own[0], *own[1], *[part for _, part in parts])


def plan(grp_count, dev_count):
    options = [n for n in range(1, dev_count + 1) if dev_count % n == 0]
    near = min(options, key=lambda n: (dev_count // n + grp_count * n, -n))
    return dev_count // near, near


def step_to(at, by, count):
    if count & (count - 1) == 0:
        return at ^ abs(by)
    return (at + by) % count


def solution(mesh):
    grp_count, dev_count = mesh.shape["grp"], mesh.shape["dev"]
    far_count, near_count = plan(grp_count, dev_count)
    low_count = 2 if far_count % 2 == 0 else 1
    high_count = far_count // low_count

    def move(value, grp=0, high=0, low=0, near=0):
        perm = []
        for g in range(grp_count):
            for h in range(high_count):
                for w in range(low_count):
                    for n in range(near_count):
                        source = ((g * high_count + h) * low_count + w) * near_count + n
                        g2 = step_to(g, grp, grp_count)
                        h2 = step_to(h, high, high_count)
                        w2 = step_to(w, low, low_count)
                        n2 = step_to(n, near, near_count)
                        target = ((g2 * high_count + h2) * low_count + w2) * near_count + n2
                        perm.append((source, target))
        return lax.ppermute(value, AXES, perm)

    def on_device(images, texts, logit_scale, logit_bias):
        params = jnp.concatenate(
            [logit_scale * -LOG2_E, logit_bias * -LOG2_E, logit_scale]
        ).reshape(1, 3)
        early = {(0, 0): images}
        for h in range(1, high_count):
            early[h, 0] = move(images, high=h)
        for w in range(1, low_count):
            early[0, w] = move(images, low=w)
        late = {}
        for h in range(1, high_count):
            block, params = lax.optimization_barrier((early[h, 0], params))
            for w in range(1, low_count):
                late[h, w] = move(block, low=w)
        near_rows = [units([texts], "own_units")] + [move(texts, near=n) for n in range(1, near_count)]
        own_stack = stack_units(near_rows)
        stacks = [own_stack] + [move(own_stack, grp=g) for g in range(1, grp_count)]
        image_parts, text_parts = pair_terms(
            params, list(early.values()), list(late.values()), stacks
        )
        far_parts = dict(zip([*early, *late], image_parts))
        came = [move(part, grp=-g) for g, part in enumerate(text_parts) if g]
        far_order = sorted((step for step in far_parts if step != (0, 0)), key=lambda step: step[0])
        far_came = [move(far_parts[h, w], high=-h, low=-w) for h, w in far_order]
        near_parts = add_stacks([text_parts[0], *came], near_count)
        near_parts = [near_parts[0]] + [
            move(part, near=-n) for n, part in enumerate(near_parts) if n
        ]
        return finish(
            own_rows([images, texts]),
            [(0, part) for part in [far_parts[0, 0]] + far_came]
            + [(1, part) for part in near_parts],
        )

    in_specs = (P(AXES, None), P(AXES, None), P(), P())
    out_specs = (P(AXES, None), P(AXES, None))
    return jax.shard_map(
        on_device, mesh=mesh, in_specs=in_specs, out_specs=out_specs, check_vma=False
    )
```

```python
import functools
import math

import jax
import jax.numpy as jnp
from jax import lax
from jax.experimental import pallas as pl
from jax.experimental.pallas import tpu as pltpu
from jax.sharding import PartitionSpec as P

AXES = ("grp", "dev")
VMEM_LIMIT = 32 * 1024 * 1024
SPAN = 256
PIECE = 32
LATE = 16500
KEPT = 60000
LOG2_E = math.log2(math.e)
VMEM = pl.BlockSpec(memory_space=pltpu.VMEM)


def unit_rows(raw):
    wide = raw.astype(jnp.float32)
    factor = lax.rsqrt(jnp.sum(wide * wide, axis=-1, keepdims=True) + 1e-06)
    return wide * factor, factor


def call(kernel, out_shape, operands, scratch=(), flops=0, transcendentals=0, name=None):
    touched = sum(x.size * x.dtype.itemsize for x in list(operands) + list(out_shape))
    outs = pl.pallas_call(
        kernel,
        out_shape=out_shape,
        in_specs=[VMEM] * len(operands),
        out_specs=[VMEM] * len(out_shape),
        scratch_shapes=scratch,
        compiler_params=pltpu.CompilerParams(vmem_limit_bytes=VMEM_LIMIT),
        cost_estimate=pl.CostEstimate(
            flops=flops, bytes_accessed=touched, transcendentals=transcendentals
        ),
        name=name,
    )(*operands)
    return tuple(outs)


def units_kernel(*refs):
    rows = refs[0].shape[0]
    for at, ref in enumerate(refs[:-1]):
        refs[-1][at * rows:(at + 1) * rows, :] = unit_rows(ref[...])[0].astype(refs[-1].dtype)


def units(blocks, name, weight=1):
    rows, width = blocks[0].shape
    out = jax.ShapeDtypeStruct((len(blocks) * rows, width), jnp.bfloat16)
    return call(units_kernel, [out], blocks, flops=4 * weight * out.size, name=name)[0]


def stack_units_kernel(*refs):
    out = refs[-1]
    rows = refs[0].shape[0]
    out[:rows, :] = refs[0][...]
    for at, ref in enumerate(refs[1:-1], 1):
        out[at * rows:(at + 1) * rows, :] = unit_rows(ref[...])[0].astype(out.dtype)


def stack_units(blocks):
    rows, width = blocks[0].shape
    out = jax.ShapeDtypeStruct((len(blocks) * rows, width), jnp.bfloat16)
    return call(stack_units_kernel, [out], blocks, flops=4 * out.size, name="stack_units")[0]


def pairs(vi, params_ref, text_ref, text_out, own=0, text_add=None):
    slope, shift, temper = (params_ref[0:1, at:at + 1] for at in range(3))
    held = text_ref.shape[0]
    total = None

    def dots_of(first):
        return lax.dot_general(
            vi,
            text_ref[first:min(first + SPAN, held), :],
            (((1,), (1,)), ((), ())),
            preferred_element_type=jnp.float32,
        )

    coming = dots_of(0)
    for first in range(0, held, SPAN):
        last = min(first + SPAN, held)
        dots, coming = coming, dots_of(last) if last < held else None
        vt = text_ref[first:last, :]
        e = jnp.exp2(slope * dots + shift)
        chance = pl.reciprocal(1.0 + e, approx=True)
        if own and first == 0:
            row = lax.broadcasted_iota(jnp.int32, chance.shape, 0)
            column = lax.broadcasted_iota(jnp.int32, chance.shape, 1)
            same = (row == column) & (row < own)
            chance = jnp.where(same, -e * chance, chance)
        coefficient = (temper * chance).astype(jnp.bfloat16)
        text_part = lax.dot_general(
            coefficient, vi, (((0,), (0,)), ((), ())), preferred_element_type=jnp.float32
        )
        if text_add is not None:
            text_part = text_add[first:last, :] + text_part
        text_out[first:last, :] = text_part.astype(text_out.dtype)
        part = jnp.dot(coefficient, vt, preferred_element_type=jnp.float32)
        total = part if total is None else total + part
    return total


def early_pairs_kernel(params_ref, text_ref, *refs):
    image_refs, (text_out, units_out, total_out) = refs[:-3], refs[-3:]
    rows = image_refs[0].shape[0]
    for a, ref in enumerate(image_refs):
        units_out[a * rows:(a + 1) * rows, :] = unit_rows(ref[...])[0].astype(jnp.bfloat16)
    total_out[...] = pairs(units_out[...], params_ref, text_ref, text_out, own=rows)


def rest_pairs_kernel(
    count, params_ref, early_ref, total_ref, own_text_ref, own_add_ref, late_ref, *refs
):
    text_refs, own_out = refs[:count], refs[count]
    other_out, image_out = refs[count + 1:2 * count + 1], refs[2 * count + 1:]
    rows = image_out[0].shape[0]
    early, late = early_ref[...], late_ref[...]
    total = jnp.concatenate(
        [
            total_ref[...],
            pairs(late, params_ref, own_text_ref, own_out, text_add=own_add_ref),
        ],
        axis=0,
    )
    vi = jnp.concatenate([early, late], axis=0)
    for text_ref, out in zip(text_refs, other_out):
        total = total + pairs(vi, params_ref, text_ref, out)
    for a, ref in enumerate(image_out):
        ref[...] = total[a * rows:(a + 1) * rows, :].astype(ref.dtype)


def pair_terms(params, early, late, texts):
    rows, width = early[0].shape
    early_rows, late_rows = rows * len(early), rows * len(late)
    own, others = texts[0], texts[1:]
    other_rows = sum(t.shape[0] for t in others)

    def cost(pair_count):
        return dict(flops=6 * pair_count * width, transcendentals=2 * pair_count)

    own_add, early_units, total = call(
        early_pairs_kernel,
        [
            jax.ShapeDtypeStruct(own.shape, jnp.float32),
            jax.ShapeDtypeStruct((early_rows, width), jnp.bfloat16),
            jax.ShapeDtypeStruct((early_rows, width), jnp.float32),
        ],
        [params, own, *early],
        name="early_pairs",
        **cost(early_rows * own.shape[0]),
    )
    late_units = units(late, "late_units", LATE)
    outs = call(
        functools.partial(rest_pairs_kernel, len(others)),
        [jax.ShapeDtypeStruct(own.shape, jnp.float32)]
        + [jax.ShapeDtypeStruct(t.shape, jnp.bfloat16) for t in others]
        + [jax.ShapeDtypeStruct((rows, width), jnp.float32)]
        + [jax.ShapeDtypeStruct((rows, width), jnp.bfloat16)] * (len(early) + len(late) - 1),
        [params, early_units, total, own, own_add, late_units, *others],
        name="rest_pairs",
        **cost(late_rows * own.shape[0] + (early_rows + late_rows) * other_rows),
    )
    count = 1 + len(others)
    return outs[count:], outs[:count]


def add_stacks_kernel(first, part_count, *refs):
    parts, outs = refs[:part_count], refs[part_count:]
    rows = outs[0].shape[0]
    for at, out in enumerate(outs, first):
        total = parts[0][at * rows:(at + 1) * rows, :]
        for part in parts[1:]:
            total = total + part[at * rows:(at + 1) * rows, :].astype(jnp.float32)
        out[...] = total.astype(out.dtype)


def add_stacks(parts, count, first, last, dtype, name, weight=1):
    shape = (parts[0].shape[0] // count, parts[0].shape[1])
    return call(
        functools.partial(add_stacks_kernel, first, len(parts)),
        [jax.ShapeDtypeStruct(shape, dtype)] * (last - first),
        parts,
        flops=weight * len(parts) * (last - first) * shape[0] * shape[1],
        name=name,
    )


def finish_kernel(sides, image_ref, text_ref, *refs):
    parts, outs = refs[:len(sides)], refs[len(sides):len(sides) + 2]
    staged, sems = refs[len(sides) + 2:]
    rows = image_ref.shape[0]
    piece = math.gcd(rows, PIECE)
    copies = []
    for side, raw in enumerate((image_ref, text_ref)):
        for first in range(0, rows, piece):
            here = pl.ds(first, piece)
            unit, factor = unit_rows(raw[here, :])
            total = sum(
                ref[here, :].astype(jnp.float32) for at, ref in zip(sides, parts) if at == side
            )
            along = jnp.sum(unit * total, axis=-1, keepdims=True)
            staged[side, here, :] = factor * (total - unit * along)
            copies.append(
                pltpu.make_async_copy(
                    staged.at[side, here, :], outs[side].at[here, :], sems.at[len(copies)]
                )
            )
            copies[-1].start()
    for copy in copies:
        copy.wait()


def finish(images, texts, parts):
    out = jax.ShapeDtypeStruct(images.shape, jnp.float32)
    return pl.pallas_call(
        functools.partial(finish_kernel, [side for side, _ in parts]),
        out_shape=(out, out),
        in_specs=[VMEM] * (2 + len(parts)),
        out_specs=[pl.BlockSpec(memory_space=pl.ANY)] * 2,
        scratch_shapes=[
            pltpu.VMEM((2,) + images.shape, jnp.float32),
            pltpu.SemaphoreType.DMA((2 * (images.shape[0] // math.gcd(images.shape[0], PIECE)),)),
        ],
        compiler_params=pltpu.CompilerParams(vmem_limit_bytes=VMEM_LIMIT),
        cost_estimate=pl.CostEstimate(
            flops=10 * len(parts) * images.size,
            bytes_accessed=3 * len(parts) * images.size,
            transcendentals=0,
        ),
        name="finish",
    )(images, texts, *[part for _, part in parts])


def plan(grp_count, dev_count):
    options = [n for n in range(1, dev_count + 1) if dev_count % n == 0]
    near = min(options, key=lambda n: (dev_count // n + grp_count * n, -n))
    return dev_count // near, near


def step_to(at, by, count):
    if count & (count - 1) == 0:
        return at ^ abs(by)
    return (at + by) % count


def solution(mesh):
    grp_count, dev_count = mesh.shape["grp"], mesh.shape["dev"]
    far_count, near_count = plan(grp_count, dev_count)
    low_count = 2 if far_count % 2 == 0 else 1
    high_count = far_count // low_count

    def move(value, grp=0, high=0, low=0, near=0):
        perm = []
        for g in range(grp_count):
            for h in range(high_count):
                for w in range(low_count):
                    for n in range(near_count):
                        source = ((g * high_count + h) * low_count + w) * near_count + n
                        g2 = step_to(g, grp, grp_count)
                        h2 = step_to(h, high, high_count)
                        w2 = step_to(w, low, low_count)
                        n2 = step_to(n, near, near_count)
                        target = ((g2 * high_count + h2) * low_count + w2) * near_count + n2
                        perm.append((source, target))
        return lax.ppermute(value, AXES, perm)

    def on_device(images, texts, logit_scale, logit_bias):
        params = jnp.concatenate(
            [logit_scale * -LOG2_E, logit_bias * -LOG2_E, logit_scale]
        ).reshape(1, 3)
        early = {(0, 0): images}
        for h in range(1, high_count):
            early[h, 0] = move(images, high=h)
        for w in range(1, low_count):
            early[0, w] = move(images, low=w)
        late = {}
        for h in range(1, high_count):
            block, params = lax.optimization_barrier((early[h, 0], params))
            for w in range(1, low_count):
                late[h, w] = move(block, low=w)
        near_rows = [units([texts], "own_units")] + [move(texts, near=n) for n in range(1, near_count)]
        own_stack = stack_units(near_rows)
        stacks = [own_stack] + [move(own_stack, grp=g) for g in range(1, grp_count)]
        image_parts, text_parts = pair_terms(
            params, list(early.values()), list(late.values()), stacks
        )
        far_parts = dict(zip([*early, *late], image_parts))
        came = [move(part, grp=-g) for g, part in enumerate(text_parts) if g]
        def give_back(h, w):
            return move(far_parts[h, w], high=-h, low=-w)

        stacks = [text_parts[0], *came]
        sent = add_stacks(stacks, near_count, 1, near_count, jnp.bfloat16, "add_sent")
        (kept,) = add_stacks(stacks, near_count, 0, 1, jnp.float32, "add_kept", KEPT)
        near_came = [move(part, near=-n) for n, part in enumerate(sent, 1)]
        far_came = [give_back(h, w) for h, w in far_parts if h]
        low_parts = [far_parts[0, w] for w in range(1, low_count)]
        low_parts, near_came[:1], kept = lax.optimization_barrier((low_parts, near_came[:1], kept))
        low_came = [move(part, low=-w) for w, part in enumerate(low_parts, 1)]
        return finish(
            images,
            texts,
            [(0, part) for part in [far_parts[0, 0]] + far_came]
            + [(1, part) for part in [kept] + near_came]
            + [(0, part) for part in low_came],
        )

    in_specs = (P(AXES, None), P(AXES, None), P(), P())
    out_specs = (P(AXES, None), P(AXES, None))
    return jax.shard_map(
        on_device, mesh=mesh, in_specs=in_specs, out_specs=out_specs, check_vma=False
    )
```

```python
import functools
import math

import jax
import jax.numpy as jnp
from jax import lax
from jax.experimental import pallas as pl
from jax.experimental.pallas import tpu as pltpu
from jax.sharding import PartitionSpec as P

AXES = ("grp", "dev")
VMEM_LIMIT = 32 * 1024 * 1024
SPAN = 256
PIECE = 32
LATE = 16500
KEPT = 60000
LOG2_E = math.log2(math.e)
VMEM = pl.BlockSpec(memory_space=pltpu.VMEM)


def unit_rows(raw):
    wide = raw.astype(jnp.float32)
    factor = lax.rsqrt(jnp.sum(wide * wide, axis=-1, keepdims=True) + 1e-06)
    return wide * factor, factor


def call(kernel, out_shape, operands, scratch=(), flops=0, transcendentals=0, name=None):
    touched = sum(x.size * x.dtype.itemsize for x in list(operands) + list(out_shape))
    outs = pl.pallas_call(
        kernel,
        out_shape=out_shape,
        in_specs=[VMEM] * len(operands),
        out_specs=[VMEM] * len(out_shape),
        scratch_shapes=scratch,
        compiler_params=pltpu.CompilerParams(vmem_limit_bytes=VMEM_LIMIT),
        cost_estimate=pl.CostEstimate(
            flops=flops, bytes_accessed=touched, transcendentals=transcendentals
        ),
        name=name,
    )(*operands)
    return tuple(outs)


def units_kernel(*refs):
    rows = refs[0].shape[0]
    for at, ref in enumerate(refs[:-1]):
        refs[-1][at * rows:(at + 1) * rows, :] = unit_rows(ref[...])[0].astype(refs[-1].dtype)


def units(blocks, name, weight=1):
    rows, width = blocks[0].shape
    out = jax.ShapeDtypeStruct((len(blocks) * rows, width), jnp.bfloat16)
    return call(units_kernel, [out], blocks, flops=4 * weight * out.size, name=name)[0]


def stack_units_kernel(*refs):
    out = refs[-1]
    rows = refs[0].shape[0]
    out[:rows, :] = refs[0][...]
    for at, ref in enumerate(refs[1:-1], 1):
        out[at * rows:(at + 1) * rows, :] = unit_rows(ref[...])[0].astype(out.dtype)


def stack_units(blocks):
    rows, width = blocks[0].shape
    out = jax.ShapeDtypeStruct((len(blocks) * rows, width), jnp.bfloat16)
    return call(stack_units_kernel, [out], blocks, flops=4 * out.size, name="stack_units")[0]


def pairs(vi, params_ref, text_ref, text_out, own=0, text_add=None):
    slope, shift, temper = (params_ref[0:1, at:at + 1] for at in range(3))
    held = text_ref.shape[0]
    total = None

    def dots_of(first):
        return lax.dot_general(
            vi,
            text_ref[first:min(first + SPAN, held), :],
            (((1,), (1,)), ((), ())),
            preferred_element_type=jnp.float32,
        )

    coming = dots_of(0)
    for first in range(0, held, SPAN):
        last = min(first + SPAN, held)
        dots, coming = coming, dots_of(last) if last < held else None
        vt = text_ref[first:last, :]
        e = jnp.exp2(slope * dots + shift)
        chance = pl.reciprocal(1.0 + e, approx=True)
        if own and first == 0:
            row = lax.broadcasted_iota(jnp.int32, chance.shape, 0)
            column = lax.broadcasted_iota(jnp.int32, chance.shape, 1)
            same = (row == column) & (row < own)
            chance = jnp.where(same, -e * chance, chance)
        coefficient = (temper * chance).astype(jnp.bfloat16)
        text_part = lax.dot_general(
            coefficient, vi, (((0,), (0,)), ((), ())), preferred_element_type=jnp.float32
        )
        if text_add is not None:
            text_part = text_add[first:last, :] + text_part
        text_out[first:last, :] = text_part.astype(text_out.dtype)
        part = jnp.dot(coefficient, vt, preferred_element_type=jnp.float32)
        total = part if total is None else total + part
    return total


def early_pairs_kernel(params_ref, text_ref, *refs):
    image_refs, (text_out, units_out, total_out) = refs[:-3], refs[-3:]
    rows = image_refs[0].shape[0]
    for a, ref in enumerate(image_refs):
        units_out[a * rows:(a + 1) * rows, :] = unit_rows(ref[...])[0].astype(jnp.bfloat16)
    total_out[...] = pairs(units_out[...], params_ref, text_ref, text_out, own=rows)


def rest_pairs_kernel(
    count, params_ref, early_ref, total_ref, own_text_ref, own_add_ref, late_ref, *refs
):
    text_refs, own_out = refs[:count], refs[count]
    other_out, image_out = refs[count + 1:2 * count + 1], refs[2 * count + 1:]
    rows = image_out[0].shape[0]
    early, late = early_ref[...], late_ref[...]
    total = jnp.concatenate(
        [
            total_ref[...],
            pairs(late, params_ref, own_text_ref, own_out, text_add=own_add_ref),
        ],
        axis=0,
    )
    vi = jnp.concatenate([early, late], axis=0)
    for text_ref, out in zip(text_refs, other_out):
        total = total + pairs(vi, params_ref, text_ref, out)
    for a, ref in enumerate(image_out):
        ref[...] = total[a * rows:(a + 1) * rows, :].astype(ref.dtype)


def pair_terms(params, early, late, texts):
    rows, width = early[0].shape
    early_rows, late_rows = rows * len(early), rows * len(late)
    own, others = texts[0], texts[1:]
    other_rows = sum(t.shape[0] for t in others)

    def cost(pair_count):
        return dict(flops=6 * pair_count * width, transcendentals=2 * pair_count)

    own_add, early_units, total = call(
        early_pairs_kernel,
        [
            jax.ShapeDtypeStruct(own.shape, jnp.float32),
            jax.ShapeDtypeStruct((early_rows, width), jnp.bfloat16),
            jax.ShapeDtypeStruct((early_rows, width), jnp.float32),
        ],
        [params, own, *early],
        name="early_pairs",
        **cost(early_rows * own.shape[0]),
    )
    late_units = units(late, "late_units", LATE)
    outs = call(
        functools.partial(rest_pairs_kernel, len(others)),
        [jax.ShapeDtypeStruct(own.shape, jnp.float32)]
        + [jax.ShapeDtypeStruct(t.shape, jnp.bfloat16) for t in others]
        + [jax.ShapeDtypeStruct((rows, width), jnp.float32)]
        + [jax.ShapeDtypeStruct((rows, width), jnp.bfloat16)] * (len(early) + len(late) - 1),
        [params, early_units, total, own, own_add, late_units, *others],
        name="rest_pairs",
        **cost(late_rows * own.shape[0] + (early_rows + late_rows) * other_rows),
    )
    count = 1 + len(others)
    return outs[count:], outs[:count]


def add_stacks_kernel(first, part_count, *refs):
    parts, outs = refs[:part_count], refs[part_count:]
    rows = outs[0].shape[0]
    for at, out in enumerate(outs, first):
        total = parts[0][at * rows:(at + 1) * rows, :]
        for part in parts[1:]:
            total = total + part[at * rows:(at + 1) * rows, :].astype(jnp.float32)
        out[...] = total.astype(out.dtype)


def add_stacks(parts, count, first, last, dtype, name, weight=1):
    shape = (parts[0].shape[0] // count, parts[0].shape[1])
    return call(
        functools.partial(add_stacks_kernel, first, len(parts)),
        [jax.ShapeDtypeStruct(shape, dtype)] * (last - first),
        parts,
        flops=weight * len(parts) * (last - first) * shape[0] * shape[1],
        name=name,
    )


def finish_kernel(sides, image_ref, text_ref, *refs):
    parts, outs = refs[:len(sides)], refs[len(sides):len(sides) + 2]
    staged, sems = refs[len(sides) + 2:]
    rows = image_ref.shape[0]
    piece = math.gcd(rows, PIECE)
    copies = []
    for side, raw in enumerate((image_ref, text_ref)):
        for first in range(0, rows, piece):
            here = pl.ds(first, piece)
            unit, factor = unit_rows(raw[here, :])
            total = sum(
                ref[here, :].astype(jnp.float32) for at, ref in zip(sides, parts) if at == side
            )
            along = jnp.sum(unit * total, axis=-1, keepdims=True)
            staged[side, here, :] = factor * (total - unit * along)
            copies.append(
                pltpu.make_async_copy(
                    staged.at[side, here, :], outs[side].at[here, :], sems.at[len(copies)]
                )
            )
            copies[-1].start()
    for copy in copies:
        copy.wait()


def finish(images, texts, parts):
    out = jax.ShapeDtypeStruct(images.shape, jnp.float32)
    return pl.pallas_call(
        functools.partial(finish_kernel, [side for side, _ in parts]),
        out_shape=(out, out),
        in_specs=[VMEM] * (2 + len(parts)),
        out_specs=[pl.BlockSpec(memory_space=pl.ANY)] * 2,
        scratch_shapes=[
            pltpu.VMEM((2,) + images.shape, jnp.float32),
            pltpu.SemaphoreType.DMA((2 * (images.shape[0] // math.gcd(images.shape[0], PIECE)),)),
        ],
        compiler_params=pltpu.CompilerParams(vmem_limit_bytes=VMEM_LIMIT),
        cost_estimate=pl.CostEstimate(
            flops=10 * len(parts) * images.size,
            bytes_accessed=3 * len(parts) * images.size,
            transcendentals=0,
        ),
        name="finish",
    )(images, texts, *[part for _, part in parts])


def plan(grp_count, dev_count):
    options = [n for n in range(1, dev_count + 1) if dev_count % n == 0]
    near = min(options, key=lambda n: (dev_count // n + grp_count * n, -n))
    return dev_count // near, near


def step_to(at, by, count):
    if count & (count - 1) == 0:
        return at ^ abs(by)
    return (at + by) % count


def solution(mesh):
    grp_count, dev_count = mesh.shape["grp"], mesh.shape["dev"]
    far_count, near_count = plan(grp_count, dev_count)
    low_count = 2 if far_count % 2 == 0 else 1
    high_count = far_count // low_count

    def move(value, grp=0, high=0, low=0, near=0):
        perm = []
        for g in range(grp_count):
            for h in range(high_count):
                for w in range(low_count):
                    for n in range(near_count):
                        source = ((g * high_count + h) * low_count + w) * near_count + n
                        g2 = step_to(g, grp, grp_count)
                        h2 = step_to(h, high, high_count)
                        w2 = step_to(w, low, low_count)
                        n2 = step_to(n, near, near_count)
                        target = ((g2 * high_count + h2) * low_count + w2) * near_count + n2
                        perm.append((source, target))
        return lax.ppermute(value, AXES, perm)

    def on_device(images, texts, logit_scale, logit_bias):
        params = jnp.concatenate(
            [logit_scale * -LOG2_E, logit_bias * -LOG2_E, logit_scale]
        ).reshape(1, 3)
        early = {(0, 0): images}
        for h in range(1, high_count):
            early[h, 0] = move(images, high=h)
        for w in range(1, low_count):
            early[0, w] = move(images, low=w)
        late = {}
        for h in range(1, high_count):
            block, params = lax.optimization_barrier((early[h, 0], params))
            for w in range(1, low_count):
                late[h, w] = move(block, low=w)
        near_rows = [units([texts], "own_units")] + [move(texts, near=n) for n in range(1, near_count)]
        own_stack = stack_units(near_rows)
        stacks = [own_stack] + [move(own_stack, grp=g) for g in range(1, grp_count)]
        image_parts, text_parts = pair_terms(
            params, list(early.values()), list(late.values()), stacks
        )
        far_parts = dict(zip([*early, *late], image_parts))
        came = [move(part, grp=-g) for g, part in enumerate(text_parts) if g]
        def give_back(h, w):
            return move(far_parts[h, w], high=-h, low=-w)

        stacks = [text_parts[0], *came]
        sent = add_stacks(stacks, near_count, 1, near_count, jnp.bfloat16, "add_sent")
        (kept,) = add_stacks(stacks, near_count, 0, 1, jnp.float32, "add_kept", KEPT)
        low_parts = [far_parts[0, w] for w in range(1, low_count)]
        low_parts, sent = lax.optimization_barrier((low_parts, list(sent)))
        near_came = [move(part, near=-n) for n, part in enumerate(sent[:-1], 1)]
        last, near_came[:1], kept = lax.optimization_barrier((sent[-1:], near_came[:1], kept))
        near_came += [move(part, near=1 - near_count) for part in last]
        far_came = [give_back(h, w) for h, w in far_parts if h]
        low_came = [move(part, low=-w) for w, part in enumerate(low_parts, 1)]
        return finish(
            images,
            texts,
            [(0, part) for part in [far_parts[0, 0]] + far_came]
            + [(1, part) for part in [kept] + near_came]
            + [(0, part) for part in low_came],
        )

    in_specs = (P(AXES, None), P(AXES, None), P(), P())
    out_specs = (P(AXES, None), P(AXES, None))
    return jax.shard_map(
        on_device, mesh=mesh, in_specs=in_specs, out_specs=out_specs, check_vma=False
    )
```

```python
import functools
import math

import jax
import jax.numpy as jnp
from jax import lax
from jax.experimental import pallas as pl
from jax.experimental.pallas import tpu as pltpu
from jax.sharding import PartitionSpec as P

AXES = ("grp", "dev")
VMEM_LIMIT = 32 * 1024 * 1024
SPAN = 256
PIECE = 32
LATE = 16500
LOG2_E = math.log2(math.e)
VMEM = pl.BlockSpec(memory_space=pltpu.VMEM)


def unit_rows(raw):
    wide = raw.astype(jnp.float32)
    factor = lax.rsqrt(jnp.sum(wide * wide, axis=-1, keepdims=True) + 1e-06)
    return wide * factor, factor


def call(kernel, out_shape, operands, scratch=(), flops=0, transcendentals=0, name=None):
    touched = sum(x.size * x.dtype.itemsize for x in list(operands) + list(out_shape))
    outs = pl.pallas_call(
        kernel,
        out_shape=out_shape,
        in_specs=[VMEM] * len(operands),
        out_specs=[VMEM] * len(out_shape),
        scratch_shapes=scratch,
        compiler_params=pltpu.CompilerParams(vmem_limit_bytes=VMEM_LIMIT),
        cost_estimate=pl.CostEstimate(
            flops=flops, bytes_accessed=touched, transcendentals=transcendentals
        ),
        name=name,
    )(*operands)
    return tuple(outs)


def units_kernel(*refs):
    rows = refs[0].shape[0]
    for at, ref in enumerate(refs[:-1]):
        refs[-1][at * rows:(at + 1) * rows, :] = unit_rows(ref[...])[0].astype(refs[-1].dtype)


def units(blocks, name, weight=1):
    rows, width = blocks[0].shape
    out = jax.ShapeDtypeStruct((len(blocks) * rows, width), jnp.bfloat16)
    return call(units_kernel, [out], blocks, flops=4 * weight * out.size, name=name)[0]


def stack_units_kernel(*refs):
    out = refs[-1]
    rows = refs[0].shape[0]
    out[:rows, :] = refs[0][...]
    for at, ref in enumerate(refs[1:-1], 1):
        out[at * rows:(at + 1) * rows, :] = unit_rows(ref[...])[0].astype(out.dtype)


def stack_units(blocks):
    rows, width = blocks[0].shape
    out = jax.ShapeDtypeStruct((len(blocks) * rows, width), jnp.bfloat16)
    return call(stack_units_kernel, [out], blocks, flops=4 * out.size, name="stack_units")[0]


def pairs(params_ref, jobs):
    slope, shift, temper = (params_ref[0:1, at:at + 1] for at in range(3))
    chunks = [
        (at, first, min(first + SPAN, job[1].shape[0]))
        for at, job in enumerate(jobs) for first in range(0, job[1].shape[0], SPAN)
    ]

    def dots_of(at, first, last):
        vi, text_ref = jobs[at][:2]
        return lax.dot_general(
            vi, text_ref[first:last, :], (((1,), (1,)), ((), ())),
            preferred_element_type=jnp.float32,
        )

    totals = [None] * len(jobs)
    coming = dots_of(*chunks[0])
    for step, (at, first, last) in enumerate(chunks):
        vi, text_ref, text_out, own, text_add = jobs[at]
        dots, coming = coming, dots_of(*chunks[step + 1]) if step + 1 < len(chunks) else None
        vt = text_ref[first:last, :]
        e = jnp.exp2(slope * dots + shift)
        chance = pl.reciprocal(1.0 + e, approx=True)
        if own and first == 0:
            row = lax.broadcasted_iota(jnp.int32, chance.shape, 0)
            column = lax.broadcasted_iota(jnp.int32, chance.shape, 1)
            same = (row == column) & (row < own)
            chance = jnp.where(same, -e * chance, chance)
        coefficient = (temper * chance).astype(jnp.bfloat16)
        text_part = lax.dot_general(
            coefficient, vi, (((0,), (0,)), ((), ())), preferred_element_type=jnp.float32
        )
        if text_add is not None:
            text_part = text_add[first:last, :] + text_part
        text_out[first:last, :] = text_part.astype(text_out.dtype)
        part = jnp.dot(coefficient, vt, preferred_element_type=jnp.float32)
        totals[at] = part if totals[at] is None else totals[at] + part
    return totals


def early_pairs_kernel(params_ref, text_ref, *refs):
    image_refs, (text_out, units_out, total_out) = refs[:-3], refs[-3:]
    rows = image_refs[0].shape[0]
    for a, ref in enumerate(image_refs):
        units_out[a * rows:(a + 1) * rows, :] = unit_rows(ref[...])[0].astype(jnp.bfloat16)
    (total,) = pairs(params_ref, [(units_out[...], text_ref, text_out, rows, None)])
    total_out[...] = total


def rest_pairs_kernel(
    count, params_ref, early_ref, total_ref, own_text_ref, own_add_ref, late_ref, *refs
):
    text_refs, own_out = refs[:count], refs[count]
    other_out, image_out = refs[count + 1:2 * count + 1], refs[2 * count + 1:]
    rows = image_out[0].shape[0]
    early, late = early_ref[...], late_ref[...]
    vi = jnp.concatenate([early, late], axis=0)
    late_total, *totals = pairs(
        params_ref,
        [(late, own_text_ref, own_out, 0, own_add_ref)]
        + [(vi, text_ref, out, 0, None) for text_ref, out in zip(text_refs, other_out)],
    )
    total = sum(totals, jnp.concatenate([total_ref[...], late_total], axis=0))
    for a, ref in enumerate(image_out):
        ref[...] = total[a * rows:(a + 1) * rows, :].astype(ref.dtype)


def pair_terms(params, early, late, texts):
    rows, width = early[0].shape
    early_rows, late_rows = rows * len(early), rows * len(late)
    own, others = texts[0], texts[1:]
    other_rows = sum(t.shape[0] for t in others)

    def cost(pair_count):
        return dict(flops=6 * pair_count * width, transcendentals=2 * pair_count)

    own_add, early_units, total = call(
        early_pairs_kernel,
        [
            jax.ShapeDtypeStruct(own.shape, jnp.float32),
            jax.ShapeDtypeStruct((early_rows, width), jnp.bfloat16),
            jax.ShapeDtypeStruct((early_rows, width), jnp.float32),
        ],
        [params, own, *early],
        name="early_pairs",
        **cost(early_rows * own.shape[0]),
    )
    late_units = units(late, "late_units", LATE)
    outs = call(
        functools.partial(rest_pairs_kernel, len(others)),
        [jax.ShapeDtypeStruct(own.shape, jnp.float32)]
        + [jax.ShapeDtypeStruct(t.shape, jnp.bfloat16) for t in others]
        + [jax.ShapeDtypeStruct((rows, width), jnp.float32)]
        + [jax.ShapeDtypeStruct((rows, width), jnp.bfloat16)] * (len(early) + len(late) - 1),
        [params, early_units, total, own, own_add, late_units, *others],
        name="rest_pairs",
        **cost(late_rows * own.shape[0] + (early_rows + late_rows) * other_rows),
    )
    count = 1 + len(others)
    return outs[count:], outs[:count]


def add_stacks_kernel(part_count, *refs):
    parts, outs = refs[:part_count], refs[part_count:]
    rows = outs[0].shape[0]
    for at, out in enumerate(outs):
        total = parts[0][at * rows:(at + 1) * rows, :].astype(jnp.float32)
        for part in parts[1:]:
            total = total + part[at * rows:(at + 1) * rows, :].astype(jnp.float32)
        out[...] = total.astype(out.dtype)


def add_stacks(parts, count):
    shape = (parts[0].shape[0] // count, parts[0].shape[1])
    types = [jnp.float32] + [jnp.bfloat16] * (count - 1)
    return call(
        functools.partial(add_stacks_kernel, len(parts)),
        [jax.ShapeDtypeStruct(shape, t) for t in types],
        parts,
        flops=len(parts) * parts[0].size,
        name="add_stacks",
    )


def finish_kernel(sides, image_ref, text_ref, *refs):
    parts, outs = refs[:len(sides)], refs[len(sides):len(sides) + 2]
    staged, sems = refs[len(sides) + 2:]
    rows = image_ref.shape[0]
    piece = math.gcd(rows, PIECE)
    copies = []
    for side, raw in enumerate((image_ref, text_ref)):
        for first in range(0, rows, piece):
            here = pl.ds(first, piece)
            unit, factor = unit_rows(raw[here, :])
            total = sum(
                ref[here, :].astype(jnp.float32) for at, ref in zip(sides, parts) if at == side
            )
            along = jnp.sum(unit * total, axis=-1, keepdims=True)
            staged[side, here, :] = factor * (total - unit * along)
            copies.append(
                pltpu.make_async_copy(
                    staged.at[side, here, :], outs[side].at[here, :], sems.at[len(copies)]
                )
            )
            copies[-1].start()
    for copy in copies:
        copy.wait()


def finish(images, texts, parts):
    out = jax.ShapeDtypeStruct(images.shape, jnp.float32)
    return pl.pallas_call(
        functools.partial(finish_kernel, [side for side, _ in parts]),
        out_shape=(out, out),
        in_specs=[VMEM] * (2 + len(parts)),
        out_specs=[pl.BlockSpec(memory_space=pl.ANY)] * 2,
        scratch_shapes=[
            pltpu.VMEM((2,) + images.shape, jnp.float32),
            pltpu.SemaphoreType.DMA((2 * (images.shape[0] // math.gcd(images.shape[0], PIECE)),)),
        ],
        compiler_params=pltpu.CompilerParams(vmem_limit_bytes=VMEM_LIMIT),
        cost_estimate=pl.CostEstimate(
            flops=10 * len(parts) * images.size,
            bytes_accessed=3 * len(parts) * images.size,
            transcendentals=0,
        ),
        name="finish",
    )(images, texts, *[part for _, part in parts])


def plan(grp_count, dev_count):
    options = [n for n in range(1, dev_count + 1) if dev_count % n == 0]
    near = min(options, key=lambda n: (dev_count // n + grp_count * n, -n))
    return dev_count // near, near


def step_to(at, by, count):
    if count & (count - 1) == 0:
        return at ^ abs(by)
    return (at + by) % count


def solution(mesh):
    grp_count, dev_count = mesh.shape["grp"], mesh.shape["dev"]
    far_count, near_count = plan(grp_count, dev_count)
    low_count = 2 if far_count % 2 == 0 else 1
    high_count = far_count // low_count

    def move(value, grp=0, high=0, low=0, near=0):
        perm = []
        for g in range(grp_count):
            for h in range(high_count):
                for w in range(low_count):
                    for n in range(near_count):
                        source = ((g * high_count + h) * low_count + w) * near_count + n
                        g2 = step_to(g, grp, grp_count)
                        h2 = step_to(h, high, high_count)
                        w2 = step_to(w, low, low_count)
                        n2 = step_to(n, near, near_count)
                        target = ((g2 * high_count + h2) * low_count + w2) * near_count + n2
                        perm.append((source, target))
        return lax.ppermute(value, AXES, perm)

    def on_device(images, texts, logit_scale, logit_bias):
        params = jnp.concatenate(
            [logit_scale * -LOG2_E, logit_bias * -LOG2_E, logit_scale]
        ).reshape(1, 3)
        early = {(0, 0): images}
        for h in range(1, high_count):
            early[h, 0] = move(images, high=h)
        for w in range(1, low_count):
            early[0, w] = move(images, low=w)
        late = {}
        for h in range(1, high_count):
            block, params = lax.optimization_barrier((early[h, 0], params))
            for w in range(1, low_count):
                late[h, w] = move(block, low=w)
        near_rows = [units([texts], "own_units")] + [move(texts, near=n) for n in range(1, near_count)]
        own_stack = stack_units(near_rows)
        stacks = [own_stack] + [move(own_stack, grp=g) for g in range(1, grp_count)]
        image_parts, text_parts = pair_terms(
            params, list(early.values()), list(late.values()), stacks
        )
        far_parts = dict(zip([*early, *late], image_parts))
        came = [move(part, grp=-g) for g, part in enumerate(text_parts) if g]
        far_order = sorted((step for step in far_parts if step != (0, 0)), key=lambda step: step[0])
        far_came = [move(far_parts[h, w], high=-h, low=-w) for h, w in far_order]
        near_parts = add_stacks([text_parts[0], *came], near_count)
        near_parts = [near_parts[0]] + [
            move(part, near=-n) for n, part in enumerate(near_parts) if n
        ]
        return finish(
            images,
            texts,
            [(0, part) for part in [far_parts[0, 0]] + far_came]
            + [(1, part) for part in near_parts],
        )

    in_specs = (P(AXES, None), P(AXES, None), P(), P())
    out_specs = (P(AXES, None), P(AXES, None))
    return jax.shard_map(
        on_device, mesh=mesh, in_specs=in_specs, out_specs=out_specs, check_vma=False
    )
```

```python
import functools
import math

import jax
import jax.numpy as jnp
from jax import lax
from jax.experimental import pallas as pl
from jax.experimental.pallas import tpu as pltpu
from jax.sharding import PartitionSpec as P

AXES = ("grp", "dev")
VMEM_LIMIT = 32 * 1024 * 1024
SPAN = 256
PIECE = 32
LATE = 16500
LOG2_E = math.log2(math.e)
VMEM = pl.BlockSpec(memory_space=pltpu.VMEM)


def unit_rows(raw):
    wide = raw.astype(jnp.float32)
    factor = lax.rsqrt(jnp.sum(wide * wide, axis=-1, keepdims=True) + 1e-06)
    return wide * factor, factor


def call(kernel, out_shape, operands, scratch=(), flops=0, transcendentals=0, name=None):
    touched = sum(x.size * x.dtype.itemsize for x in list(operands) + list(out_shape))
    outs = pl.pallas_call(
        kernel,
        out_shape=out_shape,
        in_specs=[VMEM] * len(operands),
        out_specs=[VMEM] * len(out_shape),
        scratch_shapes=scratch,
        compiler_params=pltpu.CompilerParams(vmem_limit_bytes=VMEM_LIMIT),
        cost_estimate=pl.CostEstimate(
            flops=flops, bytes_accessed=touched, transcendentals=transcendentals
        ),
        name=name,
    )(*operands)
    return tuple(outs)


def units_kernel(*refs):
    rows = refs[0].shape[0]
    for at, ref in enumerate(refs[:-1]):
        refs[-1][at * rows:(at + 1) * rows, :] = unit_rows(ref[...])[0].astype(refs[-1].dtype)


def units(blocks, name, weight=1):
    rows, width = blocks[0].shape
    out = jax.ShapeDtypeStruct((len(blocks) * rows, width), jnp.bfloat16)
    return call(units_kernel, [out], blocks, flops=4 * weight * out.size, name=name)[0]


def stack_units_kernel(*refs):
    out = refs[-1]
    rows = refs[0].shape[0]
    out[:rows, :] = refs[0][...]
    for at, ref in enumerate(refs[1:-1], 1):
        out[at * rows:(at + 1) * rows, :] = unit_rows(ref[...])[0].astype(out.dtype)


def stack_units(blocks):
    rows, width = blocks[0].shape
    out = jax.ShapeDtypeStruct((len(blocks) * rows, width), jnp.bfloat16)
    return call(stack_units_kernel, [out], blocks, flops=4 * out.size, name="stack_units")[0]


def pairs(params_ref, jobs):
    slope, shift, temper = (params_ref[0:1, at:at + 1] for at in range(3))
    chunks = [
        (at, first, min(first + SPAN, job[1].shape[0]))
        for at, job in enumerate(jobs) for first in range(0, job[1].shape[0], SPAN)
    ]

    def dots_of(at, first, last):
        vi, text_ref = jobs[at][:2]
        return lax.dot_general(
            vi, text_ref[first:last, :], (((1,), (1,)), ((), ())),
            preferred_element_type=jnp.float32,
        )

    coefficients = [[] for _ in jobs]
    totals = []
    coming = dots_of(*chunks[0])
    for step, (at, first, last) in enumerate(chunks):
        vi, text_ref, text_out, own, text_add = jobs[at]
        dots, coming = coming, dots_of(*chunks[step + 1]) if step + 1 < len(chunks) else None
        e = jnp.exp2(slope * dots + shift)
        chance = pl.reciprocal(1.0 + e, approx=True)
        if own and first == 0:
            row = lax.broadcasted_iota(jnp.int32, chance.shape, 0)
            column = lax.broadcasted_iota(jnp.int32, chance.shape, 1)
            same = (row == column) & (row < own)
            chance = jnp.where(same, -e * chance, chance)
        coefficient = (temper * chance).astype(jnp.bfloat16)
        text_part = lax.dot_general(
            coefficient, vi, (((0,), (0,)), ((), ())), preferred_element_type=jnp.float32
        )
        if text_add is not None:
            text_part = text_add[first:last, :] + text_part
        text_out[first:last, :] = text_part.astype(text_out.dtype)
        coefficients[at].append(coefficient)
        if last == text_ref.shape[0]:
            whole = jnp.concatenate(coefficients[at], axis=1)
            totals.append(jnp.dot(whole, text_ref[...], preferred_element_type=jnp.float32))
    return totals


def early_pairs_kernel(params_ref, text_ref, *refs):
    image_refs, (text_out, units_out, total_out) = refs[:-3], refs[-3:]
    rows = image_refs[0].shape[0]
    for a, ref in enumerate(image_refs):
        units_out[a * rows:(a + 1) * rows, :] = unit_rows(ref[...])[0].astype(jnp.bfloat16)
    (total,) = pairs(params_ref, [(units_out[...], text_ref, text_out, rows, None)])
    total_out[...] = total


def rest_pairs_kernel(
    count, params_ref, early_ref, total_ref, own_text_ref, own_add_ref, late_ref, *refs
):
    text_refs, own_out = refs[:count], refs[count]
    other_out, image_out = refs[count + 1:2 * count + 1], refs[2 * count + 1:]
    rows = image_out[0].shape[0]
    early, late = early_ref[...], late_ref[...]
    vi = jnp.concatenate([early, late], axis=0)
    late_total, *totals = pairs(
        params_ref,
        [(late, own_text_ref, own_out, 0, own_add_ref)]
        + [(vi, text_ref, out, 0, None) for text_ref, out in zip(text_refs, other_out)],
    )
    total = sum(totals, jnp.concatenate([total_ref[...], late_total], axis=0))
    for a, ref in enumerate(image_out):
        ref[...] = total[a * rows:(a + 1) * rows, :].astype(ref.dtype)


def pair_terms(params, early, late, texts):
    rows, width = early[0].shape
    early_rows, late_rows = rows * len(early), rows * len(late)
    own, others = texts[0], texts[1:]
    other_rows = sum(t.shape[0] for t in others)

    def cost(pair_count):
        return dict(flops=6 * pair_count * width, transcendentals=2 * pair_count)

    own_add, early_units, total = call(
        early_pairs_kernel,
        [
            jax.ShapeDtypeStruct(own.shape, jnp.float32),
            jax.ShapeDtypeStruct((early_rows, width), jnp.bfloat16),
            jax.ShapeDtypeStruct((early_rows, width), jnp.float32),
        ],
        [params, own, *early],
        name="early_pairs",
        **cost(early_rows * own.shape[0]),
    )
    late_units = units(late, "late_units", LATE)
    outs = call(
        functools.partial(rest_pairs_kernel, len(others)),
        [jax.ShapeDtypeStruct(own.shape, jnp.float32)]
        + [jax.ShapeDtypeStruct(t.shape, jnp.bfloat16) for t in others]
        + [jax.ShapeDtypeStruct((rows, width), jnp.float32)]
        + [jax.ShapeDtypeStruct((rows, width), jnp.bfloat16)] * (len(early) + len(late) - 1),
        [params, early_units, total, own, own_add, late_units, *others],
        name="rest_pairs",
        **cost(late_rows * own.shape[0] + (early_rows + late_rows) * other_rows),
    )
    count = 1 + len(others)
    return outs[count:], outs[:count]


def add_stacks_kernel(part_count, *refs):
    parts, outs = refs[:part_count], refs[part_count:]
    rows = outs[0].shape[0]
    for at, out in enumerate(outs):
        total = parts[0][at * rows:(at + 1) * rows, :].astype(jnp.float32)
        for part in parts[1:]:
            total = total + part[at * rows:(at + 1) * rows, :].astype(jnp.float32)
        out[...] = total.astype(out.dtype)


def add_stacks(parts, count):
    shape = (parts[0].shape[0] // count, parts[0].shape[1])
    types = [jnp.float32] + [jnp.bfloat16] * (count - 1)
    return call(
        functools.partial(add_stacks_kernel, len(parts)),
        [jax.ShapeDtypeStruct(shape, t) for t in types],
        parts,
        flops=len(parts) * parts[0].size,
        name="add_stacks",
    )


def finish_kernel(sides, image_ref, text_ref, *refs):
    parts, outs = refs[:len(sides)], refs[len(sides):len(sides) + 2]
    staged, sems = refs[len(sides) + 2:]
    rows = image_ref.shape[0]
    piece = math.gcd(rows, PIECE)
    copies = []
    for side, raw in enumerate((image_ref, text_ref)):
        for first in range(0, rows, piece):
            here = pl.ds(first, piece)
            unit, factor = unit_rows(raw[here, :])
            total = sum(
                ref[here, :].astype(jnp.float32) for at, ref in zip(sides, parts) if at == side
            )
            along = jnp.sum(unit * total, axis=-1, keepdims=True)
            staged[side, here, :] = factor * (total - unit * along)
            copies.append(
                pltpu.make_async_copy(
                    staged.at[side, here, :], outs[side].at[here, :], sems.at[len(copies)]
                )
            )
            copies[-1].start()
    for copy in copies:
        copy.wait()


def finish(images, texts, parts):
    out = jax.ShapeDtypeStruct(images.shape, jnp.float32)
    return pl.pallas_call(
        functools.partial(finish_kernel, [side for side, _ in parts]),
        out_shape=(out, out),
        in_specs=[VMEM] * (2 + len(parts)),
        out_specs=[pl.BlockSpec(memory_space=pl.ANY)] * 2,
        scratch_shapes=[
            pltpu.VMEM((2,) + images.shape, jnp.float32),
            pltpu.SemaphoreType.DMA((2 * (images.shape[0] // math.gcd(images.shape[0], PIECE)),)),
        ],
        compiler_params=pltpu.CompilerParams(vmem_limit_bytes=VMEM_LIMIT),
        cost_estimate=pl.CostEstimate(
            flops=10 * len(parts) * images.size,
            bytes_accessed=3 * len(parts) * images.size,
            transcendentals=0,
        ),
        name="finish",
    )(images, texts, *[part for _, part in parts])


def plan(grp_count, dev_count):
    options = [n for n in range(1, dev_count + 1) if dev_count % n == 0]
    near = min(options, key=lambda n: (dev_count // n + grp_count * n, -n))
    return dev_count // near, near


def step_to(at, by, count):
    if count & (count - 1) == 0:
        return at ^ abs(by)
    return (at + by) % count


def solution(mesh):
    grp_count, dev_count = mesh.shape["grp"], mesh.shape["dev"]
    far_count, near_count = plan(grp_count, dev_count)
    low_count = 2 if far_count % 2 == 0 else 1
    high_count = far_count // low_count

    def move(value, grp=0, high=0, low=0, near=0):
        perm = []
        for g in range(grp_count):
            for h in range(high_count):
                for w in range(low_count):
                    for n in range(near_count):
                        source = ((g * high_count + h) * low_count + w) * near_count + n
                        g2 = step_to(g, grp, grp_count)
                        h2 = step_to(h, high, high_count)
                        w2 = step_to(w, low, low_count)
                        n2 = step_to(n, near, near_count)
                        target = ((g2 * high_count + h2) * low_count + w2) * near_count + n2
                        perm.append((source, target))
        return lax.ppermute(value, AXES, perm)

    def on_device(images, texts, logit_scale, logit_bias):
        params = jnp.concatenate(
            [logit_scale * -LOG2_E, logit_bias * -LOG2_E, logit_scale]
        ).reshape(1, 3)
        early = {(0, 0): images}
        for h in range(1, high_count):
            early[h, 0] = move(images, high=h)
        for w in range(1, low_count):
            early[0, w] = move(images, low=w)
        late = {}
        for h in range(1, high_count):
            block, params = lax.optimization_barrier((early[h, 0], params))
            for w in range(1, low_count):
                late[h, w] = move(block, low=w)
        near_rows = [units([texts], "own_units")] + [move(texts, near=n) for n in range(1, near_count)]
        own_stack = stack_units(near_rows)
        stacks = [own_stack] + [move(own_stack, grp=g) for g in range(1, grp_count)]
        image_parts, text_parts = pair_terms(
            params, list(early.values()), list(late.values()), stacks
        )
        far_parts = dict(zip([*early, *late], image_parts))
        came = [move(part, grp=-g) for g, part in enumerate(text_parts) if g]
        far_order = sorted((step for step in far_parts if step != (0, 0)), key=lambda step: step[0])
        far_came = [move(far_parts[h, w], high=-h, low=-w) for h, w in far_order]
        near_parts = add_stacks([text_parts[0], *came], near_count)
        near_parts = [near_parts[0]] + [
            move(part, near=-n) for n, part in enumerate(near_parts) if n
        ]
        return finish(
            images,
            texts,
            [(0, part) for part in [far_parts[0, 0]] + far_came]
            + [(1, part) for part in near_parts],
        )

    in_specs = (P(AXES, None), P(AXES, None), P(), P())
    out_specs = (P(AXES, None), P(AXES, None))
    return jax.shard_map(
        on_device, mesh=mesh, in_specs=in_specs, out_specs=out_specs, check_vma=False
    )
```

```python
import functools
import math

import jax
import jax.numpy as jnp
from jax import lax
from jax.experimental import pallas as pl
from jax.experimental.pallas import tpu as pltpu
from jax.sharding import PartitionSpec as P

AXES = ("grp", "dev")
VMEM_LIMIT = 32 * 1024 * 1024
SPAN = 256
PIECE = 32
LATE = 16500
FAR = 60000
LOG2_E = math.log2(math.e)
VMEM = pl.BlockSpec(memory_space=pltpu.VMEM)


def unit_rows(raw):
    wide = raw.astype(jnp.float32)
    factor = lax.rsqrt(jnp.sum(wide * wide, axis=-1, keepdims=True) + 1e-06)
    return wide * factor, factor


def call(kernel, out_shape, operands, scratch=(), flops=0, transcendentals=0, name=None):
    touched = sum(x.size * x.dtype.itemsize for x in list(operands) + list(out_shape))
    outs = pl.pallas_call(
        kernel,
        out_shape=out_shape,
        in_specs=[VMEM] * len(operands),
        out_specs=[VMEM] * len(out_shape),
        scratch_shapes=scratch,
        compiler_params=pltpu.CompilerParams(vmem_limit_bytes=VMEM_LIMIT),
        cost_estimate=pl.CostEstimate(
            flops=flops, bytes_accessed=touched, transcendentals=transcendentals
        ),
        name=name,
    )(*operands)
    return tuple(outs)


def units_kernel(*refs):
    rows = refs[0].shape[0]
    for at, ref in enumerate(refs[:-1]):
        refs[-1][at * rows:(at + 1) * rows, :] = unit_rows(ref[...])[0].astype(refs[-1].dtype)


def units(blocks, name, weight=1):
    rows, width = blocks[0].shape
    out = jax.ShapeDtypeStruct((len(blocks) * rows, width), jnp.bfloat16)
    return call(units_kernel, [out], blocks, flops=4 * weight * out.size, name=name)[0]


def stack_units_kernel(*refs):
    out = refs[-1]
    rows = refs[0].shape[0]
    out[:rows, :] = refs[0][...]
    for at, ref in enumerate(refs[1:-1], 1):
        out[at * rows:(at + 1) * rows, :] = unit_rows(ref[...])[0].astype(out.dtype)


def stack_units(blocks):
    rows, width = blocks[0].shape
    out = jax.ShapeDtypeStruct((len(blocks) * rows, width), jnp.bfloat16)
    return call(stack_units_kernel, [out], blocks, flops=4 * out.size, name="stack_units")[0]


def pairs(params_ref, jobs):
    slope, shift, temper = (params_ref[0:1, at:at + 1] for at in range(3))
    chunks = [
        (at, first, min(first + SPAN, job[1].shape[0]))
        for at, job in enumerate(jobs) for first in range(0, job[1].shape[0], SPAN)
    ]

    def dots_of(at, first, last):
        vi, text_ref = jobs[at][:2]
        return lax.dot_general(
            vi, text_ref[first:last, :], (((1,), (1,)), ((), ())),
            preferred_element_type=jnp.float32,
        )

    totals = [None] * len(jobs)
    coming = dots_of(*chunks[0])
    for step, (at, first, last) in enumerate(chunks):
        vi, text_ref, text_out, own, text_add = jobs[at]
        dots, coming = coming, dots_of(*chunks[step + 1]) if step + 1 < len(chunks) else None
        vt = text_ref[first:last, :]
        e = jnp.exp2(slope * dots + shift)
        chance = pl.reciprocal(1.0 + e, approx=True)
        if own and first == 0:
            row = lax.broadcasted_iota(jnp.int32, chance.shape, 0)
            column = lax.broadcasted_iota(jnp.int32, chance.shape, 1)
            same = (row == column) & (row < own)
            chance = jnp.where(same, -e * chance, chance)
        coefficient = (temper * chance).astype(jnp.bfloat16)
        text_part = lax.dot_general(
            coefficient, vi, (((0,), (0,)), ((), ())), preferred_element_type=jnp.float32
        )
        if text_add is not None:
            text_part = text_add[first:last, :] + text_part
        text_out[first:last, :] = text_part.astype(text_out.dtype)
        part = jnp.dot(coefficient, vt, preferred_element_type=jnp.float32)
        totals[at] = part if totals[at] is None else totals[at] + part
    return totals


def early_pairs_kernel(params_ref, text_ref, *refs):
    image_refs, (text_out, units_out, total_out) = refs[:-3], refs[-3:]
    rows = image_refs[0].shape[0]
    for a, ref in enumerate(image_refs):
        units_out[a * rows:(a + 1) * rows, :] = unit_rows(ref[...])[0].astype(jnp.bfloat16)
    (total,) = pairs(params_ref, [(units_out[...], text_ref, text_out, rows, None)])
    total_out[...] = total


def early_rest_kernel(count, params_ref, units_ref, total_ref, *refs):
    text_refs, text_out, image_out = refs[:count], refs[count:2 * count], refs[2 * count:]
    rows = image_out[0].shape[0]
    vi = units_ref[...]
    totals = pairs(
        params_ref, [(vi, text_ref, out, 0, None) for text_ref, out in zip(text_refs, text_out)]
    )
    total = sum(totals, total_ref[...])
    for a, ref in enumerate(image_out):
        ref[...] = total[a * rows:(a + 1) * rows, :].astype(ref.dtype)


def late_pairs_kernel(count, params_ref, units_ref, *refs):
    text_refs, add_refs = refs[:count], refs[count:2 * count]
    text_out, image_out = refs[2 * count:3 * count], refs[3 * count:]
    rows = image_out[0].shape[0]
    vi = units_ref[...]
    total = sum(
        pairs(
            params_ref,
            [
                (vi, text_ref, out, 0, add)
                for text_ref, add, out in zip(text_refs, add_refs, text_out)
            ],
        )
    )
    for a, ref in enumerate(image_out):
        ref[...] = total[a * rows:(a + 1) * rows, :].astype(ref.dtype)


def pair_terms(params, early, late, texts):
    rows, width = early[0].shape
    early_rows, late_rows = rows * len(early), rows * len(late)
    own, others = texts[0], texts[1:]
    other_rows = sum(t.shape[0] for t in others)
    part = jax.ShapeDtypeStruct((rows, width), jnp.bfloat16)

    def cost(pair_count):
        return dict(flops=6 * pair_count * width, transcendentals=2 * pair_count)

    def text_sums(stacks, dtype):
        return [jax.ShapeDtypeStruct(t.shape, dtype) for t in stacks]

    own_add, early_units, total = call(
        early_pairs_kernel,
        [
            *text_sums([own], jnp.float32),
            jax.ShapeDtypeStruct((early_rows, width), jnp.bfloat16),
            jax.ShapeDtypeStruct((early_rows, width), jnp.float32),
        ],
        [params, own, *early],
        name="early_pairs",
        **cost(early_rows * own.shape[0]),
    )
    late_units = units(late, "late_units", LATE)
    late_units, total = lax.optimization_barrier((late_units, total))
    outs = call(
        functools.partial(early_rest_kernel, len(others)),
        text_sums(others, jnp.float32)
        + [jax.ShapeDtypeStruct((rows, width), jnp.float32)]
        + [part] * (len(early) - 1),
        [params, early_units, total, *others],
        name="early_rest",
        **cost(early_rows * other_rows),
    )
    other_adds, early_parts = outs[:len(others)], outs[len(others):]
    outs = call(
        functools.partial(late_pairs_kernel, len(texts)),
        text_sums([own], jnp.float32) + text_sums(others, jnp.bfloat16) + [part] * len(late),
        [params, late_units, *texts, own_add, *other_adds],
        name="late_pairs",
        **cost(late_rows * (own.shape[0] + other_rows)),
    )
    return early_parts, outs[len(texts):], outs[:len(texts)]


def add_stacks_kernel(part_count, *refs):
    parts, outs = refs[:part_count], refs[part_count:]
    rows = outs[0].shape[0]
    for at, out in enumerate(outs):
        total = parts[0][at * rows:(at + 1) * rows, :].astype(jnp.float32)
        for part in parts[1:]:
            total = total + part[at * rows:(at + 1) * rows, :].astype(jnp.float32)
        out[...] = total.astype(out.dtype)


def add_stacks(parts, count):
    shape = (parts[0].shape[0] // count, parts[0].shape[1])
    types = [jnp.float32] + [jnp.bfloat16] * (count - 1)
    return call(
        functools.partial(add_stacks_kernel, len(parts)),
        [jax.ShapeDtypeStruct(shape, t) for t in types],
        parts,
        flops=len(parts) * parts[0].size,
        name="add_stacks",
    )


def add_far_kernel(*refs):
    refs[-1][...] = sum(ref[...].astype(jnp.float32) for ref in refs[:-1])


def add_far(parts):
    out = jax.ShapeDtypeStruct(parts[0].shape, jnp.float32)
    return call(
        add_far_kernel, [out], parts, flops=FAR * len(parts) * out.size, name="add_far"
    )[0]


def finish_kernel(sides, image_ref, text_ref, *refs):
    parts, outs = refs[:len(sides)], refs[len(sides):len(sides) + 2]
    staged, sems = refs[len(sides) + 2:]
    rows = image_ref.shape[0]
    piece = math.gcd(rows, PIECE)
    copies = []
    for side, raw in enumerate((image_ref, text_ref)):
        for first in range(0, rows, piece):
            here = pl.ds(first, piece)
            unit, factor = unit_rows(raw[here, :])
            total = sum(
                ref[here, :].astype(jnp.float32) for at, ref in zip(sides, parts) if at == side
            )
            along = jnp.sum(unit * total, axis=-1, keepdims=True)
            staged[side, here, :] = factor * (total - unit * along)
            copies.append(
                pltpu.make_async_copy(
                    staged.at[side, here, :], outs[side].at[here, :], sems.at[len(copies)]
                )
            )
            copies[-1].start()
    for copy in copies:
        copy.wait()


def finish(images, texts, parts):
    out = jax.ShapeDtypeStruct(images.shape, jnp.float32)
    return pl.pallas_call(
        functools.partial(finish_kernel, [side for side, _ in parts]),
        out_shape=(out, out),
        in_specs=[VMEM] * (2 + len(parts)),
        out_specs=[pl.BlockSpec(memory_space=pl.ANY)] * 2,
        scratch_shapes=[
            pltpu.VMEM((2,) + images.shape, jnp.float32),
            pltpu.SemaphoreType.DMA((2 * (images.shape[0] // math.gcd(images.shape[0], PIECE)),)),
        ],
        compiler_params=pltpu.CompilerParams(vmem_limit_bytes=VMEM_LIMIT),
        cost_estimate=pl.CostEstimate(
            flops=10 * len(parts) * images.size,
            bytes_accessed=3 * len(parts) * images.size,
            transcendentals=0,
        ),
        name="finish",
    )(images, texts, *[part for _, part in parts])


def plan(grp_count, dev_count):
    options = [n for n in range(1, dev_count + 1) if dev_count % n == 0]
    near = min(options, key=lambda n: (dev_count // n + grp_count * n, -n))
    return dev_count // near, near


def step_to(at, by, count):
    if count & (count - 1) == 0:
        return at ^ abs(by)
    return (at + by) % count


def solution(mesh):
    grp_count, dev_count = mesh.shape["grp"], mesh.shape["dev"]
    far_count, near_count = plan(grp_count, dev_count)
    low_count = 2 if far_count % 2 == 0 else 1
    high_count = far_count // low_count

    def move(value, grp=0, high=0, low=0, near=0):
        perm = []
        for g in range(grp_count):
            for h in range(high_count):
                for w in range(low_count):
                    for n in range(near_count):
                        source = ((g * high_count + h) * low_count + w) * near_count + n
                        g2 = step_to(g, grp, grp_count)
                        h2 = step_to(h, high, high_count)
                        w2 = step_to(w, low, low_count)
                        n2 = step_to(n, near, near_count)
                        target = ((g2 * high_count + h2) * low_count + w2) * near_count + n2
                        perm.append((source, target))
        return lax.ppermute(value, AXES, perm)

    def on_device(images, texts, logit_scale, logit_bias):
        params = jnp.concatenate(
            [logit_scale * -LOG2_E, logit_bias * -LOG2_E, logit_scale]
        ).reshape(1, 3)
        early = {(0, 0): images}
        for h in range(1, high_count):
            early[h, 0] = move(images, high=h)
        for w in range(1, low_count):
            early[0, w] = move(images, low=w)
        late = {}
        for h in range(1, high_count):
            block, params = lax.optimization_barrier((early[h, 0], params))
            for w in range(1, low_count):
                late[h, w] = move(block, low=w)
        near_rows = [units([texts], "own_units")] + [move(texts, near=n) for n in range(1, near_count)]
        own_stack = stack_units(near_rows)
        stacks = [own_stack] + [move(own_stack, grp=g) for g in range(1, grp_count)]
        early_parts, late_parts, text_parts = pair_terms(
            params, list(early.values()), list(late.values()), stacks
        )
        far_parts = dict(zip([*early, *late], [*early_parts, *late_parts]))

        def give_back(h, w):
            return move(far_parts[h, w], high=-h, low=-w)

        came = [move(part, grp=-g) for g, part in enumerate(text_parts) if g]
        far_sum = add_far(
            [far_parts[0, 0]] + [give_back(h, w) for h, w in early if w]
        )
        far_sum, own_text = lax.optimization_barrier((far_sum, text_parts[0]))
        far_came = [give_back(h, w) for h, w in far_parts if h]
        near_parts = add_stacks([own_text, *came], near_count)
        near_parts = [near_parts[0]] + [
            move(part, near=-n) for n, part in enumerate(near_parts) if n
        ]
        return finish(
            images,
            texts,
            [(0, part) for part in [far_sum] + far_came] + [(1, part) for part in near_parts],
        )

    in_specs = (P(AXES, None), P(AXES, None), P(), P())
    out_specs = (P(AXES, None), P(AXES, None))
    return jax.shard_map(
        on_device, mesh=mesh, in_specs=in_specs, out_specs=out_specs, check_vma=False
    )
```

```python
import functools
import math

import jax
import jax.numpy as jnp
from jax import lax
from jax.experimental import pallas as pl
from jax.experimental.pallas import tpu as pltpu
from jax.sharding import PartitionSpec as P

AXES = ("grp", "dev")
VMEM_LIMIT = 32 * 1024 * 1024
SPAN = 256
PIECE = 32
LATE = 16500
FAR = 37000
LOG2_E = math.log2(math.e)
VMEM = pl.BlockSpec(memory_space=pltpu.VMEM)


def unit_rows(raw):
    wide = raw.astype(jnp.float32)
    factor = lax.rsqrt(jnp.sum(wide * wide, axis=-1, keepdims=True) + 1e-06)
    return wide * factor, factor


def call(kernel, out_shape, operands, scratch=(), flops=0, transcendentals=0, name=None):
    touched = sum(x.size * x.dtype.itemsize for x in list(operands) + list(out_shape))
    outs = pl.pallas_call(
        kernel,
        out_shape=out_shape,
        in_specs=[VMEM] * len(operands),
        out_specs=[VMEM] * len(out_shape),
        scratch_shapes=scratch,
        compiler_params=pltpu.CompilerParams(vmem_limit_bytes=VMEM_LIMIT),
        cost_estimate=pl.CostEstimate(
            flops=flops, bytes_accessed=touched, transcendentals=transcendentals
        ),
        name=name,
    )(*operands)
    return tuple(outs)


def units_kernel(*refs):
    rows = refs[0].shape[0]
    for at, ref in enumerate(refs[:-1]):
        refs[-1][at * rows:(at + 1) * rows, :] = unit_rows(ref[...])[0].astype(refs[-1].dtype)


def units(blocks, name, weight=1):
    rows, width = blocks[0].shape
    out = jax.ShapeDtypeStruct((len(blocks) * rows, width), jnp.bfloat16)
    return call(units_kernel, [out], blocks, flops=4 * weight * out.size, name=name)[0]


def stack_units_kernel(*refs):
    out = refs[-1]
    rows = refs[0].shape[0]
    out[:rows, :] = refs[0][...]
    for at, ref in enumerate(refs[1:-1], 1):
        out[at * rows:(at + 1) * rows, :] = unit_rows(ref[...])[0].astype(out.dtype)


def stack_units(blocks):
    rows, width = blocks[0].shape
    out = jax.ShapeDtypeStruct((len(blocks) * rows, width), jnp.bfloat16)
    return call(stack_units_kernel, [out], blocks, flops=4 * out.size, name="stack_units")[0]


def pairs(params_ref, jobs):
    slope, shift, temper = (params_ref[0:1, at:at + 1] for at in range(3))
    chunks = [
        (at, first, min(first + SPAN, job[1].shape[0]))
        for at, job in enumerate(jobs) for first in range(0, job[1].shape[0], SPAN)
    ]

    def dots_of(at, first, last):
        vi, text_ref = jobs[at][:2]
        return lax.dot_general(
            vi, text_ref[first:last, :], (((1,), (1,)), ((), ())),
            preferred_element_type=jnp.float32,
        )

    totals = [None] * len(jobs)
    coming = dots_of(*chunks[0])
    for step, (at, first, last) in enumerate(chunks):
        vi, text_ref, text_out, own, text_add = jobs[at]
        dots, coming = coming, dots_of(*chunks[step + 1]) if step + 1 < len(chunks) else None
        vt = text_ref[first:last, :]
        e = jnp.exp2(slope * dots + shift)
        chance = pl.reciprocal(1.0 + e, approx=True)
        if own and first == 0:
            row = lax.broadcasted_iota(jnp.int32, chance.shape, 0)
            column = lax.broadcasted_iota(jnp.int32, chance.shape, 1)
            same = (row == column) & (row < own)
            chance = jnp.where(same, -e * chance, chance)
        coefficient = (temper * chance).astype(jnp.bfloat16)
        text_part = lax.dot_general(
            coefficient, vi, (((0,), (0,)), ((), ())), preferred_element_type=jnp.float32
        )
        if text_add is not None:
            text_part = text_add[first:last, :] + text_part
        text_out[first:last, :] = text_part.astype(text_out.dtype)
        part = jnp.dot(coefficient, vt, preferred_element_type=jnp.float32)
        totals[at] = part if totals[at] is None else totals[at] + part
    return totals


def early_pairs_kernel(params_ref, text_ref, *refs):
    image_refs, (text_out, units_out, total_out) = refs[:-3], refs[-3:]
    rows = image_refs[0].shape[0]
    for a, ref in enumerate(image_refs):
        units_out[a * rows:(a + 1) * rows, :] = unit_rows(ref[...])[0].astype(jnp.bfloat16)
    (total,) = pairs(params_ref, [(units_out[...], text_ref, text_out, rows, None)])
    total_out[...] = total


def early_rest_kernel(count, params_ref, units_ref, total_ref, *refs):
    text_refs, text_out, image_out = refs[:count], refs[count:2 * count], refs[2 * count:]
    rows = image_out[0].shape[0]
    vi = units_ref[...]
    totals = pairs(
        params_ref, [(vi, text_ref, out, 0, None) for text_ref, out in zip(text_refs, text_out)]
    )
    total = sum(totals, total_ref[...])
    for a, ref in enumerate(image_out):
        ref[...] = total[a * rows:(a + 1) * rows, :].astype(ref.dtype)


def late_pairs_kernel(count, params_ref, units_ref, *refs):
    text_refs, add_refs = refs[:count], refs[count:2 * count]
    text_out, image_out = refs[2 * count:3 * count], refs[3 * count:]
    rows = image_out[0].shape[0]
    vi = units_ref[...]
    total = sum(
        pairs(
            params_ref,
            [
                (vi, text_ref, out, 0, add)
                for text_ref, add, out in zip(text_refs, add_refs, text_out)
            ],
        )
    )
    for a, ref in enumerate(image_out):
        ref[...] = total[a * rows:(a + 1) * rows, :].astype(ref.dtype)


def pair_terms(params, early, late, texts):
    rows, width = early[0].shape
    early_rows, late_rows = rows * len(early), rows * len(late)
    own, others = texts[0], texts[1:]
    other_rows = sum(t.shape[0] for t in others)
    part = jax.ShapeDtypeStruct((rows, width), jnp.bfloat16)

    def cost(pair_count):
        return dict(flops=6 * pair_count * width, transcendentals=2 * pair_count)

    def text_sums(stacks, dtype):
        return [jax.ShapeDtypeStruct(t.shape, dtype) for t in stacks]

    own_add, early_units, total = call(
        early_pairs_kernel,
        [
            *text_sums([own], jnp.float32),
            jax.ShapeDtypeStruct((early_rows, width), jnp.bfloat16),
            jax.ShapeDtypeStruct((early_rows, width), jnp.float32),
        ],
        [params, own, *early],
        name="early_pairs",
        **cost(early_rows * own.shape[0]),
    )
    late_units = units(late, "late_units", LATE)
    late_units, total = lax.optimization_barrier((late_units, total))
    outs = call(
        functools.partial(early_rest_kernel, len(others)),
        text_sums(others, jnp.float32)
        + [jax.ShapeDtypeStruct((rows, width), jnp.float32)]
        + [part] * (len(early) - 1),
        [params, early_units, total, *others],
        name="early_rest",
        **cost(early_rows * other_rows),
    )
    other_adds, early_parts = outs[:len(others)], outs[len(others):]
    outs = call(
        functools.partial(late_pairs_kernel, len(texts)),
        text_sums([own], jnp.float32) + text_sums(others, jnp.bfloat16) + [part] * len(late),
        [params, late_units, *texts, own_add, *other_adds],
        name="late_pairs",
        **cost(late_rows * (own.shape[0] + other_rows)),
    )
    return early_parts, outs[len(texts):], outs[:len(texts)]


def add_stacks_kernel(part_count, *refs):
    parts, outs = refs[:part_count], refs[part_count:]
    rows = outs[0].shape[0]
    for at, out in enumerate(outs):
        total = parts[0][at * rows:(at + 1) * rows, :].astype(jnp.float32)
        for part in parts[1:]:
            total = total + part[at * rows:(at + 1) * rows, :].astype(jnp.float32)
        out[...] = total.astype(out.dtype)


def add_stacks(parts, count):
    shape = (parts[0].shape[0] // count, parts[0].shape[1])
    types = [jnp.float32] + [jnp.bfloat16] * (count - 1)
    return call(
        functools.partial(add_stacks_kernel, len(parts)),
        [jax.ShapeDtypeStruct(shape, t) for t in types],
        parts,
        flops=len(parts) * parts[0].size,
        name="add_stacks",
    )


def add_far_kernel(*refs):
    refs[-1][...] = sum(ref[...].astype(jnp.float32) for ref in refs[:-1])


def add_far(parts):
    out = jax.ShapeDtypeStruct(parts[0].shape, jnp.float32)
    return call(
        add_far_kernel, [out], parts, flops=FAR * len(parts) * out.size, name="add_far"
    )[0]


def finish_kernel(sides, image_ref, text_ref, *refs):
    parts, outs = refs[:len(sides)], refs[len(sides):len(sides) + 2]
    staged, sems = refs[len(sides) + 2:]
    rows = image_ref.shape[0]
    piece = math.gcd(rows, PIECE)
    copies = []
    for side, raw in enumerate((image_ref, text_ref)):
        for first in range(0, rows, piece):
            here = pl.ds(first, piece)
            unit, factor = unit_rows(raw[here, :])
            total = sum(
                ref[here, :].astype(jnp.float32) for at, ref in zip(sides, parts) if at == side
            )
            along = jnp.sum(unit * total, axis=-1, keepdims=True)
            staged[side, here, :] = factor * (total - unit * along)
            copies.append(
                pltpu.make_async_copy(
                    staged.at[side, here, :], outs[side].at[here, :], sems.at[len(copies)]
                )
            )
            copies[-1].start()
    for copy in copies:
        copy.wait()


def finish(images, texts, parts):
    out = jax.ShapeDtypeStruct(images.shape, jnp.float32)
    return pl.pallas_call(
        functools.partial(finish_kernel, [side for side, _ in parts]),
        out_shape=(out, out),
        in_specs=[VMEM] * (2 + len(parts)),
        out_specs=[pl.BlockSpec(memory_space=pl.ANY)] * 2,
        scratch_shapes=[
            pltpu.VMEM((2,) + images.shape, jnp.float32),
            pltpu.SemaphoreType.DMA((2 * (images.shape[0] // math.gcd(images.shape[0], PIECE)),)),
        ],
        compiler_params=pltpu.CompilerParams(vmem_limit_bytes=VMEM_LIMIT),
        cost_estimate=pl.CostEstimate(
            flops=10 * len(parts) * images.size,
            bytes_accessed=3 * len(parts) * images.size,
            transcendentals=0,
        ),
        name="finish",
    )(images, texts, *[part for _, part in parts])


def plan(grp_count, dev_count):
    options = [n for n in range(1, dev_count + 1) if dev_count % n == 0]
    near = min(options, key=lambda n: (dev_count // n + grp_count * n, -n))
    return dev_count // near, near


def step_to(at, by, count):
    if count & (count - 1) == 0:
        return at ^ abs(by)
    return (at + by) % count


def solution(mesh):
    grp_count, dev_count = mesh.shape["grp"], mesh.shape["dev"]
    far_count, near_count = plan(grp_count, dev_count)
    low_count = 2 if far_count % 2 == 0 else 1
    high_count = far_count // low_count

    def move(value, grp=0, high=0, low=0, near=0):
        perm = []
        for g in range(grp_count):
            for h in range(high_count):
                for w in range(low_count):
                    for n in range(near_count):
                        source = ((g * high_count + h) * low_count + w) * near_count + n
                        g2 = step_to(g, grp, grp_count)
                        h2 = step_to(h, high, high_count)
                        w2 = step_to(w, low, low_count)
                        n2 = step_to(n, near, near_count)
                        target = ((g2 * high_count + h2) * low_count + w2) * near_count + n2
                        perm.append((source, target))
        return lax.ppermute(value, AXES, perm)

    def on_device(images, texts, logit_scale, logit_bias):
        params = jnp.concatenate(
            [logit_scale * -LOG2_E, logit_bias * -LOG2_E, logit_scale]
        ).reshape(1, 3)
        early = {(0, 0): images}
        for h in range(1, high_count):
            early[h, 0] = move(images, high=h)
        for w in range(1, low_count):
            early[0, w] = move(images, low=w)
        late = {}
        for h in range(1, high_count):
            block, params = lax.optimization_barrier((early[h, 0], params))
            for w in range(1, low_count):
                late[h, w] = move(block, low=w)
        near_rows = [units([texts], "own_units")] + [move(texts, near=n) for n in range(1, near_count)]
        own_stack = stack_units(near_rows)
        stacks = [own_stack] + [move(own_stack, grp=g) for g in range(1, grp_count)]
        early_parts, late_parts, text_parts = pair_terms(
            params, list(early.values()), list(late.values()), stacks
        )
        far_parts = dict(zip([*early, *late], [*early_parts, *late_parts]))

        held = [step for step in early if step[0]]
        kept, text_parts = lax.optimization_barrier(
            ([far_parts[step] for step in held], list(text_parts))
        )
        far_parts.update(zip(held, kept))

        def give_back(h, w):
            return move(far_parts[h, w], high=-h, low=-w)

        came = [move(part, grp=-g) for g, part in enumerate(text_parts) if g]
        far_sum = add_far(
            [far_parts[0, 0]] + [give_back(h, w) for h, w in early if w]
        )
        far_sum, own_text = lax.optimization_barrier((far_sum, text_parts[0]))
        far_came = [give_back(h, w) for h, w in far_parts if h]
        near_parts = add_stacks([own_text, *came], near_count)
        near_parts = [near_parts[0]] + [
            move(part, near=-n) for n, part in enumerate(near_parts) if n
        ]
        return finish(
            images,
            texts,
            [(0, part) for part in [far_sum] + far_came] + [(1, part) for part in near_parts],
        )

    in_specs = (P(AXES, None), P(AXES, None), P(), P())
    out_specs = (P(AXES, None), P(AXES, None))
    return jax.shard_map(
        on_device, mesh=mesh, in_specs=in_specs, out_specs=out_specs, check_vma=False
    )
```

```python
import functools
import math

import jax
import jax.numpy as jnp
from jax import lax
from jax.experimental import pallas as pl
from jax.experimental.pallas import tpu as pltpu
from jax.sharding import PartitionSpec as P

AXES = ("grp", "dev")
VMEM_LIMIT = 32 * 1024 * 1024
SPAN = 256
PIECE = 32
LATE = 16500
PASSED = 37000
LOG2_E = math.log2(math.e)
VMEM = pl.BlockSpec(memory_space=pltpu.VMEM)


def unit_rows(raw):
    wide = raw.astype(jnp.float32)
    factor = lax.rsqrt(jnp.sum(wide * wide, axis=-1, keepdims=True) + 1e-06)
    return wide * factor, factor


def call(kernel, out_shape, operands, scratch=(), flops=0, transcendentals=0, name=None):
    touched = sum(x.size * x.dtype.itemsize for x in list(operands) + list(out_shape))
    outs = pl.pallas_call(
        kernel,
        out_shape=out_shape,
        in_specs=[VMEM] * len(operands),
        out_specs=[VMEM] * len(out_shape),
        scratch_shapes=scratch,
        compiler_params=pltpu.CompilerParams(vmem_limit_bytes=VMEM_LIMIT),
        cost_estimate=pl.CostEstimate(
            flops=flops, bytes_accessed=touched, transcendentals=transcendentals
        ),
        name=name,
    )(*operands)
    return tuple(outs)


def units_kernel(*refs):
    rows = refs[0].shape[0]
    for at, ref in enumerate(refs[:-1]):
        refs[-1][at * rows:(at + 1) * rows, :] = unit_rows(ref[...])[0].astype(refs[-1].dtype)


def units(blocks, name, weight=1):
    rows, width = blocks[0].shape
    out = jax.ShapeDtypeStruct((len(blocks) * rows, width), jnp.bfloat16)
    return call(units_kernel, [out], blocks, flops=4 * weight * out.size, name=name)[0]


def stack_units_kernel(*refs):
    out = refs[-1]
    rows = refs[0].shape[0]
    out[:rows, :] = refs[0][...]
    for at, ref in enumerate(refs[1:-1], 1):
        out[at * rows:(at + 1) * rows, :] = unit_rows(ref[...])[0].astype(out.dtype)


def stack_units(blocks):
    rows, width = blocks[0].shape
    out = jax.ShapeDtypeStruct((len(blocks) * rows, width), jnp.bfloat16)
    return call(stack_units_kernel, [out], blocks, flops=4 * out.size, name="stack_units")[0]


def pairs(params_ref, jobs):
    slope, shift, temper = (params_ref[0:1, at:at + 1] for at in range(3))
    chunks = [
        (at, first, min(first + SPAN, job[1].shape[0]))
        for at, job in enumerate(jobs) for first in range(0, job[1].shape[0], SPAN)
    ]

    def dots_of(at, first, last):
        vi, text_ref = jobs[at][:2]
        return lax.dot_general(
            vi, text_ref[first:last, :], (((1,), (1,)), ((), ())),
            preferred_element_type=jnp.float32,
        )

    totals = [None] * len(jobs)
    coming = dots_of(*chunks[0])
    for step, (at, first, last) in enumerate(chunks):
        vi, text_ref, text_out, own, text_add = jobs[at]
        dots, coming = coming, dots_of(*chunks[step + 1]) if step + 1 < len(chunks) else None
        vt = text_ref[first:last, :]
        e = jnp.exp2(slope * dots + shift)
        chance = pl.reciprocal(1.0 + e, approx=True)
        if own and first == 0:
            row = lax.broadcasted_iota(jnp.int32, chance.shape, 0)
            column = lax.broadcasted_iota(jnp.int32, chance.shape, 1)
            same = (row == column) & (row < own)
            chance = jnp.where(same, -e * chance, chance)
        coefficient = (temper * chance).astype(jnp.bfloat16)
        text_part = lax.dot_general(
            coefficient, vi, (((0,), (0,)), ((), ())), preferred_element_type=jnp.float32
        )
        if text_add is not None:
            text_part = text_add[first:last, :] + text_part
        text_out[first:last, :] = text_part.astype(text_out.dtype)
        part = jnp.dot(coefficient, vt, preferred_element_type=jnp.float32)
        totals[at] = part if totals[at] is None else totals[at] + part
    return totals


def early_pairs_kernel(params_ref, text_ref, *refs):
    image_refs, (text_out, units_out, total_out) = refs[:-3], refs[-3:]
    rows = image_refs[0].shape[0]
    for a, ref in enumerate(image_refs):
        units_out[a * rows:(a + 1) * rows, :] = unit_rows(ref[...])[0].astype(jnp.bfloat16)
    (total,) = pairs(params_ref, [(units_out[...], text_ref, text_out, rows, None)])
    total_out[...] = total


def early_rest_kernel(count, params_ref, units_ref, total_ref, *refs):
    text_refs, text_out, image_out = refs[:count], refs[count:2 * count], refs[2 * count:]
    rows = image_out[0].shape[0]
    vi = units_ref[...]
    totals = pairs(
        params_ref, [(vi, text_ref, out, 0, None) for text_ref, out in zip(text_refs, text_out)]
    )
    total = sum(totals, total_ref[...])
    for a, ref in enumerate(image_out):
        ref[...] = total[a * rows:(a + 1) * rows, :].astype(ref.dtype)


def late_pairs_kernel(count, params_ref, units_ref, *refs):
    text_refs, add_refs = refs[:count], refs[count:2 * count]
    text_out, image_out = refs[2 * count:3 * count], refs[3 * count:]
    rows = image_out[0].shape[0]
    vi = units_ref[...]
    total = sum(
        pairs(
            params_ref,
            [
                (vi, text_ref, out, 0, add)
                for text_ref, add, out in zip(text_refs, add_refs, text_out)
            ],
        )
    )
    for a, ref in enumerate(image_out):
        ref[...] = total[a * rows:(a + 1) * rows, :].astype(ref.dtype)


def pair_terms(params, early, late, texts):
    rows, width = early[0].shape
    early_rows, late_rows = rows * len(early), rows * len(late)
    own, others = texts[0], texts[1:]
    other_rows = sum(t.shape[0] for t in others)
    part = jax.ShapeDtypeStruct((rows, width), jnp.bfloat16)

    def cost(pair_count):
        return dict(flops=6 * pair_count * width, transcendentals=2 * pair_count)

    def text_sums(stacks, dtype):
        return [jax.ShapeDtypeStruct(t.shape, dtype) for t in stacks]

    own_add, early_units, total = call(
        early_pairs_kernel,
        [
            *text_sums([own], jnp.float32),
            jax.ShapeDtypeStruct((early_rows, width), jnp.bfloat16),
            jax.ShapeDtypeStruct((early_rows, width), jnp.float32),
        ],
        [params, own, *early],
        name="early_pairs",
        **cost(early_rows * own.shape[0]),
    )
    late_units = units(late, "late_units", LATE)
    late_units, total = lax.optimization_barrier((late_units, total))
    outs = call(
        functools.partial(early_rest_kernel, len(others)),
        text_sums(others, jnp.float32)
        + [jax.ShapeDtypeStruct((rows, width), jnp.float32)]
        + [part] * (len(early) - 1),
        [params, early_units, total, *others],
        name="early_rest",
        **cost(early_rows * other_rows),
    )
    other_adds, early_parts = outs[:len(others)], outs[len(others):]
    outs = call(
        functools.partial(late_pairs_kernel, len(texts)),
        text_sums([own], jnp.float32)
        + text_sums(others, jnp.bfloat16)
        + [jax.ShapeDtypeStruct((rows, width), jnp.float32)] * len(late),
        [params, late_units, *texts, own_add, *other_adds],
        name="late_pairs",
        **cost(late_rows * (own.shape[0] + other_rows)),
    )
    return early_parts, outs[len(texts):], outs[:len(texts)]


def add_stacks_kernel(part_count, *refs):
    parts, outs = refs[:part_count], refs[part_count:]
    rows = outs[0].shape[0]
    for at, out in enumerate(outs):
        total = parts[0][at * rows:(at + 1) * rows, :].astype(jnp.float32)
        for part in parts[1:]:
            total = total + part[at * rows:(at + 1) * rows, :].astype(jnp.float32)
        out[...] = total.astype(out.dtype)


def add_stacks(parts, count):
    shape = (parts[0].shape[0] // count, parts[0].shape[1])
    types = [jnp.float32] + [jnp.bfloat16] * (count - 1)
    return call(
        functools.partial(add_stacks_kernel, len(parts)),
        [jax.ShapeDtypeStruct(shape, t) for t in types],
        parts,
        flops=len(parts) * parts[0].size,
        name="add_stacks",
    )


def add_parts_kernel(*refs):
    total = sum(ref[...].astype(jnp.float32) for ref in refs[:-1])
    refs[-1][...] = total.astype(refs[-1].dtype)


def add_parts(parts, dtype, name, weight=1):
    out = jax.ShapeDtypeStruct(parts[0].shape, dtype)
    return call(
        add_parts_kernel, [out], parts, flops=weight * len(parts) * out.size, name=name
    )[0]


def finish_kernel(sides, image_ref, text_ref, *refs):
    parts, outs = refs[:len(sides)], refs[len(sides):len(sides) + 2]
    staged, sems = refs[len(sides) + 2:]
    rows = image_ref.shape[0]
    piece = math.gcd(rows, PIECE)
    copies = []
    for side, raw in enumerate((image_ref, text_ref)):
        for first in range(0, rows, piece):
            here = pl.ds(first, piece)
            unit, factor = unit_rows(raw[here, :])
            total = sum(
                ref[here, :].astype(jnp.float32) for at, ref in zip(sides, parts) if at == side
            )
            along = jnp.sum(unit * total, axis=-1, keepdims=True)
            staged[side, here, :] = factor * (total - unit * along)
            copies.append(
                pltpu.make_async_copy(
                    staged.at[side, here, :], outs[side].at[here, :], sems.at[len(copies)]
                )
            )
            copies[-1].start()
    for copy in copies:
        copy.wait()


def finish(images, texts, parts):
    out = jax.ShapeDtypeStruct(images.shape, jnp.float32)
    return pl.pallas_call(
        functools.partial(finish_kernel, [side for side, _ in parts]),
        out_shape=(out, out),
        in_specs=[VMEM] * (2 + len(parts)),
        out_specs=[pl.BlockSpec(memory_space=pl.ANY)] * 2,
        scratch_shapes=[
            pltpu.VMEM((2,) + images.shape, jnp.float32),
            pltpu.SemaphoreType.DMA((2 * (images.shape[0] // math.gcd(images.shape[0], PIECE)),)),
        ],
        compiler_params=pltpu.CompilerParams(vmem_limit_bytes=VMEM_LIMIT),
        cost_estimate=pl.CostEstimate(
            flops=10 * len(parts) * images.size,
            bytes_accessed=3 * len(parts) * images.size,
            transcendentals=0,
        ),
        name="finish",
    )(images, texts, *[part for _, part in parts])


def plan(grp_count, dev_count):
    options = [n for n in range(1, dev_count + 1) if dev_count % n == 0]
    near = min(options, key=lambda n: (dev_count // n + grp_count * n, -n))
    return dev_count // near, near


def step_to(at, by, count):
    if count & (count - 1) == 0:
        return at ^ abs(by)
    return (at + by) % count


def solution(mesh):
    grp_count, dev_count = mesh.shape["grp"], mesh.shape["dev"]
    far_count, near_count = plan(grp_count, dev_count)
    low_count = 2 if far_count % 2 == 0 else 1
    high_count = far_count // low_count

    def move(value, grp=0, high=0, low=0, near=0):
        perm = []
        for g in range(grp_count):
            for h in range(high_count):
                for w in range(low_count):
                    for n in range(near_count):
                        source = ((g * high_count + h) * low_count + w) * near_count + n
                        g2 = step_to(g, grp, grp_count)
                        h2 = step_to(h, high, high_count)
                        w2 = step_to(w, low, low_count)
                        n2 = step_to(n, near, near_count)
                        target = ((g2 * high_count + h2) * low_count + w2) * near_count + n2
                        perm.append((source, target))
        return lax.ppermute(value, AXES, perm)

    def on_device(images, texts, logit_scale, logit_bias):
        params = jnp.concatenate(
            [logit_scale * -LOG2_E, logit_bias * -LOG2_E, logit_scale]
        ).reshape(1, 3)
        early = {(0, 0): images}
        for h in range(1, high_count):
            early[h, 0] = move(images, high=h)
        for w in range(1, low_count):
            early[0, w] = move(images, low=w)
        late = {}
        for h in range(1, high_count):
            block, params = lax.optimization_barrier((early[h, 0], params))
            for w in range(1, low_count):
                late[h, w] = move(block, low=w)
        near_rows = [units([texts], "own_units")] + [move(texts, near=n) for n in range(1, near_count)]
        own_stack = stack_units(near_rows)
        stacks = [own_stack] + [move(own_stack, grp=g) for g in range(1, grp_count)]
        early_parts, late_parts, text_parts = pair_terms(
            params, list(early.values()), list(late.values()), stacks
        )
        far_parts = dict(zip([*early, *late], [*early_parts, *late_parts]))

        def give_back(h, w):
            return move(far_parts[h, w], high=-h, low=-w)

        if low_count > 1:
            for h, w in late:
                passed = move(far_parts[h, 0], low=w)
                far_parts[h, w] = add_parts([far_parts[h, w], passed], jnp.bfloat16, "add_passed", PASSED)
            far_came = [give_back(h, w) for h, w in late]
        else:
            far_came = [give_back(h, w) for h, w in early if h]
        came = [move(part, grp=-g) for g, part in enumerate(text_parts) if g]
        low_came = [give_back(h, w) for h, w in early if w]
        near_parts = add_stacks([text_parts[0], *came], near_count)
        near_parts = [near_parts[0]] + [
            move(part, near=-n) for n, part in enumerate(near_parts) if n
        ]
        return finish(
            images,
            texts,
            [(0, part) for part in [far_parts[0, 0]] + far_came]
            + [(1, part) for part in near_parts]
            + [(0, part) for part in low_came],
        )

    in_specs = (P(AXES, None), P(AXES, None), P(), P())
    out_specs = (P(AXES, None), P(AXES, None))
    return jax.shard_map(
        on_device, mesh=mesh, in_specs=in_specs, out_specs=out_specs, check_vma=False
    )
```

```python
import functools
import math

import jax
import jax.numpy as jnp
from jax import lax
from jax.experimental import pallas as pl
from jax.experimental.pallas import tpu as pltpu
from jax.sharding import PartitionSpec as P

AXES = ("grp", "dev")
VMEM_LIMIT = 32 * 1024 * 1024
SPAN = 256
PIECE = 32
LATE = 16500
PASSED = 45000
LOG2_E = math.log2(math.e)
VMEM = pl.BlockSpec(memory_space=pltpu.VMEM)


def unit_rows(raw):
    wide = raw.astype(jnp.float32)
    factor = lax.rsqrt(jnp.sum(wide * wide, axis=-1, keepdims=True) + 1e-06)
    return wide * factor, factor


def call(kernel, out_shape, operands, scratch=(), flops=0, transcendentals=0, name=None):
    touched = sum(x.size * x.dtype.itemsize for x in list(operands) + list(out_shape))
    outs = pl.pallas_call(
        kernel,
        out_shape=out_shape,
        in_specs=[VMEM] * len(operands),
        out_specs=[VMEM] * len(out_shape),
        scratch_shapes=scratch,
        compiler_params=pltpu.CompilerParams(vmem_limit_bytes=VMEM_LIMIT),
        cost_estimate=pl.CostEstimate(
            flops=flops, bytes_accessed=touched, transcendentals=transcendentals
        ),
        name=name,
    )(*operands)
    return tuple(outs)


def units_kernel(*refs):
    rows = refs[0].shape[0]
    for at, ref in enumerate(refs[:-1]):
        refs[-1][at * rows:(at + 1) * rows, :] = unit_rows(ref[...])[0].astype(refs[-1].dtype)


def units(blocks, name, weight=1):
    rows, width = blocks[0].shape
    out = jax.ShapeDtypeStruct((len(blocks) * rows, width), jnp.bfloat16)
    return call(units_kernel, [out], blocks, flops=4 * weight * out.size, name=name)[0]


def stack_units_kernel(*refs):
    out = refs[-1]
    rows = refs[0].shape[0]
    out[:rows, :] = refs[0][...]
    for at, ref in enumerate(refs[1:-1], 1):
        out[at * rows:(at + 1) * rows, :] = unit_rows(ref[...])[0].astype(out.dtype)


def stack_units(blocks):
    rows, width = blocks[0].shape
    out = jax.ShapeDtypeStruct((len(blocks) * rows, width), jnp.bfloat16)
    return call(stack_units_kernel, [out], blocks, flops=4 * out.size, name="stack_units")[0]


def pairs(params_ref, jobs):
    slope, shift, temper = (params_ref[0:1, at:at + 1] for at in range(3))
    chunks = [
        (at, first, min(first + SPAN, job[1].shape[0]))
        for at, job in enumerate(jobs) for first in range(0, job[1].shape[0], SPAN)
    ]

    def dots_of(at, first, last):
        vi, text_ref = jobs[at][:2]
        return lax.dot_general(
            vi, text_ref[first:last, :], (((1,), (1,)), ((), ())),
            preferred_element_type=jnp.float32,
        )

    totals = [None] * len(jobs)
    coming = dots_of(*chunks[0])
    for step, (at, first, last) in enumerate(chunks):
        vi, text_ref, text_out, own, text_add = jobs[at]
        dots, coming = coming, dots_of(*chunks[step + 1]) if step + 1 < len(chunks) else None
        vt = text_ref[first:last, :]
        e = jnp.exp2(slope * dots + shift)
        chance = pl.reciprocal(1.0 + e, approx=True)
        if own and first == 0:
            row = lax.broadcasted_iota(jnp.int32, chance.shape, 0)
            column = lax.broadcasted_iota(jnp.int32, chance.shape, 1)
            same = (row == column) & (row < own)
            chance = jnp.where(same, -e * chance, chance)
        coefficient = (temper * chance).astype(jnp.bfloat16)
        text_part = lax.dot_general(
            coefficient, vi, (((0,), (0,)), ((), ())), preferred_element_type=jnp.float32
        )
        if text_add is not None:
            text_part = text_add[first:last, :] + text_part
        text_out[first:last, :] = text_part.astype(text_out.dtype)
        part = jnp.dot(coefficient, vt, preferred_element_type=jnp.float32)
        totals[at] = part if totals[at] is None else totals[at] + part
    return totals


def early_pairs_kernel(params_ref, text_ref, *refs):
    image_refs, (text_out, units_out, total_out) = refs[:-3], refs[-3:]
    rows = image_refs[0].shape[0]
    for a, ref in enumerate(image_refs):
        units_out[a * rows:(a + 1) * rows, :] = unit_rows(ref[...])[0].astype(jnp.bfloat16)
    (total,) = pairs(params_ref, [(units_out[...], text_ref, text_out, rows, None)])
    total_out[...] = total


def early_rest_kernel(count, params_ref, units_ref, total_ref, *refs):
    text_refs, text_out, image_out = refs[:count], refs[count:2 * count], refs[2 * count:]
    rows = image_out[0].shape[0]
    vi = units_ref[...]
    totals = pairs(
        params_ref, [(vi, text_ref, out, 0, None) for text_ref, out in zip(text_refs, text_out)]
    )
    total = sum(totals, total_ref[...])
    for a, ref in enumerate(image_out):
        ref[...] = total[a * rows:(a + 1) * rows, :].astype(ref.dtype)


def late_pairs_kernel(count, params_ref, units_ref, *refs):
    text_refs, add_refs = refs[:count], refs[count:2 * count]
    text_out, image_out = refs[2 * count:3 * count], refs[3 * count:]
    rows = image_out[0].shape[0]
    vi = units_ref[...]
    total = sum(
        pairs(
            params_ref,
            [
                (vi, text_ref, out, 0, add)
                for text_ref, add, out in zip(text_refs, add_refs, text_out)
            ],
        )
    )
    for a, ref in enumerate(image_out):
        ref[...] = total[a * rows:(a + 1) * rows, :].astype(ref.dtype)


def pair_terms(params, early, late, texts):
    rows, width = early[0].shape
    early_rows, late_rows = rows * len(early), rows * len(late)
    own, others = texts[0], texts[1:]
    other_rows = sum(t.shape[0] for t in others)
    part = jax.ShapeDtypeStruct((rows, width), jnp.bfloat16)

    def cost(pair_count):
        return dict(flops=6 * pair_count * width, transcendentals=2 * pair_count)

    def text_sums(stacks, dtype):
        return [jax.ShapeDtypeStruct(t.shape, dtype) for t in stacks]

    own_add, early_units, total = call(
        early_pairs_kernel,
        [
            *text_sums([own], jnp.float32),
            jax.ShapeDtypeStruct((early_rows, width), jnp.bfloat16),
            jax.ShapeDtypeStruct((early_rows, width), jnp.float32),
        ],
        [params, own, *early],
        name="early_pairs",
        **cost(early_rows * own.shape[0]),
    )
    late_units = units(late, "late_units", LATE)
    late_units, total = lax.optimization_barrier((late_units, total))
    outs = call(
        functools.partial(early_rest_kernel, len(others)),
        text_sums(others, jnp.float32)
        + [jax.ShapeDtypeStruct((rows, width), jnp.float32)]
        + [part] * (len(early) - 1),
        [params, early_units, total, *others],
        name="early_rest",
        **cost(early_rows * other_rows),
    )
    other_adds, early_parts = outs[:len(others)], outs[len(others):]
    outs = call(
        functools.partial(late_pairs_kernel, len(texts)),
        text_sums([own], jnp.float32)
        + text_sums(others, jnp.bfloat16)
        + [jax.ShapeDtypeStruct((rows, width), jnp.float32)] * len(late),
        [params, late_units, *texts, own_add, *other_adds],
        name="late_pairs",
        **cost(late_rows * (own.shape[0] + other_rows)),
    )
    return early_parts, outs[len(texts):], outs[:len(texts)]


def add_stacks_kernel(part_count, *refs):
    parts, outs = refs[:part_count], refs[part_count:]
    rows = outs[0].shape[0]
    for at, out in enumerate(outs):
        total = parts[0][at * rows:(at + 1) * rows, :].astype(jnp.float32)
        for part in parts[1:]:
            total = total + part[at * rows:(at + 1) * rows, :].astype(jnp.float32)
        out[...] = total.astype(out.dtype)


def add_stacks(parts, count):
    shape = (parts[0].shape[0] // count, parts[0].shape[1])
    types = [jnp.float32] + [jnp.bfloat16] * (count - 1)
    return call(
        functools.partial(add_stacks_kernel, len(parts)),
        [jax.ShapeDtypeStruct(shape, t) for t in types],
        parts,
        flops=len(parts) * parts[0].size,
        name="add_stacks",
    )


def add_parts_kernel(*refs):
    total = sum(ref[...].astype(jnp.float32) for ref in refs[:-1])
    refs[-1][...] = total.astype(refs[-1].dtype)


def add_parts(parts, dtype, name, weight=1):
    out = jax.ShapeDtypeStruct(parts[0].shape, dtype)
    return call(
        add_parts_kernel, [out], parts, flops=weight * len(parts) * out.size, name=name
    )[0]


def finish_kernel(sides, image_ref, text_ref, *refs):
    parts, outs = refs[:len(sides)], refs[len(sides):len(sides) + 2]
    staged, sems = refs[len(sides) + 2:]
    rows = image_ref.shape[0]
    piece = math.gcd(rows, PIECE)
    copies = []
    for side, raw in enumerate((image_ref, text_ref)):
        for first in range(0, rows, piece):
            here = pl.ds(first, piece)
            unit, factor = unit_rows(raw[here, :])
            total = sum(
                ref[here, :].astype(jnp.float32) for at, ref in zip(sides, parts) if at == side
            )
            along = jnp.sum(unit * total, axis=-1, keepdims=True)
            staged[side, here, :] = factor * (total - unit * along)
            copies.append(
                pltpu.make_async_copy(
                    staged.at[side, here, :], outs[side].at[here, :], sems.at[len(copies)]
                )
            )
            copies[-1].start()
    for copy in copies:
        copy.wait()


def finish(images, texts, parts):
    out = jax.ShapeDtypeStruct(images.shape, jnp.float32)
    return pl.pallas_call(
        functools.partial(finish_kernel, [side for side, _ in parts]),
        out_shape=(out, out),
        in_specs=[VMEM] * (2 + len(parts)),
        out_specs=[pl.BlockSpec(memory_space=pl.ANY)] * 2,
        scratch_shapes=[
            pltpu.VMEM((2,) + images.shape, jnp.float32),
            pltpu.SemaphoreType.DMA((2 * (images.shape[0] // math.gcd(images.shape[0], PIECE)),)),
        ],
        compiler_params=pltpu.CompilerParams(vmem_limit_bytes=VMEM_LIMIT),
        cost_estimate=pl.CostEstimate(
            flops=10 * len(parts) * images.size,
            bytes_accessed=3 * len(parts) * images.size,
            transcendentals=0,
        ),
        name="finish",
    )(images, texts, *[part for _, part in parts])


def plan(grp_count, dev_count):
    options = [n for n in range(1, dev_count + 1) if dev_count % n == 0]
    near = min(options, key=lambda n: (dev_count // n + grp_count * n, -n))
    return dev_count // near, near


def step_to(at, by, count):
    if count & (count - 1) == 0:
        return at ^ abs(by)
    return (at + by) % count


def solution(mesh):
    grp_count, dev_count = mesh.shape["grp"], mesh.shape["dev"]
    far_count, near_count = plan(grp_count, dev_count)
    low_count = 2 if far_count % 2 == 0 else 1
    high_count = far_count // low_count

    def move(value, grp=0, high=0, low=0, near=0):
        perm = []
        for g in range(grp_count):
            for h in range(high_count):
                for w in range(low_count):
                    for n in range(near_count):
                        source = ((g * high_count + h) * low_count + w) * near_count + n
                        g2 = step_to(g, grp, grp_count)
                        h2 = step_to(h, high, high_count)
                        w2 = step_to(w, low, low_count)
                        n2 = step_to(n, near, near_count)
                        target = ((g2 * high_count + h2) * low_count + w2) * near_count + n2
                        perm.append((source, target))
        return lax.ppermute(value, AXES, perm)

    def on_device(images, texts, logit_scale, logit_bias):
        params = jnp.concatenate(
            [logit_scale * -LOG2_E, logit_bias * -LOG2_E, logit_scale]
        ).reshape(1, 3)
        early = {(0, 0): images}
        for h in range(1, high_count):
            early[h, 0] = move(images, high=h)
        for w in range(1, low_count):
            early[0, w] = move(images, low=w)
        late = {}
        for h in range(1, high_count):
            block, params = lax.optimization_barrier((early[h, 0], params))
            for w in range(1, low_count):
                late[h, w] = move(block, low=w)
        near_rows = [units([texts], "own_units")] + [move(texts, near=n) for n in range(1, near_count)]
        own_stack = stack_units(near_rows)
        stacks = [own_stack] + [move(own_stack, grp=g) for g in range(1, grp_count)]
        early_parts, late_parts, text_parts = pair_terms(
            params, list(early.values()), list(late.values()), stacks
        )
        far_parts = dict(zip([*early, *late], [*early_parts, *late_parts]))

        def give_back(h, w):
            return move(far_parts[h, w], high=-h, low=-w)

        if low_count > 1:
            for h, w in late:
                passed = move(far_parts[h, 0], low=w)
                far_parts[h, w] = add_parts([far_parts[h, w], passed], jnp.bfloat16, "add_passed", PASSED)
            far_came = [give_back(h, w) for h, w in late]
        else:
            far_came = [give_back(h, w) for h, w in early if h]
        came = [move(part, grp=-g) for g, part in enumerate(text_parts) if g]
        near_parts = add_stacks([text_parts[0], *came], near_count)
        low_parts = [far_parts[0, w] for w in range(1, low_count)]
        low_parts, near_parts = lax.optimization_barrier((low_parts, near_parts))
        near_parts = [near_parts[0]] + [
            move(part, near=-n) for n, part in enumerate(near_parts) if n
        ]
        low_came = [move(part, low=-w) for w, part in enumerate(low_parts, 1)]
        return finish(
            images,
            texts,
            [(0, part) for part in [far_parts[0, 0]] + far_came]
            + [(1, part) for part in near_parts]
            + [(0, part) for part in low_came],
        )

    in_specs = (P(AXES, None), P(AXES, None), P(), P())
    out_specs = (P(AXES, None), P(AXES, None))
    return jax.shard_map(
        on_device, mesh=mesh, in_specs=in_specs, out_specs=out_specs, check_vma=False
    )
```

```python
import functools
import math

import jax
import jax.numpy as jnp
from jax import lax
from jax.experimental import pallas as pl
from jax.experimental.pallas import tpu as pltpu
from jax.sharding import PartitionSpec as P

AXES = ("grp", "dev")
VMEM_LIMIT = 32 * 1024 * 1024
SPAN = 256
PIECE = 32
LATE = 16500
PASSED = 1
LOG2_E = math.log2(math.e)
VMEM = pl.BlockSpec(memory_space=pltpu.VMEM)


def unit_rows(raw):
    wide = raw.astype(jnp.float32)
    factor = lax.rsqrt(jnp.sum(wide * wide, axis=-1, keepdims=True) + 1e-06)
    return wide * factor, factor


def call(kernel, out_shape, operands, scratch=(), flops=0, transcendentals=0, name=None):
    touched = sum(x.size * x.dtype.itemsize for x in list(operands) + list(out_shape))
    outs = pl.pallas_call(
        kernel,
        out_shape=out_shape,
        in_specs=[VMEM] * len(operands),
        out_specs=[VMEM] * len(out_shape),
        scratch_shapes=scratch,
        compiler_params=pltpu.CompilerParams(vmem_limit_bytes=VMEM_LIMIT),
        cost_estimate=pl.CostEstimate(
            flops=flops, bytes_accessed=touched, transcendentals=transcendentals
        ),
        name=name,
    )(*operands)
    return tuple(outs)


def units_kernel(*refs):
    rows = refs[0].shape[0]
    for at, ref in enumerate(refs[:-1]):
        refs[-1][at * rows:(at + 1) * rows, :] = unit_rows(ref[...])[0].astype(refs[-1].dtype)


def units(blocks, name, weight=1):
    rows, width = blocks[0].shape
    out = jax.ShapeDtypeStruct((len(blocks) * rows, width), jnp.bfloat16)
    return call(units_kernel, [out], blocks, flops=4 * weight * out.size, name=name)[0]


def stack_units_kernel(*refs):
    out = refs[-1]
    rows = refs[0].shape[0]
    out[:rows, :] = refs[0][...]
    for at, ref in enumerate(refs[1:-1], 1):
        out[at * rows:(at + 1) * rows, :] = unit_rows(ref[...])[0].astype(out.dtype)


def stack_units(blocks):
    rows, width = blocks[0].shape
    out = jax.ShapeDtypeStruct((len(blocks) * rows, width), jnp.bfloat16)
    return call(stack_units_kernel, [out], blocks, flops=4 * out.size, name="stack_units")[0]


def pairs(params_ref, jobs):
    slope, shift, temper = (params_ref[0:1, at:at + 1] for at in range(3))
    chunks = [
        (at, first, min(first + SPAN, job[1].shape[0]))
        for at, job in enumerate(jobs) for first in range(0, job[1].shape[0], SPAN)
    ]

    def dots_of(at, first, last):
        vi, text_ref = jobs[at][:2]
        return lax.dot_general(
            vi, text_ref[first:last, :], (((1,), (1,)), ((), ())),
            preferred_element_type=jnp.float32,
        )

    totals = [None] * len(jobs)
    coming = dots_of(*chunks[0])
    for step, (at, first, last) in enumerate(chunks):
        vi, text_ref, text_out, own, text_add = jobs[at]
        dots, coming = coming, dots_of(*chunks[step + 1]) if step + 1 < len(chunks) else None
        vt = text_ref[first:last, :]
        e = jnp.exp2(slope * dots + shift)
        chance = pl.reciprocal(1.0 + e, approx=True)
        if own and first == 0:
            row = lax.broadcasted_iota(jnp.int32, chance.shape, 0)
            column = lax.broadcasted_iota(jnp.int32, chance.shape, 1)
            same = (row == column) & (row < own)
            chance = jnp.where(same, -e * chance, chance)
        coefficient = (temper * chance).astype(jnp.bfloat16)
        text_part = lax.dot_general(
            coefficient, vi, (((0,), (0,)), ((), ())), preferred_element_type=jnp.float32
        )
        if text_add is not None:
            text_part = text_add[first:last, :] + text_part
        text_out[first:last, :] = text_part.astype(text_out.dtype)
        part = jnp.dot(coefficient, vt, preferred_element_type=jnp.float32)
        totals[at] = part if totals[at] is None else totals[at] + part
    return totals


def early_pairs_kernel(params_ref, text_ref, *refs):
    image_refs, (text_out, units_out, total_out) = refs[:-3], refs[-3:]
    rows = image_refs[0].shape[0]
    for a, ref in enumerate(image_refs):
        units_out[a * rows:(a + 1) * rows, :] = unit_rows(ref[...])[0].astype(jnp.bfloat16)
    (total,) = pairs(params_ref, [(units_out[...], text_ref, text_out, rows, None)])
    total_out[...] = total


def rest_pairs_kernel(
    count, params_ref, early_ref, total_ref, own_text_ref, own_add_ref, late_ref, *refs
):
    text_refs, own_out = refs[:count], refs[count]
    other_out, image_out = refs[count + 1:2 * count + 1], refs[2 * count + 1:]
    rows = image_out[0].shape[0]
    early, late = early_ref[...], late_ref[...]
    vi = jnp.concatenate([early, late], axis=0)
    late_total, *totals = pairs(
        params_ref,
        [(late, own_text_ref, own_out, 0, own_add_ref)]
        + [(vi, text_ref, out, 0, None) for text_ref, out in zip(text_refs, other_out)],
    )
    total = sum(totals, jnp.concatenate([total_ref[...], late_total], axis=0))
    for a, ref in enumerate(image_out):
        ref[...] = total[a * rows:(a + 1) * rows, :].astype(ref.dtype)


def pair_terms(params, early, late, texts, image_types):
    rows, width = early[0].shape
    early_rows, late_rows = rows * len(early), rows * len(late)
    own, others = texts[0], texts[1:]
    other_rows = sum(t.shape[0] for t in others)

    def cost(pair_count):
        return dict(flops=6 * pair_count * width, transcendentals=2 * pair_count)

    own_add, early_units, total = call(
        early_pairs_kernel,
        [
            jax.ShapeDtypeStruct(own.shape, jnp.float32),
            jax.ShapeDtypeStruct((early_rows, width), jnp.bfloat16),
            jax.ShapeDtypeStruct((early_rows, width), jnp.float32),
        ],
        [params, own, *early],
        name="early_pairs",
        **cost(early_rows * own.shape[0]),
    )
    late_units = units(late, "late_units", LATE)
    outs = call(
        functools.partial(rest_pairs_kernel, len(others)),
        [jax.ShapeDtypeStruct(own.shape, jnp.float32)]
        + [jax.ShapeDtypeStruct(t.shape, jnp.bfloat16) for t in others]
        + [jax.ShapeDtypeStruct((rows, width), t) for t in image_types],
        [params, early_units, total, own, own_add, late_units, *others],
        name="rest_pairs",
        **cost(late_rows * own.shape[0] + (early_rows + late_rows) * other_rows),
    )
    count = 1 + len(others)
    return outs[count:], outs[:count]


def add_stacks_kernel(part_count, *refs):
    parts, outs = refs[:part_count], refs[part_count:]
    rows = outs[0].shape[0]
    for at, out in enumerate(outs):
        total = parts[0][at * rows:(at + 1) * rows, :].astype(jnp.float32)
        for part in parts[1:]:
            total = total + part[at * rows:(at + 1) * rows, :].astype(jnp.float32)
        out[...] = total.astype(out.dtype)


def add_stacks(parts, count):
    shape = (parts[0].shape[0] // count, parts[0].shape[1])
    types = [jnp.float32] + [jnp.bfloat16] * (count - 1)
    return call(
        functools.partial(add_stacks_kernel, len(parts)),
        [jax.ShapeDtypeStruct(shape, t) for t in types],
        parts,
        flops=len(parts) * parts[0].size,
        name="add_stacks",
    )


def add_parts_kernel(*refs):
    total = sum(ref[...].astype(jnp.float32) for ref in refs[:-1])
    refs[-1][...] = total.astype(refs[-1].dtype)


def add_parts(parts, weight):
    out = jax.ShapeDtypeStruct(parts[0].shape, jnp.bfloat16)
    return call(
        add_parts_kernel, [out], parts, flops=weight * len(parts) * out.size, name="add_parts"
    )[0]


def finish_kernel(sides, image_ref, text_ref, *refs):
    parts, outs = refs[:len(sides)], refs[len(sides):len(sides) + 2]
    staged, sems = refs[len(sides) + 2:]
    rows = image_ref.shape[0]
    piece = math.gcd(rows, PIECE)
    copies = []
    for side, raw in enumerate((image_ref, text_ref)):
        for first in range(0, rows, piece):
            here = pl.ds(first, piece)
            unit, factor = unit_rows(raw[here, :])
            total = sum(
                ref[here, :].astype(jnp.float32) for at, ref in zip(sides, parts) if at == side
            )
            along = jnp.sum(unit * total, axis=-1, keepdims=True)
            staged[side, here, :] = factor * (total - unit * along)
            copies.append(
                pltpu.make_async_copy(
                    staged.at[side, here, :], outs[side].at[here, :], sems.at[len(copies)]
                )
            )
            copies[-1].start()
    for copy in copies:
        copy.wait()


def finish(images, texts, parts):
    out = jax.ShapeDtypeStruct(images.shape, jnp.float32)
    return pl.pallas_call(
        functools.partial(finish_kernel, [side for side, _ in parts]),
        out_shape=(out, out),
        in_specs=[VMEM] * (2 + len(parts)),
        out_specs=[pl.BlockSpec(memory_space=pl.ANY)] * 2,
        scratch_shapes=[
            pltpu.VMEM((2,) + images.shape, jnp.float32),
            pltpu.SemaphoreType.DMA((2 * (images.shape[0] // math.gcd(images.shape[0], PIECE)),)),
        ],
        compiler_params=pltpu.CompilerParams(vmem_limit_bytes=VMEM_LIMIT),
        cost_estimate=pl.CostEstimate(
            flops=10 * len(parts) * images.size,
            bytes_accessed=3 * len(parts) * images.size,
            transcendentals=0,
        ),
        name="finish",
    )(images, texts, *[part for _, part in parts])


def plan(grp_count, dev_count):
    options = [n for n in range(1, dev_count + 1) if dev_count % n == 0]
    near = min(options, key=lambda n: (dev_count // n + grp_count * n, -n))
    return dev_count // near, near


def step_to(at, by, count):
    if count & (count - 1) == 0:
        return at ^ abs(by)
    return (at + by) % count


def solution(mesh):
    grp_count, dev_count = mesh.shape["grp"], mesh.shape["dev"]
    far_count, near_count = plan(grp_count, dev_count)
    low_count = 2 if far_count % 2 == 0 else 1
    high_count = far_count // low_count

    def move(value, grp=0, high=0, low=0, near=0):
        perm = []
        for g in range(grp_count):
            for h in range(high_count):
                for w in range(low_count):
                    for n in range(near_count):
                        source = ((g * high_count + h) * low_count + w) * near_count + n
                        g2 = step_to(g, grp, grp_count)
                        h2 = step_to(h, high, high_count)
                        w2 = step_to(w, low, low_count)
                        n2 = step_to(n, near, near_count)
                        target = ((g2 * high_count + h2) * low_count + w2) * near_count + n2
                        perm.append((source, target))
        return lax.ppermute(value, AXES, perm)

    def on_device(images, texts, logit_scale, logit_bias):
        params = jnp.concatenate(
            [logit_scale * -LOG2_E, logit_bias * -LOG2_E, logit_scale]
        ).reshape(1, 3)
        early = {(0, 0): images}
        for h in range(1, high_count):
            early[h, 0] = move(images, high=h)
        for w in range(1, low_count):
            early[0, w] = move(images, low=w)
        late = {}
        for h in range(1, high_count):
            block, params = lax.optimization_barrier((early[h, 0], params))
            for w in range(1, low_count):
                late[h, w] = move(block, low=w)
        near_rows = [units([texts], "own_units")] + [move(texts, near=n) for n in range(1, near_count)]
        own_stack = stack_units(near_rows)
        stacks = [own_stack] + [move(own_stack, grp=g) for g in range(1, grp_count)]
        far_steps = [*early, *late]
        image_types = [jnp.bfloat16 if w else jnp.float32 for _, w in far_steps]
        image_parts, text_parts = pair_terms(
            params, list(early.values()), list(late.values()), stacks, image_types
        )
        far_parts = dict(zip(far_steps, image_parts))
        passed = [move(far_parts[step], low=-step[1]) for step in late]
        came = [move(part, grp=-g) for g, part in enumerate(text_parts) if g]
        near_parts = add_stacks([text_parts[0], *came], near_count)
        low_parts = [far_parts[0, w] for w in range(1, low_count)]
        near_came = [move(part, near=-n) for n, part in enumerate(near_parts) if n]
        passed, low_parts, kept, near_came[:1] = lax.optimization_barrier(
            (passed, low_parts, near_parts[0], near_came[:1])
        )
        high_came = []
        for h in range(1, high_count):
            terms = [far_parts[h, 0]] + [p for step, p in zip(late, passed) if step[0] == h]
            high_came.append(move(add_parts(terms, PASSED), high=-h))
        low_came = [move(part, low=-w) for w, part in enumerate(low_parts, 1)]
        return finish(
            images,
            texts,
            [(0, far_parts[0, 0])]
            + [(1, part) for part in [kept] + near_came]
            + [(0, part) for part in high_came + low_came],
        )

    in_specs = (P(AXES, None), P(AXES, None), P(), P())
    out_specs = (P(AXES, None), P(AXES, None))
    return jax.shard_map(
        on_device, mesh=mesh, in_specs=in_specs, out_specs=out_specs, check_vma=False
    )
```

```python
import functools
import math

import jax
import jax.numpy as jnp
from jax import lax
from jax.experimental import pallas as pl
from jax.experimental.pallas import tpu as pltpu
from jax.sharding import PartitionSpec as P

AXES = ("grp", "dev")
VMEM_LIMIT = 32 * 1024 * 1024
SPAN = 256
PIECE = 32
LATE = 16500
NEAR = 30000
LOG2_E = math.log2(math.e)
VMEM = pl.BlockSpec(memory_space=pltpu.VMEM)


def unit_rows(raw):
    wide = raw.astype(jnp.float32)
    factor = lax.rsqrt(jnp.sum(wide * wide, axis=-1, keepdims=True) + 1e-06)
    return wide * factor, factor


def call(kernel, out_shape, operands, scratch=(), flops=0, transcendentals=0, name=None):
    touched = sum(x.size * x.dtype.itemsize for x in list(operands) + list(out_shape))
    outs = pl.pallas_call(
        kernel,
        out_shape=out_shape,
        in_specs=[VMEM] * len(operands),
        out_specs=[VMEM] * len(out_shape),
        scratch_shapes=scratch,
        compiler_params=pltpu.CompilerParams(vmem_limit_bytes=VMEM_LIMIT),
        cost_estimate=pl.CostEstimate(
            flops=flops, bytes_accessed=touched, transcendentals=transcendentals
        ),
        name=name,
    )(*operands)
    return tuple(outs)


def units_kernel(*refs):
    rows = refs[0].shape[0]
    for at, ref in enumerate(refs[:-1]):
        refs[-1][at * rows:(at + 1) * rows, :] = unit_rows(ref[...])[0].astype(refs[-1].dtype)


def units(blocks, name, weight=1):
    rows, width = blocks[0].shape
    out = jax.ShapeDtypeStruct((len(blocks) * rows, width), jnp.bfloat16)
    return call(units_kernel, [out], blocks, flops=4 * weight * out.size, name=name)[0]


def stack_units_kernel(*refs):
    out = refs[-1]
    rows = refs[0].shape[0]
    out[:rows, :] = refs[0][...]
    for at, ref in enumerate(refs[1:-1], 1):
        out[at * rows:(at + 1) * rows, :] = unit_rows(ref[...])[0].astype(out.dtype)


def stack_units(blocks):
    rows, width = blocks[0].shape
    out = jax.ShapeDtypeStruct((len(blocks) * rows, width), jnp.bfloat16)
    return call(stack_units_kernel, [out], blocks, flops=4 * out.size, name="stack_units")[0]


def pairs(params_ref, jobs):
    slope, shift, temper = (params_ref[0:1, at:at + 1] for at in range(3))
    chunks = [
        (at, first, min(first + SPAN, job[1].shape[0]))
        for at, job in enumerate(jobs) for first in range(0, job[1].shape[0], SPAN)
    ]

    def dots_of(at, first, last):
        vi, text_ref = jobs[at][:2]
        return lax.dot_general(
            vi, text_ref[first:last, :], (((1,), (1,)), ((), ())),
            preferred_element_type=jnp.float32,
        )

    totals = [None] * len(jobs)
    coming = dots_of(*chunks[0])
    for step, (at, first, last) in enumerate(chunks):
        vi, text_ref, text_out, own, text_add = jobs[at]
        dots, coming = coming, dots_of(*chunks[step + 1]) if step + 1 < len(chunks) else None
        vt = text_ref[first:last, :]
        e = jnp.exp2(slope * dots + shift)
        chance = pl.reciprocal(1.0 + e, approx=True)
        if own and first == 0:
            row = lax.broadcasted_iota(jnp.int32, chance.shape, 0)
            column = lax.broadcasted_iota(jnp.int32, chance.shape, 1)
            same = (row == column) & (row < own)
            chance = jnp.where(same, -e * chance, chance)
        coefficient = (temper * chance).astype(jnp.bfloat16)
        text_part = lax.dot_general(
            coefficient, vi, (((0,), (0,)), ((), ())), preferred_element_type=jnp.float32
        )
        if text_add is not None:
            text_part = text_add[first:last, :] + text_part
        text_out[first:last, :] = text_part.astype(text_out.dtype)
        part = jnp.dot(coefficient, vt, preferred_element_type=jnp.float32)
        totals[at] = part if totals[at] is None else totals[at] + part
    return totals


def early_pairs_kernel(params_ref, text_ref, *refs):
    image_refs, (text_out, units_out, total_out) = refs[:-3], refs[-3:]
    rows = image_refs[0].shape[0]
    for a, ref in enumerate(image_refs):
        units_out[a * rows:(a + 1) * rows, :] = unit_rows(ref[...])[0].astype(jnp.bfloat16)
    (total,) = pairs(params_ref, [(units_out[...], text_ref, text_out, rows, None)])
    total_out[...] = total


def rest_pairs_kernel(
    count, params_ref, early_ref, total_ref, own_text_ref, own_add_ref, late_ref, *refs
):
    text_refs, own_out = refs[:count], refs[count]
    other_out, image_out = refs[count + 1:2 * count + 1], refs[2 * count + 1:]
    rows = image_out[0].shape[0]
    early, late = early_ref[...], late_ref[...]
    vi = jnp.concatenate([early, late], axis=0)
    late_total, *totals = pairs(
        params_ref,
        [(late, own_text_ref, own_out, 0, own_add_ref)]
        + [(vi, text_ref, out, 0, None) for text_ref, out in zip(text_refs, other_out)],
    )
    total = sum(totals, jnp.concatenate([total_ref[...], late_total], axis=0))
    for a, ref in enumerate(image_out):
        ref[...] = total[a * rows:(a + 1) * rows, :].astype(ref.dtype)


def pair_terms(params, early, late, texts, image_types):
    rows, width = early[0].shape
    early_rows, late_rows = rows * len(early), rows * len(late)
    own, others = texts[0], texts[1:]
    other_rows = sum(t.shape[0] for t in others)

    def cost(pair_count):
        return dict(flops=6 * pair_count * width, transcendentals=2 * pair_count)

    own_add, early_units, total = call(
        early_pairs_kernel,
        [
            jax.ShapeDtypeStruct(own.shape, jnp.float32),
            jax.ShapeDtypeStruct((early_rows, width), jnp.bfloat16),
            jax.ShapeDtypeStruct((early_rows, width), jnp.float32),
        ],
        [params, own, *early],
        name="early_pairs",
        **cost(early_rows * own.shape[0]),
    )
    late_units = units(late, "late_units", LATE)
    outs = call(
        functools.partial(rest_pairs_kernel, len(others)),
        [jax.ShapeDtypeStruct(own.shape, jnp.float32)]
        + [jax.ShapeDtypeStruct(t.shape, jnp.bfloat16) for t in others]
        + [jax.ShapeDtypeStruct((rows, width), t) for t in image_types],
        [params, early_units, total, own, own_add, late_units, *others],
        name="rest_pairs",
        **cost(late_rows * own.shape[0] + (early_rows + late_rows) * other_rows),
    )
    count = 1 + len(others)
    return outs[count:], outs[:count]


def add_stacks_kernel(part_count, *refs):
    parts, outs = refs[:part_count], refs[part_count:]
    rows = outs[0].shape[0]
    for at, out in enumerate(outs):
        total = parts[0][at * rows:(at + 1) * rows, :].astype(jnp.float32)
        for part in parts[1:]:
            total = total + part[at * rows:(at + 1) * rows, :].astype(jnp.float32)
        out[...] = total.astype(out.dtype)


def add_stacks(parts, count):
    shape = (parts[0].shape[0] // count, parts[0].shape[1])
    types = [jnp.float32] + [jnp.bfloat16] * (count - 1)
    return call(
        functools.partial(add_stacks_kernel, len(parts)),
        [jax.ShapeDtypeStruct(shape, t) for t in types],
        parts,
        flops=len(parts) * parts[0].size,
        name="add_stacks",
    )


def add_parts_kernel(*refs):
    total = sum(ref[...].astype(jnp.float32) for ref in refs[:-1])
    refs[-1][...] = total.astype(refs[-1].dtype)


def add_parts(parts, dtype, weight, name):
    out = jax.ShapeDtypeStruct(parts[0].shape, dtype)
    return call(
        add_parts_kernel, [out], parts, flops=weight * len(parts) * out.size, name=name
    )[0]


def finish_kernel(sides, image_ref, text_ref, *refs):
    parts, outs = refs[:len(sides)], refs[len(sides):len(sides) + 2]
    staged, sems = refs[len(sides) + 2:]
    rows = image_ref.shape[0]
    piece = math.gcd(rows, PIECE)
    copies = []
    for side, raw in enumerate((image_ref, text_ref)):
        for first in range(0, rows, piece):
            here = pl.ds(first, piece)
            unit, factor = unit_rows(raw[here, :])
            total = sum(
                ref[here, :].astype(jnp.float32) for at, ref in zip(sides, parts) if at == side
            )
            along = jnp.sum(unit * total, axis=-1, keepdims=True)
            staged[side, here, :] = factor * (total - unit * along)
            copies.append(
                pltpu.make_async_copy(
                    staged.at[side, here, :], outs[side].at[here, :], sems.at[len(copies)]
                )
            )
            copies[-1].start()
    for copy in copies:
        copy.wait()


def finish(images, texts, parts):
    out = jax.ShapeDtypeStruct(images.shape, jnp.float32)
    return pl.pallas_call(
        functools.partial(finish_kernel, [side for side, _ in parts]),
        out_shape=(out, out),
        in_specs=[VMEM] * (2 + len(parts)),
        out_specs=[pl.BlockSpec(memory_space=pl.ANY)] * 2,
        scratch_shapes=[
            pltpu.VMEM((2,) + images.shape, jnp.float32),
            pltpu.SemaphoreType.DMA((2 * (images.shape[0] // math.gcd(images.shape[0], PIECE)),)),
        ],
        compiler_params=pltpu.CompilerParams(vmem_limit_bytes=VMEM_LIMIT),
        cost_estimate=pl.CostEstimate(
            flops=10 * len(parts) * images.size,
            bytes_accessed=3 * len(parts) * images.size,
            transcendentals=0,
        ),
        name="finish",
    )(images, texts, *[part for _, part in parts])


def plan(grp_count, dev_count):
    options = [n for n in range(1, dev_count + 1) if dev_count % n == 0]
    near = min(options, key=lambda n: (dev_count // n + grp_count * n, -n))
    return dev_count // near, near


def step_to(at, by, count):
    if count & (count - 1) == 0:
        return at ^ abs(by)
    return (at + by) % count


def solution(mesh):
    grp_count, dev_count = mesh.shape["grp"], mesh.shape["dev"]
    far_count, near_count = plan(grp_count, dev_count)
    low_count = 2 if far_count % 2 == 0 else 1
    high_count = far_count // low_count

    def move(value, grp=0, high=0, low=0, near=0):
        perm = []
        for g in range(grp_count):
            for h in range(high_count):
                for w in range(low_count):
                    for n in range(near_count):
                        source = ((g * high_count + h) * low_count + w) * near_count + n
                        g2 = step_to(g, grp, grp_count)
                        h2 = step_to(h, high, high_count)
                        w2 = step_to(w, low, low_count)
                        n2 = step_to(n, near, near_count)
                        target = ((g2 * high_count + h2) * low_count + w2) * near_count + n2
                        perm.append((source, target))
        return lax.ppermute(value, AXES, perm)

    def on_device(images, texts, logit_scale, logit_bias):
        params = jnp.concatenate(
            [logit_scale * -LOG2_E, logit_bias * -LOG2_E, logit_scale]
        ).reshape(1, 3)
        early = {(0, 0): images}
        for h in range(1, high_count):
            early[h, 0] = move(images, high=h)
        for w in range(1, low_count):
            early[0, w] = move(images, low=w)
        late = {}
        for h in range(1, high_count):
            block, params = lax.optimization_barrier((early[h, 0], params))
            for w in range(1, low_count):
                late[h, w] = move(block, low=w)
        near_rows = [units([texts], "own_units")] + [move(texts, near=n) for n in range(1, near_count)]
        own_stack = stack_units(near_rows)
        stacks = [own_stack] + [move(own_stack, grp=g) for g in range(1, grp_count)]
        far_steps = [*early, *late]
        image_types = [jnp.bfloat16 if w else jnp.float32 for _, w in far_steps]
        image_parts, text_parts = pair_terms(
            params, list(early.values()), list(late.values()), stacks, image_types
        )
        far_parts = dict(zip(far_steps, image_parts))
        passed = [move(far_parts[step], low=-step[1]) for step in late]
        came = [move(part, grp=-g) for g, part in enumerate(text_parts) if g]
        near_parts = add_stacks([text_parts[0], *came], near_count)
        low_parts = [far_parts[0, w] for w in range(1, low_count)]
        near_came = [move(part, near=-n) for n, part in enumerate(near_parts) if n]
        high_came = []
        for h in range(1, high_count):
            terms = [far_parts[h, 0]] + [p for step, p in zip(late, passed) if step[0] == h]
            both = add_parts(terms, jnp.bfloat16, 1, "add_passed")
            both, low_parts = lax.optimization_barrier((both, low_parts))
            high_came.append(move(both, high=-h))
        low_came = [move(part, low=-w) for w, part in enumerate(low_parts, 1)]
        return finish(
            images,
            texts,
            [(1, add_parts([near_parts[0], *near_came], jnp.float32, NEAR, "add_near"))]
            + [(0, part) for part in [far_parts[0, 0]] + high_came + low_came],
        )

    in_specs = (P(AXES, None), P(AXES, None), P(), P())
    out_specs = (P(AXES, None), P(AXES, None))
    return jax.shard_map(
        on_device, mesh=mesh, in_specs=in_specs, out_specs=out_specs, check_vma=False
    )
```

```python
import functools
import math

import jax
import jax.numpy as jnp
from jax import lax
from jax.experimental import pallas as pl
from jax.experimental.pallas import tpu as pltpu
from jax.sharding import PartitionSpec as P

AXES = ("grp", "dev")
VMEM_LIMIT = 32 * 1024 * 1024
SPAN = 256
PIECE = 32
LATE = 16500
NEAR = 30000
LOW = 3000
LOG2_E = math.log2(math.e)
VMEM = pl.BlockSpec(memory_space=pltpu.VMEM)


def unit_rows(raw):
    wide = raw.astype(jnp.float32)
    factor = lax.rsqrt(jnp.sum(wide * wide, axis=-1, keepdims=True) + 1e-06)
    return wide * factor, factor


def call(kernel, out_shape, operands, scratch=(), flops=0, transcendentals=0, name=None):
    touched = sum(x.size * x.dtype.itemsize for x in list(operands) + list(out_shape))
    outs = pl.pallas_call(
        kernel,
        out_shape=out_shape,
        in_specs=[VMEM] * len(operands),
        out_specs=[VMEM] * len(out_shape),
        scratch_shapes=scratch,
        compiler_params=pltpu.CompilerParams(vmem_limit_bytes=VMEM_LIMIT),
        cost_estimate=pl.CostEstimate(
            flops=flops, bytes_accessed=touched, transcendentals=transcendentals
        ),
        name=name,
    )(*operands)
    return tuple(outs)


def units_kernel(*refs):
    rows = refs[0].shape[0]
    for at, ref in enumerate(refs[:-1]):
        refs[-1][at * rows:(at + 1) * rows, :] = unit_rows(ref[...])[0].astype(refs[-1].dtype)


def units(blocks, name, weight=1):
    rows, width = blocks[0].shape
    out = jax.ShapeDtypeStruct((len(blocks) * rows, width), jnp.bfloat16)
    return call(units_kernel, [out], blocks, flops=4 * weight * out.size, name=name)[0]


def stack_units_kernel(*refs):
    out = refs[-1]
    rows = refs[0].shape[0]
    out[:rows, :] = refs[0][...]
    for at, ref in enumerate(refs[1:-1], 1):
        out[at * rows:(at + 1) * rows, :] = unit_rows(ref[...])[0].astype(out.dtype)


def stack_units(blocks):
    rows, width = blocks[0].shape
    out = jax.ShapeDtypeStruct((len(blocks) * rows, width), jnp.bfloat16)
    return call(stack_units_kernel, [out], blocks, flops=4 * out.size, name="stack_units")[0]


def pairs(params_ref, jobs):
    slope, shift, temper = (params_ref[0:1, at:at + 1] for at in range(3))
    chunks = [
        (at, first, min(first + SPAN, job[1].shape[0]))
        for at, job in enumerate(jobs) for first in range(0, job[1].shape[0], SPAN)
    ]

    def dots_of(at, first, last):
        vi, text_ref = jobs[at][:2]
        return lax.dot_general(
            vi, text_ref[first:last, :], (((1,), (1,)), ((), ())),
            preferred_element_type=jnp.float32,
        )

    totals = [None] * len(jobs)
    coming = dots_of(*chunks[0])
    for step, (at, first, last) in enumerate(chunks):
        vi, text_ref, text_out, own, text_add = jobs[at]
        dots, coming = coming, dots_of(*chunks[step + 1]) if step + 1 < len(chunks) else None
        vt = text_ref[first:last, :]
        e = jnp.exp2(slope * dots + shift)
        chance = pl.reciprocal(1.0 + e, approx=True)
        if own and first == 0:
            row = lax.broadcasted_iota(jnp.int32, chance.shape, 0)
            column = lax.broadcasted_iota(jnp.int32, chance.shape, 1)
            same = (row == column) & (row < own)
            chance = jnp.where(same, -e * chance, chance)
        coefficient = (temper * chance).astype(jnp.bfloat16)
        text_part = lax.dot_general(
            coefficient, vi, (((0,), (0,)), ((), ())), preferred_element_type=jnp.float32
        )
        if text_add is not None:
            text_part = text_add[first:last, :] + text_part
        text_out[first:last, :] = text_part.astype(text_out.dtype)
        part = jnp.dot(coefficient, vt, preferred_element_type=jnp.float32)
        totals[at] = part if totals[at] is None else totals[at] + part
    return totals


def early_pairs_kernel(params_ref, text_ref, *refs):
    image_refs, (text_out, units_out, total_out) = refs[:-3], refs[-3:]
    rows = image_refs[0].shape[0]
    for a, ref in enumerate(image_refs):
        units_out[a * rows:(a + 1) * rows, :] = unit_rows(ref[...])[0].astype(jnp.bfloat16)
    (total,) = pairs(params_ref, [(units_out[...], text_ref, text_out, rows, None)])
    total_out[...] = total


def rest_pairs_kernel(
    count, params_ref, early_ref, total_ref, own_text_ref, own_add_ref, late_ref, *refs
):
    text_refs, own_out = refs[:count], refs[count]
    other_out, image_out = refs[count + 1:2 * count + 1], refs[2 * count + 1:]
    rows = image_out[0].shape[0]
    early, late = early_ref[...], late_ref[...]
    vi = jnp.concatenate([early, late], axis=0)
    late_total, *totals = pairs(
        params_ref,
        [(late, own_text_ref, own_out, 0, own_add_ref)]
        + [(vi, text_ref, out, 0, None) for text_ref, out in zip(text_refs, other_out)],
    )
    total = sum(totals, jnp.concatenate([total_ref[...], late_total], axis=0))
    for a, ref in enumerate(image_out):
        ref[...] = total[a * rows:(a + 1) * rows, :].astype(ref.dtype)


def pair_terms(params, early, late, texts, image_types):
    rows, width = early[0].shape
    early_rows, late_rows = rows * len(early), rows * len(late)
    own, others = texts[0], texts[1:]
    other_rows = sum(t.shape[0] for t in others)

    def cost(pair_count):
        return dict(flops=6 * pair_count * width, transcendentals=2 * pair_count)

    own_add, early_units, total = call(
        early_pairs_kernel,
        [
            jax.ShapeDtypeStruct(own.shape, jnp.float32),
            jax.ShapeDtypeStruct((early_rows, width), jnp.bfloat16),
            jax.ShapeDtypeStruct((early_rows, width), jnp.float32),
        ],
        [params, own, *early],
        name="early_pairs",
        **cost(early_rows * own.shape[0]),
    )
    late_units = units(late, "late_units", LATE)
    outs = call(
        functools.partial(rest_pairs_kernel, len(others)),
        [jax.ShapeDtypeStruct(own.shape, jnp.float32)]
        + [jax.ShapeDtypeStruct(t.shape, jnp.bfloat16) for t in others]
        + [jax.ShapeDtypeStruct((rows, width), t) for t in image_types],
        [params, early_units, total, own, own_add, late_units, *others],
        name="rest_pairs",
        **cost(late_rows * own.shape[0] + (early_rows + late_rows) * other_rows),
    )
    count = 1 + len(others)
    return outs[count:], outs[:count]


def add_stacks_kernel(part_count, *refs):
    parts, outs = refs[:part_count], refs[part_count:]
    rows = outs[0].shape[0]
    for at, out in enumerate(outs):
        total = parts[0][at * rows:(at + 1) * rows, :].astype(jnp.float32)
        for part in parts[1:]:
            total = total + part[at * rows:(at + 1) * rows, :].astype(jnp.float32)
        out[...] = total.astype(out.dtype)


def add_stacks(parts, count):
    shape = (parts[0].shape[0] // count, parts[0].shape[1])
    types = [jnp.float32] + [jnp.bfloat16] * (count - 1)
    return call(
        functools.partial(add_stacks_kernel, len(parts)),
        [jax.ShapeDtypeStruct(shape, t) for t in types],
        parts,
        flops=len(parts) * parts[0].size,
        name="add_stacks",
    )


def add_parts_kernel(*refs):
    total = sum(ref[...].astype(jnp.float32) for ref in refs[:-1])
    refs[-1][...] = total.astype(refs[-1].dtype)


def add_parts(parts, dtype, weight, name):
    out = jax.ShapeDtypeStruct(parts[0].shape, dtype)
    return call(
        add_parts_kernel, [out], parts, flops=weight * len(parts) * out.size, name=name
    )[0]


def finish_kernel(sides, image_ref, text_ref, *refs):
    parts, outs = refs[:len(sides)], refs[len(sides):len(sides) + 2]
    staged, sems = refs[len(sides) + 2:]
    rows = image_ref.shape[0]
    piece = math.gcd(rows, PIECE)
    copies = []
    for side, raw in enumerate((image_ref, text_ref)):
        for first in range(0, rows, piece):
            here = pl.ds(first, piece)
            unit, factor = unit_rows(raw[here, :])
            total = sum(
                ref[here, :].astype(jnp.float32) for at, ref in zip(sides, parts) if at == side
            )
            along = jnp.sum(unit * total, axis=-1, keepdims=True)
            staged[side, here, :] = factor * (total - unit * along)
            copies.append(
                pltpu.make_async_copy(
                    staged.at[side, here, :], outs[side].at[here, :], sems.at[len(copies)]
                )
            )
            copies[-1].start()
    for copy in copies:
        copy.wait()


def finish(images, texts, parts):
    out = jax.ShapeDtypeStruct(images.shape, jnp.float32)
    return pl.pallas_call(
        functools.partial(finish_kernel, [side for side, _ in parts]),
        out_shape=(out, out),
        in_specs=[VMEM] * (2 + len(parts)),
        out_specs=[pl.BlockSpec(memory_space=pl.ANY)] * 2,
        scratch_shapes=[
            pltpu.VMEM((2,) + images.shape, jnp.float32),
            pltpu.SemaphoreType.DMA((2 * (images.shape[0] // math.gcd(images.shape[0], PIECE)),)),
        ],
        compiler_params=pltpu.CompilerParams(vmem_limit_bytes=VMEM_LIMIT),
        cost_estimate=pl.CostEstimate(
            flops=10 * len(parts) * images.size,
            bytes_accessed=3 * len(parts) * images.size,
            transcendentals=0,
        ),
        name="finish",
    )(images, texts, *[part for _, part in parts])


def plan(grp_count, dev_count):
    options = [n for n in range(1, dev_count + 1) if dev_count % n == 0]
    near = min(options, key=lambda n: (dev_count // n + grp_count * n, -n))
    return dev_count // near, near


def step_to(at, by, count):
    if count & (count - 1) == 0:
        return at ^ abs(by)
    return (at + by) % count


def solution(mesh):
    grp_count, dev_count = mesh.shape["grp"], mesh.shape["dev"]
    far_count, near_count = plan(grp_count, dev_count)
    low_count = 2 if far_count % 2 == 0 else 1
    high_count = far_count // low_count

    def move(value, grp=0, high=0, low=0, near=0):
        perm = []
        for g in range(grp_count):
            for h in range(high_count):
                for w in range(low_count):
                    for n in range(near_count):
                        source = ((g * high_count + h) * low_count + w) * near_count + n
                        g2 = step_to(g, grp, grp_count)
                        h2 = step_to(h, high, high_count)
                        w2 = step_to(w, low, low_count)
                        n2 = step_to(n, near, near_count)
                        target = ((g2 * high_count + h2) * low_count + w2) * near_count + n2
                        perm.append((source, target))
        return lax.ppermute(value, AXES, perm)

    def on_device(images, texts, logit_scale, logit_bias):
        params = jnp.concatenate(
            [logit_scale * -LOG2_E, logit_bias * -LOG2_E, logit_scale]
        ).reshape(1, 3)
        early = {(0, 0): images}
        for h in range(1, high_count):
            early[h, 0] = move(images, high=h)
        for w in range(1, low_count):
            early[0, w] = move(images, low=w)
        late = {}
        for h in range(1, high_count):
            block, params = lax.optimization_barrier((early[h, 0], params))
            for w in range(1, low_count):
                late[h, w] = move(block, low=w)
        near_rows = [units([texts], "own_units")] + [move(texts, near=n) for n in range(1, near_count)]
        own_stack = stack_units(near_rows)
        stacks = [own_stack] + [move(own_stack, grp=g) for g in range(1, grp_count)]
        far_steps = [*early, *late]
        image_types = [jnp.bfloat16 if w else jnp.float32 for _, w in far_steps]
        image_parts, text_parts = pair_terms(
            params, list(early.values()), list(late.values()), stacks, image_types
        )
        far_parts = dict(zip(far_steps, image_parts))
        passed = [move(far_parts[step], low=-step[1]) for step in late]
        came = [move(part, grp=-g) for g, part in enumerate(text_parts) if g]
        near_parts = list(add_stacks([text_parts[0], *came], near_count))
        near_came = [move(part, near=-n) for n, part in enumerate(near_parts) if n]
        high_came = []
        for h in range(1, high_count):
            terms = [far_parts[h, 0]] + [p for step, p in zip(late, passed) if step[0] == h]
            both = add_parts(terms, jnp.bfloat16, 1, "add_passed")
            high_came.append(move(both, high=-h))
        low_came = [move(far_parts[0, w], low=-w) for w in range(1, low_count)]
        low_sum = add_parts([far_parts[0, 0], *low_came], jnp.float32, LOW, "add_low")
        low_sum, near_parts[0] = lax.optimization_barrier((low_sum, near_parts[0]))
        near_sum = add_parts([near_parts[0], *near_came], jnp.float32, NEAR, "add_near")
        return finish(images, texts, [(1, near_sum)] + [(0, part) for part in [low_sum] + high_came])

    in_specs = (P(AXES, None), P(AXES, None), P(), P())
    out_specs = (P(AXES, None), P(AXES, None))
    return jax.shard_map(
        on_device, mesh=mesh, in_specs=in_specs, out_specs=out_specs, check_vma=False
    )
```

```python
import functools
import math

import jax
import jax.numpy as jnp
from jax import lax
from jax.experimental import pallas as pl
from jax.experimental.pallas import tpu as pltpu
from jax.sharding import PartitionSpec as P

AXES = ("grp", "dev")
VMEM_LIMIT = 32 * 1024 * 1024
SPAN = 256
PIECE = 32
LATE = 16500
LOG2_E = math.log2(math.e)
VMEM = pl.BlockSpec(memory_space=pltpu.VMEM)


def unit_rows(raw):
    wide = raw.astype(jnp.float32)
    factor = lax.rsqrt(jnp.sum(wide * wide, axis=-1, keepdims=True) + 1e-06)
    return wide * factor, factor


def call(kernel, out_shape, operands, scratch=(), flops=0, transcendentals=0, name=None):
    touched = sum(x.size * x.dtype.itemsize for x in list(operands) + list(out_shape))
    outs = pl.pallas_call(
        kernel,
        out_shape=out_shape,
        in_specs=[VMEM] * len(operands),
        out_specs=[VMEM] * len(out_shape),
        scratch_shapes=scratch,
        compiler_params=pltpu.CompilerParams(vmem_limit_bytes=VMEM_LIMIT),
        cost_estimate=pl.CostEstimate(
            flops=flops, bytes_accessed=touched, transcendentals=transcendentals
        ),
        name=name,
    )(*operands)
    return tuple(outs)


def units_kernel(*refs):
    rows = refs[0].shape[0]
    for at, ref in enumerate(refs[:-1]):
        refs[-1][at * rows:(at + 1) * rows, :] = unit_rows(ref[...])[0].astype(refs[-1].dtype)


def units(blocks, name, weight=1):
    rows, width = blocks[0].shape
    out = jax.ShapeDtypeStruct((len(blocks) * rows, width), jnp.bfloat16)
    return call(units_kernel, [out], blocks, flops=4 * weight * out.size, name=name)[0]


def stack_units_kernel(*refs):
    out = refs[-1]
    rows = refs[0].shape[0]
    out[:rows, :] = refs[0][...]
    for at, ref in enumerate(refs[1:-1], 1):
        out[at * rows:(at + 1) * rows, :] = unit_rows(ref[...])[0].astype(out.dtype)


def stack_units(blocks):
    rows, width = blocks[0].shape
    out = jax.ShapeDtypeStruct((len(blocks) * rows, width), jnp.bfloat16)
    return call(stack_units_kernel, [out], blocks, flops=4 * out.size, name="stack_units")[0]


def pairs(params_ref, jobs):
    slope, shift, temper = (params_ref[0:1, at:at + 1] for at in range(3))
    chunks = [
        (at, first, min(first + SPAN, job[1].shape[0]))
        for at, job in enumerate(jobs) for first in range(0, job[1].shape[0], SPAN)
    ]

    def dots_of(at, first, last):
        vi, text_ref = jobs[at][:2]
        return lax.dot_general(
            vi, text_ref[first:last, :], (((1,), (1,)), ((), ())),
            preferred_element_type=jnp.float32,
        )

    totals = [None] * len(jobs)
    coming = dots_of(*chunks[0])
    for step, (at, first, last) in enumerate(chunks):
        vi, text_ref, text_out, own, text_add = jobs[at]
        dots, coming = coming, dots_of(*chunks[step + 1]) if step + 1 < len(chunks) else None
        vt = text_ref[first:last, :]
        e = jnp.exp2(slope * dots + shift)
        chance = pl.reciprocal(1.0 + e, approx=True)
        if own and first == 0:
            row = lax.broadcasted_iota(jnp.int32, chance.shape, 0)
            column = lax.broadcasted_iota(jnp.int32, chance.shape, 1)
            same = (row == column) & (row < own)
            chance = jnp.where(same, -e * chance, chance)
        coefficient = (temper * chance).astype(jnp.bfloat16)
        text_part = lax.dot_general(
            coefficient, vi, (((0,), (0,)), ((), ())), preferred_element_type=jnp.float32
        )
        if text_add is not None:
            text_part = text_add[first:last, :] + text_part
        text_out[first:last, :] = text_part.astype(text_out.dtype)
        part = jnp.dot(coefficient, vt, preferred_element_type=jnp.float32)
        totals[at] = part if totals[at] is None else totals[at] + part
    return totals


def early_pairs_kernel(params_ref, text_ref, *refs):
    image_refs, (text_out, units_out, total_out) = refs[:-3], refs[-3:]
    rows = image_refs[0].shape[0]
    for a, ref in enumerate(image_refs):
        units_out[a * rows:(a + 1) * rows, :] = unit_rows(ref[...])[0].astype(jnp.bfloat16)
    (total,) = pairs(params_ref, [(units_out[...], text_ref, text_out, rows, None)])
    total_out[...] = total


def rest_pairs_kernel(
    count, params_ref, early_ref, total_ref, own_text_ref, own_add_ref, late_ref, *refs
):
    text_refs, own_out = refs[:count], refs[count]
    other_out, image_out = refs[count + 1:2 * count + 1], refs[2 * count + 1:]
    rows = image_out[0].shape[0]
    early, late = early_ref[...], late_ref[...]
    vi = jnp.concatenate([early, late], axis=0)
    late_total, *totals = pairs(
        params_ref,
        [(late, own_text_ref, own_out, 0, own_add_ref)]
        + [(vi, text_ref, out, 0, None) for text_ref, out in zip(text_refs, other_out)],
    )
    total = sum(totals, jnp.concatenate([total_ref[...], late_total], axis=0))
    for a, ref in enumerate(image_out):
        ref[...] = total[a * rows:(a + 1) * rows, :].astype(ref.dtype)


def pair_terms(params, early, late, texts):
    rows, width = early[0].shape
    early_rows, late_rows = rows * len(early), rows * len(late)
    own, others = texts[0], texts[1:]
    other_rows = sum(t.shape[0] for t in others)

    def cost(pair_count):
        return dict(flops=6 * pair_count * width, transcendentals=2 * pair_count)

    own_add, early_units, total = call(
        early_pairs_kernel,
        [
            jax.ShapeDtypeStruct(own.shape, jnp.float32),
            jax.ShapeDtypeStruct((early_rows, width), jnp.bfloat16),
            jax.ShapeDtypeStruct((early_rows, width), jnp.float32),
        ],
        [params, own, *early],
        name="early_pairs",
        **cost(early_rows * own.shape[0]),
    )
    late_units = units(late, "late_units", LATE)
    outs = call(
        functools.partial(rest_pairs_kernel, len(others)),
        [jax.ShapeDtypeStruct(own.shape, jnp.float32)]
        + [jax.ShapeDtypeStruct(t.shape, jnp.bfloat16) for t in others]
        + [jax.ShapeDtypeStruct((rows, width), jnp.float32)]
        + [jax.ShapeDtypeStruct((rows, width), jnp.bfloat16)] * (len(early) + len(late) - 1),
        [params, early_units, total, own, own_add, late_units, *others],
        name="rest_pairs",
        **cost(late_rows * own.shape[0] + (early_rows + late_rows) * other_rows),
    )
    count = 1 + len(others)
    return outs[count:], outs[:count]


def add_stacks_kernel(part_count, *refs):
    parts, outs = refs[:part_count], refs[part_count:]
    rows = outs[0].shape[0]
    for at, out in enumerate(outs):
        total = parts[0][at * rows:(at + 1) * rows, :].astype(jnp.float32)
        for part in parts[1:]:
            total = total + part[at * rows:(at + 1) * rows, :].astype(jnp.float32)
        out[...] = total.astype(out.dtype)


def add_stacks(parts, count):
    shape = (parts[0].shape[0] // count, parts[0].shape[1])
    types = [jnp.float32] + [jnp.bfloat16] * (count - 1)
    return call(
        functools.partial(add_stacks_kernel, len(parts)),
        [jax.ShapeDtypeStruct(shape, t) for t in types],
        parts,
        flops=len(parts) * parts[0].size,
        name="add_stacks",
    )


def finish_kernel(sides, image_ref, text_ref, *refs):
    parts, outs = refs[:len(sides)], refs[len(sides):len(sides) + 2]
    staged, sems = refs[len(sides) + 2:]
    rows = image_ref.shape[0]
    piece = math.gcd(rows, PIECE)
    copies = []
    for side, raw in enumerate((image_ref, text_ref)):
        for first in range(0, rows, piece):
            here = pl.ds(first, piece)
            unit, factor = unit_rows(raw[here, :])
            total = sum(
                ref[here, :].astype(jnp.float32) for at, ref in zip(sides, parts) if at == side
            )
            along = jnp.sum(unit * total, axis=-1, keepdims=True)
            staged[side, here, :] = factor * (total - unit * along)
            copies.append(
                pltpu.make_async_copy(
                    staged.at[side, here, :], outs[side].at[here, :], sems.at[len(copies)]
                )
            )
            copies[-1].start()
    for copy in copies:
        copy.wait()


def finish(images, texts, parts):
    out = jax.ShapeDtypeStruct(images.shape, jnp.float32)
    return pl.pallas_call(
        functools.partial(finish_kernel, [side for side, _ in parts]),
        out_shape=(out, out),
        in_specs=[VMEM] * (2 + len(parts)),
        out_specs=[pl.BlockSpec(memory_space=pl.ANY)] * 2,
        scratch_shapes=[
            pltpu.VMEM((2,) + images.shape, jnp.float32),
            pltpu.SemaphoreType.DMA((2 * (images.shape[0] // math.gcd(images.shape[0], PIECE)),)),
        ],
        compiler_params=pltpu.CompilerParams(vmem_limit_bytes=VMEM_LIMIT),
        cost_estimate=pl.CostEstimate(
            flops=10 * len(parts) * images.size,
            bytes_accessed=3 * len(parts) * images.size,
            transcendentals=0,
        ),
        name="finish",
    )(images, texts, *[part for _, part in parts])


def plan(grp_count, dev_count):
    options = [n for n in range(1, dev_count + 1) if dev_count % n == 0]
    near = min(options, key=lambda n: (dev_count // n + grp_count * n, -n))
    return dev_count // near, near


def step_to(at, by, count):
    if count & (count - 1) == 0:
        return at ^ abs(by)
    return (at + by) % count


def solution(mesh):
    grp_count, dev_count = mesh.shape["grp"], mesh.shape["dev"]
    far_count, near_count = plan(grp_count, dev_count)
    low_count = 2 if far_count % 2 == 0 else 1
    high_count = far_count // low_count

    def move(value, grp=0, high=0, low=0, near=0):
        perm = []
        for g in range(grp_count):
            for h in range(high_count):
                for w in range(low_count):
                    for n in range(near_count):
                        source = ((g * high_count + h) * low_count + w) * near_count + n
                        g2 = step_to(g, grp, grp_count)
                        h2 = step_to(h, high, high_count)
                        w2 = step_to(w, low, low_count)
                        n2 = step_to(n, near, near_count)
                        target = ((g2 * high_count + h2) * low_count + w2) * near_count + n2
                        perm.append((source, target))
        return lax.ppermute(value, AXES, perm)

    def on_device(images, texts, logit_scale, logit_bias):
        params = jnp.concatenate(
            [logit_scale * -LOG2_E, logit_bias * -LOG2_E, logit_scale]
        ).reshape(1, 3)
        early = {(0, 0): images}
        for h in range(1, high_count):
            early[h, 0] = move(images, high=h)
        for w in range(1, low_count):
            early[0, w] = move(images, low=w)
        late = {}
        for h in range(1, high_count):
            block, params = lax.optimization_barrier((early[h, 0], params))
            for w in range(1, low_count):
                late[h, w] = move(block, low=w)
        near_rows = [units([texts], "own_units")] + [move(texts, near=n) for n in range(1, near_count)]
        own_stack = stack_units(near_rows)
        stacks = [own_stack] + [move(own_stack, grp=g) for g in range(1, grp_count)]
        image_parts, text_parts = pair_terms(
            params, list(early.values()), list(late.values()), stacks
        )
        far_parts = dict(zip([*early, *late], image_parts))
        came = [move(part, grp=-g) for g, part in enumerate(text_parts) if g]
        far_order = sorted((step for step in far_parts if step != (0, 0)), key=lambda step: (step[0], -step[1]) if step[0] else step)
        far_came = [move(far_parts[h, w], high=-h, low=-w) for h, w in far_order]
        near_parts = add_stacks([text_parts[0], *came], near_count)
        near_parts = [near_parts[0]] + [
            move(part, near=-n) for n, part in enumerate(near_parts) if n
        ]
        return finish(
            images,
            texts,
            [(0, part) for part in [far_parts[0, 0]] + far_came]
            + [(1, part) for part in near_parts],
        )

    in_specs = (P(AXES, None), P(AXES, None), P(), P())
    out_specs = (P(AXES, None), P(AXES, None))
    return jax.shard_map(
        on_device, mesh=mesh, in_specs=in_specs, out_specs=out_specs, check_vma=False
    )
```

```python
import functools
import math

import jax
import jax.numpy as jnp
from jax import lax
from jax.experimental import pallas as pl
from jax.experimental.pallas import tpu as pltpu
from jax.sharding import PartitionSpec as P

AXES = ("grp", "dev")
VMEM_LIMIT = 32 * 1024 * 1024
SPAN = 256
PIECE = 32
LATE = 16500
NEAR = 30000
LOW = 3000
LOG2_E = math.log2(math.e)
VMEM = pl.BlockSpec(memory_space=pltpu.VMEM)


def unit_rows(raw):
    wide = raw.astype(jnp.float32)
    factor = lax.rsqrt(jnp.sum(wide * wide, axis=-1, keepdims=True) + 1e-06)
    return wide * factor, factor


def call(kernel, out_shape, operands, scratch=(), flops=0, transcendentals=0, name=None):
    touched = sum(x.size * x.dtype.itemsize for x in list(operands) + list(out_shape))
    outs = pl.pallas_call(
        kernel,
        out_shape=out_shape,
        in_specs=[VMEM] * len(operands),
        out_specs=[VMEM] * len(out_shape),
        scratch_shapes=scratch,
        compiler_params=pltpu.CompilerParams(vmem_limit_bytes=VMEM_LIMIT),
        cost_estimate=pl.CostEstimate(
            flops=flops, bytes_accessed=touched, transcendentals=transcendentals
        ),
        name=name,
    )(*operands)
    return tuple(outs)


def units_kernel(*refs):
    rows = refs[0].shape[0]
    for at, ref in enumerate(refs[:-1]):
        refs[-1][at * rows:(at + 1) * rows, :] = unit_rows(ref[...])[0].astype(refs[-1].dtype)


def units(blocks, name, weight=1):
    rows, width = blocks[0].shape
    out = jax.ShapeDtypeStruct((len(blocks) * rows, width), jnp.bfloat16)
    return call(units_kernel, [out], blocks, flops=4 * weight * out.size, name=name)[0]


def stack_units_kernel(*refs):
    out = refs[-1]
    rows = refs[0].shape[0]
    out[:rows, :] = refs[0][...]
    for at, ref in enumerate(refs[1:-1], 1):
        out[at * rows:(at + 1) * rows, :] = unit_rows(ref[...])[0].astype(out.dtype)


def stack_units(blocks):
    rows, width = blocks[0].shape
    out = jax.ShapeDtypeStruct((len(blocks) * rows, width), jnp.bfloat16)
    return call(stack_units_kernel, [out], blocks, flops=4 * out.size, name="stack_units")[0]


def pairs(params_ref, jobs):
    slope, shift, temper = (params_ref[0:1, at:at + 1] for at in range(3))
    chunks = [
        (at, first, min(first + SPAN, job[1].shape[0]))
        for at, job in enumerate(jobs) for first in range(0, job[1].shape[0], SPAN)
    ]

    def dots_of(at, first, last):
        vi, text_ref = jobs[at][:2]
        return lax.dot_general(
            vi, text_ref[first:last, :], (((1,), (1,)), ((), ())),
            preferred_element_type=jnp.float32,
        )

    totals = [None] * len(jobs)
    coming = dots_of(*chunks[0])
    for step, (at, first, last) in enumerate(chunks):
        vi, text_ref, text_out, own, text_add = jobs[at]
        dots, coming = coming, dots_of(*chunks[step + 1]) if step + 1 < len(chunks) else None
        vt = text_ref[first:last, :]
        e = jnp.exp2(slope * dots + shift)
        chance = pl.reciprocal(1.0 + e, approx=True)
        if own and first == 0:
            row = lax.broadcasted_iota(jnp.int32, chance.shape, 0)
            column = lax.broadcasted_iota(jnp.int32, chance.shape, 1)
            same = (row == column) & (row < own)
            chance = jnp.where(same, -e * chance, chance)
        coefficient = (temper * chance).astype(jnp.bfloat16)
        text_part = lax.dot_general(
            coefficient, vi, (((0,), (0,)), ((), ())), preferred_element_type=jnp.float32
        )
        if text_add is not None:
            text_part = text_add[first:last, :] + text_part
        text_out[first:last, :] = text_part.astype(text_out.dtype)
        part = jnp.dot(coefficient, vt, preferred_element_type=jnp.float32)
        totals[at] = part if totals[at] is None else totals[at] + part
    return totals


def early_pairs_kernel(params_ref, text_ref, *refs):
    image_refs, (text_out, units_out, total_out) = refs[:-3], refs[-3:]
    rows = image_refs[0].shape[0]
    for a, ref in enumerate(image_refs):
        units_out[a * rows:(a + 1) * rows, :] = unit_rows(ref[...])[0].astype(jnp.bfloat16)
    (total,) = pairs(params_ref, [(units_out[...], text_ref, text_out, rows, None)])
    total_out[...] = total


def rest_pairs_kernel(
    count, params_ref, early_ref, total_ref, own_text_ref, own_add_ref, late_ref, *refs
):
    text_refs, own_out = refs[:count], refs[count]
    other_out, image_out = refs[count + 1:2 * count + 1], refs[2 * count + 1:]
    rows = image_out[0].shape[0]
    early, late = early_ref[...], late_ref[...]
    vi = jnp.concatenate([early, late], axis=0)
    late_total, *totals = pairs(
        params_ref,
        [(late, own_text_ref, own_out, 0, own_add_ref)]
        + [(vi, text_ref, out, 0, None) for text_ref, out in zip(text_refs, other_out)],
    )
    total = sum(totals, jnp.concatenate([total_ref[...], late_total], axis=0))
    for a, ref in enumerate(image_out):
        ref[...] = total[a * rows:(a + 1) * rows, :].astype(ref.dtype)


def pair_terms(params, early, late, texts, image_types):
    rows, width = early[0].shape
    early_rows, late_rows = rows * len(early), rows * len(late)
    own, others = texts[0], texts[1:]
    other_rows = sum(t.shape[0] for t in others)

    def cost(pair_count):
        return dict(flops=6 * pair_count * width, transcendentals=2 * pair_count)

    own_add, early_units, total = call(
        early_pairs_kernel,
        [
            jax.ShapeDtypeStruct(own.shape, jnp.float32),
            jax.ShapeDtypeStruct((early_rows, width), jnp.bfloat16),
            jax.ShapeDtypeStruct((early_rows, width), jnp.float32),
        ],
        [params, own, *early],
        name="early_pairs",
        **cost(early_rows * own.shape[0]),
    )
    late_units = units(late, "late_units", LATE)
    outs = call(
        functools.partial(rest_pairs_kernel, len(others)),
        [jax.ShapeDtypeStruct(own.shape, jnp.float32)]
        + [jax.ShapeDtypeStruct(t.shape, jnp.bfloat16) for t in others]
        + [jax.ShapeDtypeStruct((rows, width), t) for t in image_types],
        [params, early_units, total, own, own_add, late_units, *others],
        name="rest_pairs",
        **cost(late_rows * own.shape[0] + (early_rows + late_rows) * other_rows),
    )
    count = 1 + len(others)
    return outs[count:], outs[:count]


def add_stacks_kernel(part_count, *refs):
    parts, outs = refs[:part_count], refs[part_count:]
    rows = outs[0].shape[0]
    for at, out in enumerate(outs):
        total = parts[0][at * rows:(at + 1) * rows, :].astype(jnp.float32)
        for part in parts[1:]:
            total = total + part[at * rows:(at + 1) * rows, :].astype(jnp.float32)
        out[...] = total.astype(out.dtype)


def add_stacks(parts, count):
    shape = (parts[0].shape[0] // count, parts[0].shape[1])
    types = [jnp.float32] + [jnp.bfloat16] * (count - 1)
    return call(
        functools.partial(add_stacks_kernel, len(parts)),
        [jax.ShapeDtypeStruct(shape, t) for t in types],
        parts,
        flops=len(parts) * parts[0].size,
        name="add_stacks",
    )


def add_parts_kernel(*refs):
    total = sum(ref[...].astype(jnp.float32) for ref in refs[:-1])
    refs[-1][...] = total.astype(refs[-1].dtype)


def add_parts(parts, dtype, weight, name):
    out = jax.ShapeDtypeStruct(parts[0].shape, dtype)
    return call(
        add_parts_kernel, [out], parts, flops=weight * len(parts) * out.size, name=name
    )[0]


def finish_kernel(sides, image_ref, text_ref, *refs):
    parts, outs = refs[:len(sides)], refs[len(sides):len(sides) + 2]
    staged, sems = refs[len(sides) + 2:]
    rows = image_ref.shape[0]
    piece = math.gcd(rows, PIECE)
    copies = []
    for side, raw in enumerate((image_ref, text_ref)):
        for first in range(0, rows, piece):
            here = pl.ds(first, piece)
            unit, factor = unit_rows(raw[here, :])
            total = sum(
                ref[here, :].astype(jnp.float32) for at, ref in zip(sides, parts) if at == side
            )
            along = jnp.sum(unit * total, axis=-1, keepdims=True)
            staged[side, here, :] = factor * (total - unit * along)
            copies.append(
                pltpu.make_async_copy(
                    staged.at[side, here, :], outs[side].at[here, :], sems.at[len(copies)]
                )
            )
            copies[-1].start()
    for copy in copies:
        copy.wait()


def finish(images, texts, parts):
    out = jax.ShapeDtypeStruct(images.shape, jnp.float32)
    return pl.pallas_call(
        functools.partial(finish_kernel, [side for side, _ in parts]),
        out_shape=(out, out),
        in_specs=[VMEM] * (2 + len(parts)),
        out_specs=[pl.BlockSpec(memory_space=pl.ANY)] * 2,
        scratch_shapes=[
            pltpu.VMEM((2,) + images.shape, jnp.float32),
            pltpu.SemaphoreType.DMA((2 * (images.shape[0] // math.gcd(images.shape[0], PIECE)),)),
        ],
        compiler_params=pltpu.CompilerParams(vmem_limit_bytes=VMEM_LIMIT),
        cost_estimate=pl.CostEstimate(
            flops=10 * len(parts) * images.size,
            bytes_accessed=3 * len(parts) * images.size,
            transcendentals=0,
        ),
        name="finish",
    )(images, texts, *[part for _, part in parts])


def plan(grp_count, dev_count):
    options = [n for n in range(1, dev_count + 1) if dev_count % n == 0]
    near = min(options, key=lambda n: (dev_count // n + grp_count * n, -n))
    return dev_count // near, near


def step_to(at, by, count):
    if count & (count - 1) == 0:
        return at ^ abs(by)
    return (at + by) % count


def solution(mesh):
    grp_count, dev_count = mesh.shape["grp"], mesh.shape["dev"]
    far_count, near_count = plan(grp_count, dev_count)
    low_count = 2 if far_count % 2 == 0 else 1
    high_count = far_count // low_count

    def move(value, grp=0, high=0, low=0, near=0):
        perm = []
        for g in range(grp_count):
            for h in range(high_count):
                for w in range(low_count):
                    for n in range(near_count):
                        source = ((g * high_count + h) * low_count + w) * near_count + n
                        g2 = step_to(g, grp, grp_count)
                        h2 = step_to(h, high, high_count)
                        w2 = step_to(w, low, low_count)
                        n2 = step_to(n, near, near_count)
                        target = ((g2 * high_count + h2) * low_count + w2) * near_count + n2
                        perm.append((source, target))
        return lax.ppermute(value, AXES, perm)

    def on_device(images, texts, logit_scale, logit_bias):
        params = jnp.concatenate(
            [logit_scale * -LOG2_E, logit_bias * -LOG2_E, logit_scale]
        ).reshape(1, 3)
        early = {(0, 0): images}
        for h in range(1, high_count):
            early[h, 0] = move(images, high=h)
        for w in range(1, low_count):
            early[0, w] = move(images, low=w)
        late = {}
        for h in range(1, high_count):
            block, params = lax.optimization_barrier((early[h, 0], params))
            for w in range(1, low_count):
                late[h, w] = move(block, low=w)
        near_rows = [units([texts], "own_units")] + [move(texts, near=n) for n in range(1, near_count)]
        own_stack = stack_units(near_rows)
        stacks = [own_stack] + [move(own_stack, grp=g) for g in range(1, grp_count)]
        far_steps = [*early, *late]
        image_types = [jnp.bfloat16 if w else jnp.float32 for _, w in far_steps]
        image_parts, text_parts = pair_terms(
            params, list(early.values()), list(late.values()), stacks, image_types
        )
        far_parts = dict(zip(far_steps, image_parts))
        passed = [move(far_parts[step], low=-step[1]) for step in late]
        came = [move(part, grp=-g) for g, part in enumerate(text_parts) if g]
        near_parts = list(add_stacks([text_parts[0], *came], near_count))
        near_came = [move(part, near=-n) for n, part in enumerate(near_parts) if n]
        high_came = []
        for h in range(1, high_count):
            terms = [far_parts[h, 0]] + [p for step, p in zip(late, passed) if step[0] == h]
            both = add_parts(terms, jnp.bfloat16, 1, "add_passed")
            high_came.append(move(both, high=-h))
        low_parts = [far_parts[0, w] for w in range(1, low_count)]
        low_parts, near_parts[0] = lax.optimization_barrier((low_parts, near_parts[0]))
        low_came = [move(part, low=-w) for w, part in enumerate(low_parts, 1)]
        low_sum = add_parts([far_parts[0, 0], *low_came], jnp.float32, LOW, "add_low")
        low_sum, near_parts[0] = lax.optimization_barrier((low_sum, near_parts[0]))
        near_sum = add_parts([near_parts[0], *near_came], jnp.float32, NEAR, "add_near")
        return finish(images, texts, [(1, near_sum)] + [(0, part) for part in [low_sum] + high_came])

    in_specs = (P(AXES, None), P(AXES, None), P(), P())
    out_specs = (P(AXES, None), P(AXES, None))
    return jax.shard_map(
        on_device, mesh=mesh, in_specs=in_specs, out_specs=out_specs, check_vma=False
    )
```

```python
import functools
import math

import jax
import jax.numpy as jnp
from jax import lax
from jax.experimental import pallas as pl
from jax.experimental.pallas import tpu as pltpu
from jax.sharding import PartitionSpec as P

AXES = ("grp", "dev")
VMEM_LIMIT = 32 * 1024 * 1024
SPAN = 256
PIECE = 32
LATE = 16500
LOG2_E = math.log2(math.e)
VMEM = pl.BlockSpec(memory_space=pltpu.VMEM)


def unit_rows(raw):
    wide = raw.astype(jnp.float32)
    factor = lax.rsqrt(jnp.sum(wide * wide, axis=-1, keepdims=True) + 1e-06)
    return wide * factor, factor


def call(kernel, out_shape, operands, scratch=(), flops=0, transcendentals=0, name=None):
    touched = sum(x.size * x.dtype.itemsize for x in list(operands) + list(out_shape))
    outs = pl.pallas_call(
        kernel,
        out_shape=out_shape,
        in_specs=[VMEM] * len(operands),
        out_specs=[VMEM] * len(out_shape),
        scratch_shapes=scratch,
        compiler_params=pltpu.CompilerParams(vmem_limit_bytes=VMEM_LIMIT),
        cost_estimate=pl.CostEstimate(
            flops=flops, bytes_accessed=touched, transcendentals=transcendentals
        ),
        name=name,
    )(*operands)
    return tuple(outs)


def units_kernel(*refs):
    rows = refs[0].shape[0]
    for at, ref in enumerate(refs[:-1]):
        refs[-1][at * rows:(at + 1) * rows, :] = unit_rows(ref[...])[0].astype(refs[-1].dtype)


def units(blocks, name, weight=1):
    rows, width = blocks[0].shape
    out = jax.ShapeDtypeStruct((len(blocks) * rows, width), jnp.bfloat16)
    return call(units_kernel, [out], blocks, flops=4 * weight * out.size, name=name)[0]


def stack_units_kernel(*refs):
    out = refs[-1]
    rows = refs[0].shape[0]
    out[:rows, :] = refs[0][...]
    for at, ref in enumerate(refs[1:-1], 1):
        out[at * rows:(at + 1) * rows, :] = unit_rows(ref[...])[0].astype(out.dtype)


def stack_units(blocks):
    rows, width = blocks[0].shape
    out = jax.ShapeDtypeStruct((len(blocks) * rows, width), jnp.bfloat16)
    return call(stack_units_kernel, [out], blocks, flops=4 * out.size, name="stack_units")[0]


def pairs(params_ref, jobs):
    slope, shift, temper = (params_ref[0:1, at:at + 1] for at in range(3))
    chunks = [
        (at, first, min(first + SPAN, job[1].shape[0]))
        for at, job in enumerate(jobs) for first in range(0, job[1].shape[0], SPAN)
    ]

    def dots_of(at, first, last):
        vi, text_ref = jobs[at][:2]
        return lax.dot_general(
            vi, text_ref[first:last, :], (((1,), (1,)), ((), ())),
            preferred_element_type=jnp.float32,
        )

    totals = [None] * len(jobs)
    coming = dots_of(*chunks[0])
    for step, (at, first, last) in enumerate(chunks):
        vi, text_ref, text_out, own, text_add = jobs[at]
        dots, coming = coming, dots_of(*chunks[step + 1]) if step + 1 < len(chunks) else None
        vt = text_ref[first:last, :]
        e = jnp.exp2(slope * dots + shift)
        chance = pl.reciprocal(1.0 + e, approx=True)
        if own and first == 0:
            row = lax.broadcasted_iota(jnp.int32, chance.shape, 0)
            column = lax.broadcasted_iota(jnp.int32, chance.shape, 1)
            same = (row == column) & (row < own)
            chance = jnp.where(same, -e * chance, chance)
        coefficient = (temper * chance).astype(jnp.bfloat16)
        text_part = lax.dot_general(
            coefficient, vi, (((0,), (0,)), ((), ())), preferred_element_type=jnp.float32
        )
        if text_add is not None:
            text_part = text_add[first:last, :] + text_part
        text_out[first:last, :] = text_part.astype(text_out.dtype)
        part = jnp.dot(coefficient, vt, preferred_element_type=jnp.float32)
        totals[at] = part if totals[at] is None else totals[at] + part
    return totals


def early_pairs_kernel(params_ref, text_ref, *refs):
    image_refs, (text_out, units_out, total_out) = refs[:-3], refs[-3:]
    rows = image_refs[0].shape[0]
    for a, ref in enumerate(image_refs):
        units_out[a * rows:(a + 1) * rows, :] = unit_rows(ref[...])[0].astype(jnp.bfloat16)
    (total,) = pairs(params_ref, [(units_out[...], text_ref, text_out, rows, None)])
    total_out[...] = total


def rest_pairs_kernel(
    count, params_ref, early_ref, total_ref, own_text_ref, own_add_ref, late_ref, *refs
):
    text_refs, own_out = refs[:count], refs[count]
    other_out, image_out = refs[count + 1:2 * count + 1], refs[2 * count + 1:]
    rows = image_out[0].shape[0]
    early, late = early_ref[...], late_ref[...]
    vi = jnp.concatenate([early, late], axis=0)
    late_total, *totals = pairs(
        params_ref,
        [(late, own_text_ref, own_out, 0, own_add_ref)]
        + [(vi, text_ref, out, 0, None) for text_ref, out in zip(text_refs, other_out)],
    )
    total = sum(totals, jnp.concatenate([total_ref[...], late_total], axis=0))
    for a, ref in enumerate(image_out):
        ref[...] = total[a * rows:(a + 1) * rows, :].astype(ref.dtype)


def pair_terms(params, early, late, texts):
    rows, width = early[0].shape
    early_rows, late_rows = rows * len(early), rows * len(late)
    own, others = texts[0], texts[1:]
    other_rows = sum(t.shape[0] for t in others)

    def cost(pair_count):
        return dict(flops=6 * pair_count * width, transcendentals=2 * pair_count)

    own_add, early_units, total = call(
        early_pairs_kernel,
        [
            jax.ShapeDtypeStruct(own.shape, jnp.float32),
            jax.ShapeDtypeStruct((early_rows, width), jnp.bfloat16),
            jax.ShapeDtypeStruct((early_rows, width), jnp.float32),
        ],
        [params, own, *early],
        name="early_pairs",
        **cost(early_rows * own.shape[0]),
    )
    late_units = units(late, "late_units", LATE)
    outs = call(
        functools.partial(rest_pairs_kernel, len(others)),
        [jax.ShapeDtypeStruct(own.shape, jnp.float32)]
        + [jax.ShapeDtypeStruct(t.shape, jnp.bfloat16) for t in others]
        + [jax.ShapeDtypeStruct((rows, width), jnp.float32)]
        + [jax.ShapeDtypeStruct((rows, width), jnp.bfloat16)] * (len(early) + len(late) - 1),
        [params, early_units, total, own, own_add, late_units, *others],
        name="rest_pairs",
        **cost(late_rows * own.shape[0] + (early_rows + late_rows) * other_rows),
    )
    count = 1 + len(others)
    return outs[count:], outs[:count]


def add_stacks_kernel(part_count, *refs):
    parts, outs = refs[:part_count], refs[part_count:]
    rows = outs[0].shape[0]
    for at, out in enumerate(outs):
        total = parts[0][at * rows:(at + 1) * rows, :].astype(jnp.float32)
        for part in parts[1:]:
            total = total + part[at * rows:(at + 1) * rows, :].astype(jnp.float32)
        out[...] = total.astype(out.dtype)


def add_stacks(parts, count):
    shape = (parts[0].shape[0] // count, parts[0].shape[1])
    types = [jnp.float32] + [jnp.bfloat16] * (count - 1)
    return call(
        functools.partial(add_stacks_kernel, len(parts)),
        [jax.ShapeDtypeStruct(shape, t) for t in types],
        parts,
        flops=len(parts) * parts[0].size,
        name="add_stacks",
    )


def finish_kernel(sides, image_ref, text_ref, *refs):
    parts, outs = refs[:len(sides)], refs[len(sides):len(sides) + 2]
    staged, sems = refs[len(sides) + 2:]
    rows = image_ref.shape[0]
    piece = math.gcd(rows, PIECE)
    copies = []
    for side, raw in enumerate((image_ref, text_ref)):
        for first in range(0, rows, piece):
            here = pl.ds(first, piece)
            unit, factor = unit_rows(raw[here, :])
            total = sum(
                ref[here, :].astype(jnp.float32) for at, ref in zip(sides, parts) if at == side
            )
            along = jnp.sum(unit * total, axis=-1, keepdims=True)
            staged[side, here, :] = factor * (total - unit * along)
            copies.append(
                pltpu.make_async_copy(
                    staged.at[side, here, :], outs[side].at[here, :], sems.at[len(copies)]
                )
            )
            copies[-1].start()
    for copy in copies:
        copy.wait()


def finish(images, texts, parts):
    out = jax.ShapeDtypeStruct(images.shape, jnp.float32)
    return pl.pallas_call(
        functools.partial(finish_kernel, [side for side, _ in parts]),
        out_shape=(out, out),
        in_specs=[VMEM] * (2 + len(parts)),
        out_specs=[pl.BlockSpec(memory_space=pl.ANY)] * 2,
        scratch_shapes=[
            pltpu.VMEM((2,) + images.shape, jnp.float32),
            pltpu.SemaphoreType.DMA((2 * (images.shape[0] // math.gcd(images.shape[0], PIECE)),)),
        ],
        compiler_params=pltpu.CompilerParams(vmem_limit_bytes=VMEM_LIMIT),
        cost_estimate=pl.CostEstimate(
            flops=10 * len(parts) * images.size,
            bytes_accessed=3 * len(parts) * images.size,
            transcendentals=0,
        ),
        name="finish",
    )(images, texts, *[part for _, part in parts])


def plan(grp_count, dev_count):
    options = [n for n in range(1, dev_count + 1) if dev_count % n == 0]
    near = min(options, key=lambda n: (dev_count // n + grp_count * n, -n))
    return dev_count // near, near


def step_to(at, by, count):
    if count & (count - 1) == 0:
        return at ^ abs(by)
    return (at + by) % count


def solution(mesh):
    grp_count, dev_count = mesh.shape["grp"], mesh.shape["dev"]
    far_count, near_count = plan(grp_count, dev_count)
    low_count = 2 if far_count % 2 == 0 else 1
    high_count = far_count // low_count

    def move(value, grp=0, high=0, low=0, near=0):
        perm = []
        for g in range(grp_count):
            for h in range(high_count):
                for w in range(low_count):
                    for n in range(near_count):
                        source = ((g * high_count + h) * low_count + w) * near_count + n
                        g2 = step_to(g, grp, grp_count)
                        h2 = step_to(h, high, high_count)
                        w2 = step_to(w, low, low_count)
                        n2 = step_to(n, near, near_count)
                        target = ((g2 * high_count + h2) * low_count + w2) * near_count + n2
                        perm.append((source, target))
        return lax.ppermute(value, AXES, perm)

    def on_device(images, texts, logit_scale, logit_bias):
        params = jnp.concatenate(
            [logit_scale * -LOG2_E, logit_bias * -LOG2_E, logit_scale]
        ).reshape(1, 3)
        early = {(0, 0): images}
        for h in range(1, high_count):
            early[h, 0] = move(images, high=h)
        for w in range(1, low_count):
            early[0, w] = move(images, low=w)
        late = {}
        for h in range(1, high_count):
            block, params = lax.optimization_barrier((early[h, 0], params))
            for w in range(1, low_count):
                late[h, w] = move(block, low=w)
        near_rows = [units([texts], "own_units")] + [move(texts, near=n) for n in range(1, near_count)]
        own_stack = stack_units(near_rows)
        stacks = [own_stack] + [move(own_stack, grp=g) for g in range(1, grp_count)]
        image_parts, text_parts = pair_terms(
            params, list(early.values()), list(late.values()), stacks
        )
        far_parts = dict(zip([*early, *late], image_parts))
        came = [move(part, grp=-g) for g, part in enumerate(text_parts) if g]
        far_order = sorted((step for step in far_parts if step != (0, 0)), key=lambda step: step[0])
        far_came = [move(far_parts[h, w], high=-h, low=-w) for h, w in far_order]
        near_parts = add_stacks([text_parts[0], *came], near_count)
        near_parts = [near_parts[0]] + [
            move(near_parts[n], near=-n)
            for n in sorted(range(1, near_count), key=lambda n: (2 * n != near_count, n))
        ]
        return finish(
            images,
            texts,
            [(0, part) for part in [far_parts[0, 0]] + far_came]
            + [(1, part) for part in near_parts],
        )

    in_specs = (P(AXES, None), P(AXES, None), P(), P())
    out_specs = (P(AXES, None), P(AXES, None))
    return jax.shard_map(
        on_device, mesh=mesh, in_specs=in_specs, out_specs=out_specs, check_vma=False
    )
```
